512 devices in a mesh: rows: 16 (over y_hi, x), cols: 32 (over y_lo, z, core).
Axes of the slice: x: 4, y: 8 (y_hi: 4, y_lo: 2; y = y_hi * 2 + y_lo), z: 8, core: 2. Of those that a mesh axis runs over, the one named last changes fastest.
Arguments:
- frames: bfloat16 [2, 64, 32768], P(None, 'rows', 'cols'), may hold values from -6 to 6
- hidden_start: bfloat16 [64, 1024, 128], P('rows', 'cols'), may hold values from -3 to 3
- cell_start: float32 [64, 1024, 128], P('rows', 'cols'), may hold values from -6 to 6
- kernel: bfloat16 [1440, 512], replicated, may hold values from -0.15625 to 0.15625
- gate_bias: float32 [512], replicated, may hold values from -4 to 4
- cotangent: bfloat16 [2, 64, 1024, 128], P(None, 'rows', 'cols'), may hold values from -6 to 6
Outputs:
- hidden_final: bfloat16 [64, 1024, 128], P('rows', 'cols')
- grad_hidden_start: float32 [64, 1024, 128], P('rows', 'cols')
- grad_cell_start: float32 [64, 1024, 128], P('rows', 'cols')
- kernel_grad: float32 [1440, 512], replicated
- bias_grad: float32 [512], replicated
The draws below stay inside these ranges and needn't reach their ends.
All inputs are finite; a program needn't handle non-finite values.
Results may differ from the reference program's by a relative error of at most 0.015.
Values may be sent and summed in bfloat16 or wider, within the bound.
A program may use at most 64 MiB of HBM per device.

```python
import jax
import jax.numpy as jnp
from jax import lax

HC = 128
CI = 32
KS = 3
STEPS = 2
NH = 64
NW = 1024
GATES = 512
KIN = 1440


def shard_levels(key, shape, shards, low, high):
    gain = 1.0
    for position, shards_of in shards:
        draws = jax.random.uniform(jax.random.fold_in(jax.random.fold_in(key, 6), position), (shards_of,), jnp.float32, low / len(shards), high / len(shards))
        gain = gain * jnp.repeat(jnp.exp(draws), shape[position] // shards_of).reshape((-1,) + (1,) * (len(shape) - 1 - position))
    return gain


def gaussian(stream_key, shape, spread, limit, pieces=(), held_as=jnp.bfloat16):
    values = jax.random.normal(stream_key, shape, jnp.float32) * spread
    if len(pieces) > 0:
        values = shard_levels(stream_key, shape, pieces, -0.22, 0.18) * values
    return jnp.clip(values, min=-limit, max=limit).astype(held_as)


def setup_inputs(seed: int = 0) -> dict:
    splits = jax.random.split(jax.random.key(seed), 7)
    return {
        "frames": gaussian(splits[0], (STEPS, NH, NW * CI), 1.0, 6.0, ((1, 16), (2, 32))),
        "hidden_start": gaussian(splits[1], (NH, NW, HC), 0.5, 3.0, ((0, 16), (1, 32))),
        "cell_start": gaussian(splits[2], (NH, NW, HC), 1.0, 6.0, ((0, 16), (1, 32)), jnp.float32),
        "kernel": gaussian(splits[3], (KIN, GATES), KIN ** -0.5, 0.15625),
        "gate_bias": gaussian(splits[4], (GATES,), 1.0, 4.0, (), jnp.float32),
        "cotangent": gaussian(splits[5], (STEPS, NH, NW, HC), 1.0, 6.0, ((1, 16), (2, 32))),
    }


def convolve(field, weights):
    numbers = ('NHWC', 'HWIO', 'NHWC')
    result = lax.conv_general_dilated(field[None], weights, (1, 1), 'SAME', dimension_numbers=numbers, preferred_element_type=jnp.float32)
    return result[0]

def reference(frames, hidden_start, cell_start, kernel, gate_bias, cotangent):
    chans = CI + HC
    weights = kernel.reshape(KS, KS, chans, GATES)
    flipped = jnp.transpose(weights[::-1, ::-1], (0, 1, 3, 2))
    hidden = hidden_start
    cell = cell_start
    saved = []
    for moment in range(STEPS):
        inputs = frames[moment].reshape(NH, NW, CI)
        stacked = jnp.concatenate([inputs, hidden], axis=-1)
        gates = convolve(stacked, weights) + gate_bias
        gate_in = jax.nn.sigmoid(gates[..., :HC])
        gate_forget = jax.nn.sigmoid(gates[..., HC:2 * HC])
        gate_cand = jnp.tanh(gates[..., 2 * HC:3 * HC])
        gate_out = jax.nn.sigmoid(gates[..., 3 * HC:])
        cell_prev = cell
        cell = gate_forget * cell_prev + gate_in * gate_cand
        hidden = (gate_out * jnp.tanh(cell)).astype(jnp.bfloat16)
        saved.append((stacked, gate_in, gate_forget, gate_cand, gate_out, cell_prev, cell))
    hidden_final = hidden
    grad_hidden = cotangent[STEPS - 1].astype(jnp.float32)
    grad_cell = jnp.zeros((NH, NW, HC), jnp.float32)
    kernel_total = jnp.zeros((KS * KS, chans, GATES), jnp.float32)
    bias_total = jnp.zeros((GATES,), jnp.float32)
    for moment in range(STEPS - 1, -1, -1):
        stacked, gate_in, gate_forget, gate_cand, gate_out, cell_prev, cell_now = saved[moment]
        tanh_cell = jnp.tanh(cell_now)
        summed = grad_cell + grad_hidden * gate_out * (1.0 - tanh_cell * tanh_cell)
        pre_in = summed * gate_cand * gate_in * (1.0 - gate_in)
        pre_forget = summed * cell_prev * gate_forget * (1.0 - gate_forget)
        pre_cand = summed * gate_in * (1.0 - gate_cand * gate_cand)
        pre_out = grad_hidden * tanh_cell * gate_out * (1.0 - gate_out)
        grad_cell = summed * gate_forget
        grad_gates = jnp.concatenate([pre_in, pre_forget, pre_cand, pre_out], axis=-1).astype(jnp.bfloat16)
        padded = jnp.pad(stacked, ((1, 1), (1, 1), (0, 0)))
        flat_grads = grad_gates.reshape(NH * NW, GATES)
        parts = []
        for tap_row in range(KS):
            for tap_col in range(KS):
                window = padded[tap_row:tap_row + NH, tap_col:tap_col + NW].reshape(NH * NW, chans)
                parts.append(jnp.dot(window.T, flat_grads, preferred_element_type=jnp.float32))
        kernel_total = kernel_total + jnp.stack(parts)
        bias_total = bias_total + lax.optimization_barrier(jnp.sum(grad_gates.astype(jnp.float32), axis=(0, 1)))
        grad_stacked = convolve(grad_gates, flipped)
        grad_hidden = grad_stacked[..., CI:]
        if moment > 0:
            grad_hidden = grad_hidden + cotangent[moment - 1].astype(jnp.float32)
    norm_scale = 1.0 / jnp.sqrt(jnp.float32(STEPS * NH * NW))
    kernel_grad = kernel_total.reshape(KIN, GATES) * norm_scale
    bias_grad = bias_total * norm_scale
    return (hidden_final, grad_hidden, grad_cell, kernel_grad, bias_grad)
```

```python
import functools
import math

import jax
import jax.numpy as jnp
from jax import lax
from jax.experimental import pallas as pl
from jax.experimental.pallas import tpu as pltpu
from jax.sharding import PartitionSpec as P

HC = 128
CI = 32
KS = 3
STEPS = 2
GATES = 512
KIN = 1440
TAPS = 9

NX = 4
NYL = 2
NZ = 8

BF = jnp.bfloat16
F32 = jnp.float32
MESH = pl.DeviceIdType.MESH

RD = 4
CD = 32
WD = 48
EDGE = 8
ROWS_W = 1536
PARTS = 3
PART = ROWS_W // PARTS
HALF = GATES // 2
BIAS_ROW = TAPS * HC + 3 * CI
SIDES = [(dr, dc) for dr in (-1, 0, 1) for dc in (-1, 0, 1) if (dr, dc) != (0, 0)]


def span(step, halo, size):
    if step == 0:
        return (0, size), (halo, size)
    if step > 0:
        return (size - halo, halo), (0, halo)
    return (0, halo), (halo + size, halo)


def place(x, y, z, core):
    return ((y // NYL) * NX + x, ((y % NYL) * NZ + z) * 2 + core)


def body(
    n_rows,
    n_cols,
    frames_ref,
    hidden_ref,
    cell_ref,
    kernel_ref,
    bias_ref,
    cot_ref,
    hid_out,
    gh_out,
    gc_out,
    total_out,
    hl,
    fl,
    cl,
    kl,
    wp,
    fs,
    x32,
    xb,
    s1,
    s2,
    hs1,
    hs2,
    ga,
    sv,
    c1s,
    dcs,
    dg2,
    dg1,
    dgo,
    zs,
    a0,
    o0,
    r0,
    a1,
    r1z,
    r1y,
    r1x,
    a2z,
    a2y,
    a2x,
    r2z,
    r2y,
    r2x,
    r3z,
    r3y,
    r3x,
    gs,
    halo_send,
    halo_recv,
    loc_sem,
    st_send,
    st_recv,
):
    r = lax.axis_index("rows")
    c = lax.axis_index("cols")
    ny = (n_rows // NX) * NYL
    x = lax.rem(r, NX)
    core = lax.rem(c, 2)
    z = lax.rem(c // 2, NZ)
    y = (r // NX) * NYL + c // (2 * NZ)
    size = {"x": NX, "y": ny, "z": NZ}
    mine = {"x": x, "y": y, "z": z}

    def peer(axis, d):
        at = dict(mine)
        at[axis] = lax.rem(mine[axis] + d, size[axis])
        return place(at["x"], at["y"], at["z"], core)

    sibling = place(x, y, z, 1 - core)

    def neighbour(dr, dc):
        return (lax.rem(r + dr + n_rows, n_rows), lax.rem(c + dc + n_cols, n_cols))

    barrier = pltpu.get_barrier_semaphore()
    greet = [neighbour(dr, dc) for dr, dc in SIDES] + [sibling]
    for axis in ("x", "y", "z"):
        greet += [peer(axis, d) for d in range(1, size[axis])]
    for who in greet:
        pl.semaphore_signal(barrier, inc=1, device_id=who, device_id_type=MESH)

    local = []

    def fetch(src, dst):
        copy = pltpu.make_async_copy(src, dst, loc_sem.at[len(local)])
        copy.start()
        local.append(copy)

    fetch(hidden_ref, hl.at[pl.ds(4, RD), pl.ds(16, CD), :])
    fetch(frames_ref, fl.at[1, :, :, pl.ds(128, CD * CI)])
    fetch(cell_ref, cl.at[pl.ds(3, RD), pl.ds(8, CD), :])
    fetch(cot_ref, kl.at[:, pl.ds(2, RD), pl.ds(16, CD), :])
    for tap in range(TAPS):
        a, b = divmod(tap, KS)
        fetch(kernel_ref.at[pl.ds(tap * 160 + CI, HC), :], wp.at[pl.ds(tap * HC, HC), :])
        fetch(
            kernel_ref.at[pl.ds(tap * 160, CI), :],
            wp.at[pl.ds(TAPS * HC + a * 128 + b * CI, CI), :],
        )
    pl.semaphore_wait(barrier, len(greet))

    halos = []
    for i, (dr, dc) in enumerate(SIDES):
        who = neighbour(dr, dc)

        def send(kind, src, dst):
            copy = pltpu.make_async_remote_copy(
                src_ref=src,
                dst_ref=dst,
                send_sem=halo_send.at[i, kind],
                recv_sem=halo_recv.at[i, kind],
                device_id=who,
                device_id_type=MESH,
            )
            copy.start()
            halos.append(copy)

        (rs, rn), (rt, _) = span(dr, 4, RD)
        (cs, cn), (ct, _) = span(dc, 16, CD)
        send(
            0,
            hidden_ref.at[pl.ds(rs, rn), pl.ds(cs, cn), :],
            hl.at[pl.ds(rt, rn), pl.ds(ct, cn), :],
        )
        (ls, ln), (lt, _) = span(dc, 128, CD * CI)
        send(1, frames_ref.at[:, :, pl.ds(ls, ln)], fl.at[1 - dr, :, :, pl.ds(lt, ln)])
        (rs, rn), (rt, _) = span(dr, 3, RD)
        (cs, cn), (ct, _) = span(dc, 8, CD)
        send(
            2,
            cell_ref.at[pl.ds(rs, rn), pl.ds(cs, cn), :],
            cl.at[pl.ds(rt, rn), pl.ds(ct, cn), :],
        )
        (rs, rn), (rt, _) = span(dr, 2, RD)
        (cs, cn), (ct, _) = span(dc, 16, CD)
        send(
            3,
            cot_ref.at[:, pl.ds(rs, rn), pl.ds(cs, cn), :],
            kl.at[:, pl.ds(rt, rn), pl.ds(ct, cn), :],
        )

    for a in range(KS):
        wp[pl.ds(TAPS * HC + a * 128 + 96, 32), :] = jnp.zeros((32, GATES), BF)
    x32[...] = jnp.zeros_like(x32)
    edge = jnp.zeros((EDGE, HC), F32)
    s1[pl.ds(0, EDGE), :] = edge
    s1[pl.ds(EDGE + 12 * WD, EDGE), :] = edge
    s2[pl.ds(0, EDGE), :] = edge
    s2[pl.ds(EDGE + 10 * WD, EDGE), :] = edge
    wide = jnp.zeros((EDGE, TAPS * HC), F32)
    zs[pl.ds(0, EDGE), :] = wide
    zs[pl.ds(EDGE + 8 * WD, EDGE), :] = wide
    fs[...] = jnp.zeros_like(fs)

    at_col = lax.broadcasted_iota(jnp.int32, (WD, HC), 0) - 8
    in_raster = (at_col + c * CD >= 0) & (at_col + c * CD < n_cols * CD)
    col_mask = jnp.where(in_raster, 1.0, 0.0).astype(F32)
    own_mask = jnp.where((at_col >= 0) & (at_col < CD), 1.0, 0.0).astype(F32)

    def row_mask(row):
        there = r * RD + row
        inside = (there >= 0) & (there < n_rows * RD)
        return col_mask * jnp.where(inside, 1.0, 0.0).astype(F32)

    lane = lax.broadcasted_iota(jnp.int32, (16, 1280), 1)
    line = lax.broadcasted_iota(jnp.int32, (16, 1280), 0)
    there_col = lane // CI - 4 + c * CD
    there_row = line - 4 + r * RD
    frame_mask = jnp.where(
        (there_col >= 0)
        & (there_col < n_cols * CD)
        & (there_row >= 0)
        & (there_row < n_rows * RD),
        1.0,
        0.0,
    ).astype(F32)

    for copy in local:
        copy.wait()
    for copy in halos:
        copy.wait_recv()

    for row in range(12):
        vals = hl[row].astype(F32)[8 : 8 + WD, :]
        s1[pl.ds(EDGE + row * WD, WD), :] = vals * row_mask(row - 4)
    for b in range(KS):
        hs1[b] = s1[pl.ds(EDGE + b - 1, 12 * WD), :].astype(BF)
    low = lax.broadcasted_iota(jnp.int32, (12, HC), 1) < CI
    ones = jnp.where(
        lax.broadcasted_iota(jnp.int32, (WD, HC), 1) == 3 * CI, 1.0, 0.0
    ).astype(F32)
    for t in range(STEPS):
        for k in range(3):
            fs[t, pl.ds(4 * k, 4), :] = fl[k, t].astype(F32)
        for g in range(10):
            vals = fs[t, pl.ds(0, 12), pl.ds(g * 128, 128)] * frame_mask[:12, g * 128 : (g + 1) * 128]
            for j in range(4):
                turned = vals if j == 0 else pltpu.roll(vals, 128 - 32 * j, 1)
                x32[t, pl.ds(EDGE + 4 + 4 * g + j, 12, stride=WD), :] = jnp.where(low, turned, 0.0)
        for row in range(12):
            at = EDGE + row * WD
            joined = (
                x32[t, pl.ds(at - 1, WD), :]
                + pltpu.roll(x32[t, pl.ds(at, WD), :], 32, 1)
                + pltpu.roll(x32[t, pl.ds(at + 1, WD), :], 64, 1)
                + ones
            )
            xb[t, pl.ds(row * WD, WD), :] = joined.astype(BF)

    bias = bias_ref[...]

    def gates_of(hs, t, first, count):
        size_m = count * WD
        blocks = [
            hs[b, pl.ds(a * WD, size_m), :] for a in range(KS) for b in range(KS)
        ] + [xb[t, pl.ds((first + a) * WD, size_m), :] for a in range(KS)]
        lhs = jnp.concatenate(blocks, axis=1)
        ga[pl.ds(0, size_m), :] = jnp.dot(lhs, wp[...], preferred_element_type=F32)

    def sigmoid(v):
        return 0.5 * jnp.tanh(0.5 * v) + 0.5

    def activated(row):
        pre = ga[pl.ds(row * WD, WD), :] + bias
        return (
            sigmoid(pre[:, :HC]),
            sigmoid(pre[:, HC : 2 * HC]),
            jnp.tanh(pre[:, 2 * HC : 3 * HC]),
            sigmoid(pre[:, 3 * HC :]),
        )

    gates_of(hs1, 0, 0, 10)
    for k in range(10):
        row = k - 3
        gi, gf, gg, go = activated(k)
        now = gf * cl[k] + gi * gg
        th = jnp.tanh(now)
        c1s[pl.ds(k * WD, WD), :] = now
        if -1 <= row <= 4:
            at = pl.ds((row + 1) * WD, WD)
            for q, val in enumerate((gi, gf, gg, go, th)):
                sv[q, at, :] = val
        h = (go * th).astype(BF).astype(F32)
        s2[pl.ds(EDGE + k * WD, WD), :] = h * row_mask(row)
    for b in range(KS):
        hs2[b] = s2[pl.ds(EDGE + b - 1, 10 * WD), :].astype(BF)

    gates_of(hs2, 1, 1, 8)

    def backward(k, row, s, dh, gi, gf, gg, go, th, before, dg, own_at):
        mask = row_mask(row)
        pres = (
            s * gg * gi * (1.0 - gi),
            s * before * gf * (1.0 - gf),
            s * gi * (1.0 - gg * gg),
            dh * th * go * (1.0 - go),
        )
        for q, pre in enumerate(pres):
            cols = pl.ds(q * HC, HC)
            masked = pre * mask
            dg[pl.ds(k * WD, WD), cols] = masked.astype(BF)
            if 0 <= row < RD:
                dgo[pl.ds(own_at + row * WD, WD), cols] = (masked * own_mask).astype(BF)

    for k in range(8):
        row = k - 2
        gi, gf, gg, go = activated(k)
        before = c1s[pl.ds((k + 1) * WD, WD), :]
        now = gf * before + gi * gg
        th = jnp.tanh(now)
        if 0 <= row < RD:
            hid_out[row] = (go * th)[8 : 8 + CD, :].astype(BF)
        dh = kl[1, k].astype(F32)[8 : 8 + WD, :]
        s = dh * go * (1.0 - th * th)
        if -1 <= row <= 4:
            dcs[pl.ds((row + 1) * WD, WD), :] = s * gf
        backward(k, row, s, dh, gi, gf, gg, go, th, before, dg2, RD * WD)

    def adjoint(dg, count):
        size_m = count * WD
        zs[pl.ds(EDGE, size_m), :] = lax.dot_general(
            dg[pl.ds(0, size_m), :],
            wp[pl.ds(0, TAPS * HC), :],
            (((1,), (1,)), ((), ())),
            preferred_element_type=F32,
        )

    def gathered(k):
        total = None
        for tap in range(TAPS):
            a, b = divmod(tap, KS)
            term = zs[pl.ds(EDGE + (k + 2 - a) * WD - (b - 1), WD), pl.ds(tap * HC, HC)]
            total = term if total is None else total + term
        return total

    adjoint(dg2, 8)
    for k in range(6):
        row = k - 1
        at = pl.ds(k * WD, WD)
        gi, gf, gg, go, th = (sv[q, at, :] for q in range(5))
        dh = gathered(k) + kl[0, k + 1].astype(F32)[8 : 8 + WD, :]
        s = dcs[at, :] + dh * go * (1.0 - th * th)
        if 0 <= row < RD:
            gc_out[row] = (s * gf)[8 : 8 + CD, :]
        backward(k, row, s, dh, gi, gf, gg, go, th, cl[k + 2], dg1, 0)

    count = [0]

    def copy_to(src, dst, who):
        i = count[0]
        count[0] += 1
        return pltpu.make_async_remote_copy(
            src_ref=src,
            dst_ref=dst,
            send_sem=st_send.at[i],
            recv_sem=st_recv.at[i],
            device_id=who,
            device_id_type=MESH,
        )

    sent = []
    mine_at = pl.multiple_of(core * HALF, HALF)
    other_at = pl.multiple_of((1 - core) * HALF, HALF)

    def weight_blocks(p):
        blocks = []
        for q in range(4 * p, 4 * p + 4):
            if q < TAPS:
                a, b = divmod(q, KS)
                one = hs1[b, pl.ds((3 + a) * WD, RD * WD), :]
                two = hs2[b, pl.ds((2 + a) * WD, RD * WD), :]
            else:
                a = q - TAPS
                one = xb[0, pl.ds((3 + a) * WD, RD * WD), :]
                two = xb[1, pl.ds((3 + a) * WD, RD * WD), :]
            blocks.append(jnp.concatenate([one, two], axis=0))
        return jnp.concatenate(blocks, axis=1)

    swaps = []
    for p in range(PARTS):
        lhs = weight_blocks(p)
        dims = (((0,), (0,)), ((), ()))
        a0[p] = lax.dot_general(
            lhs, dgo[:, pl.ds(other_at, HALF)], dims, preferred_element_type=F32
        ).astype(BF)
        copy = copy_to(a0.at[p], r0.at[p], sibling)
        copy.start()
        swaps.append(copy)
        o0[p] = lax.dot_general(
            lhs, dgo[:, pl.ds(mine_at, HALF)], dims, preferred_element_type=F32
        )
    sent += swaps

    adjoint(dg1, 6)
    for row in range(RD):
        gh_out[row] = gathered(row)[8 : 8 + CD, :]

    plans = [
        ("z", "y", "x", r1z, a2z, r2z, r3z),
        ("y", "z", "x", r1y, a2y, r2y, r3y),
        ("x", "z", "y", r1x, a2x, r2x, r3x),
    ]
    state = []
    for p, (ax1, ax2, ax3, r1, a2, r2, r3) in enumerate(plans):
        n1, n2, n3 = size[ax1], size[ax2], size[ax3]
        rows1 = PART // n1
        rows2 = rows1 // n2
        if rows2 >= 16:
            unit = (rows2, HALF)
        else:
            unit = (16, HALF * rows2 // 16)
        across = HALF // unit[1]

        def unit_at(u, unit=unit, across=across):
            return (
                pl.multiple_of((u // across) * unit[0], 16),
                pl.multiple_of(lax.rem(u, across) * unit[1], 128),
            )

        state.append((n1, n2, n3, rows1, unit, unit_at))

    stage1 = []
    for p, (ax1, ax2, ax3, r1, a2, r2, r3) in enumerate(plans):
        n1, n2, n3, rows1, unit, unit_at = state[p]
        swaps[p].wait_recv()
        a1[p] = (o0[p] + r0[p].astype(F32)).astype(BF)
        copies = []
        for d in range(1, n1):
            to = lax.rem(mine[ax1] + d, n1)
            copy = copy_to(
                a1.at[p, pl.ds(pl.multiple_of(to * rows1, 16), rows1), :],
                r1.at[d - 1],
                peer(ax1, d),
            )
            copy.start()
            copies.append(copy)
        stage1.append(copies)
        sent += copies

    stage2 = []
    for p, (ax1, ax2, ax3, r1, a2, r2, r3) in enumerate(plans):
        n1, n2, n3, rows1, unit, unit_at = state[p]
        for copy in stage1[p]:
            copy.wait_recv()
        at = pl.ds(pl.multiple_of(mine[ax1] * rows1, 16), rows1)
        total = a1[p, at, :].astype(F32)
        for d in range(1, n1):
            total = total + r1[d - 1].astype(F32)
        a2[...] = total.astype(BF)
        copies = []
        for d in range(1, n2):
            ur, uc = unit_at(lax.rem(mine[ax2] + d, n2))
            copy = copy_to(
                a2.at[pl.ds(ur, unit[0]), pl.ds(uc, unit[1])], r2.at[d - 1], peer(ax2, d)
            )
            copy.start()
            copies.append(copy)
        stage2.append(copies)
        sent += copies

    stage3 = []
    for p, (ax1, ax2, ax3, r1, a2, r2, r3) in enumerate(plans):
        n1, n2, n3, rows1, unit, unit_at = state[p]
        for copy in stage2[p]:
            copy.wait_recv()
        ur, uc = unit_at(mine[ax2])
        total = a2[pl.ds(ur, unit[0]), pl.ds(uc, unit[1])].astype(F32)
        for d in range(1, n2):
            total = total + r2[d - 1].astype(F32)
        r3[mine[ax3]] = total.astype(BF)
        copies = []
        for d in range(1, n3):
            copy = copy_to(r3.at[mine[ax3]], r3.at[mine[ax3]], peer(ax3, d))
            copy.start()
            copies.append(copy)
        stage3.append(copies)
        sent += copies

    stage4 = []
    for p, (ax1, ax2, ax3, r1, a2, r2, r3) in enumerate(plans):
        n1, n2, n3, rows1, unit, unit_at = state[p]
        for copy in stage3[p]:
            copy.wait_recv()
        total = r3[0].astype(F32)
        for d in range(1, n3):
            total = total + r3[d].astype(F32)
        ur, uc = unit_at(mine[ax2])
        slot = gs.at[
            pl.ds(pl.multiple_of(p * PART + mine[ax1] * rows1 + ur, 16), unit[0]),
            pl.ds(pl.multiple_of(mine_at + uc, 128), unit[1]),
        ]
        slot[...] = total.astype(BF)
        copies = []
        for d in range(1, n2):
            copy = copy_to(slot, slot, peer(ax2, d))
            copy.start()
            copies.append(copy)
        stage4.append(copies)
        sent += copies

    stage5 = []
    for p, (ax1, ax2, ax3, r1, a2, r2, r3) in enumerate(plans):
        n1, n2, n3, rows1, unit, unit_at = state[p]
        for copy in stage4[p]:
            copy.wait_recv()
        slot = gs.at[
            pl.ds(pl.multiple_of(p * PART + mine[ax1] * rows1, 16), rows1),
            pl.ds(mine_at, HALF),
        ]
        copies = []
        for d in range(1, n1):
            copy = copy_to(slot, slot, peer(ax1, d))
            copy.start()
            copies.append(copy)
        stage5.append(copies)
        sent += copies

    stage6 = []
    for p in range(PARTS):
        for copy in stage5[p]:
            copy.wait_recv()
        slot = gs.at[pl.ds(p * PART, PART), pl.ds(mine_at, HALF)]
        copy = copy_to(slot, slot, sibling)
        copy.start()
        stage6.append(copy)
    sent += stage6
    for copy in stage6:
        copy.wait_recv()

    for tap in range(TAPS):
        a, b = divmod(tap, KS)
        total_out[pl.ds(tap * 160, CI), :] = gs[
            pl.ds(TAPS * HC + a * 128 + b * CI, CI), :
        ]
        total_out[pl.ds(tap * 160 + CI, HC), :] = gs[pl.ds(tap * HC, HC), :]
    total_out[pl.ds(KIN, 16), :] = gs[pl.ds(BIAS_ROW, 16), :]

    for copy in halos:
        copy.wait_send()
    for copy in sent:
        copy.wait_send()


def units(n1, n2):
    rows1 = PART // n1
    rows2 = rows1 // n2
    return (rows2, HALF) if rows2 >= 16 else (16, HALF * rows2 // 16)


def shards(frames, hidden_start, cell_start, kernel, gate_bias, cotangent):
    n_rows = lax.axis_size("rows")
    n_cols = lax.axis_size("cols")
    ny = (n_rows // NX) * NYL
    uz = units(NZ, ny)
    uy = units(ny, NZ)
    ux = units(NX, NZ)
    vmem = pltpu.VMEM
    scratch = [
        vmem((12, 64, HC), BF),
        vmem((3, STEPS, RD, 1280), BF),
        vmem((10, WD, HC), F32),
        vmem((STEPS, 8, 64, HC), BF),
        vmem((ROWS_W, GATES), BF),
        vmem((STEPS, 16, 1280), F32),
        vmem((STEPS, 12 * WD + 2 * EDGE, HC), F32),
        vmem((STEPS, 12 * WD, HC), BF),
        vmem((12 * WD + 2 * EDGE, HC), F32),
        vmem((10 * WD + 2 * EDGE, HC), F32),
        vmem((KS, 12 * WD, HC), BF),
        vmem((KS, 10 * WD, HC), BF),
        vmem((10 * WD, GATES), F32),
        vmem((5, 6 * WD, HC), F32),
        vmem((10 * WD, HC), F32),
        vmem((6 * WD, HC), F32),
        vmem((8 * WD, GATES), BF),
        vmem((6 * WD, GATES), BF),
        vmem((2 * RD * WD, GATES), BF),
        vmem((8 * WD + 2 * EDGE, TAPS * HC), F32),
        vmem((PARTS, PART, HALF), BF),
        vmem((PARTS, PART, HALF), F32),
        vmem((PARTS, PART, HALF), BF),
        vmem((PARTS, PART, HALF), BF),
        vmem((NZ - 1, PART // NZ, HALF), BF),
        vmem((ny - 1, PART // ny, HALF), BF),
        vmem((NX - 1, PART // NX, HALF), BF),
        vmem((PART // NZ, HALF), BF),
        vmem((PART // ny, HALF), BF),
        vmem((PART // NX, HALF), BF),
        vmem((ny - 1,) + uz, BF),
        vmem((NZ - 1,) + uy, BF),
        vmem((NZ - 1,) + ux, BF),
        vmem((NX,) + uz, BF),
        vmem((NX,) + uy, BF),
        vmem((ny,) + ux, BF),
        vmem((ROWS_W, GATES), BF),
        pltpu.SemaphoreType.DMA((8, 4)),
        pltpu.SemaphoreType.DMA((8, 4)),
        pltpu.SemaphoreType.DMA((22,)),
        pltpu.SemaphoreType.DMA((stages(n_rows),)),
        pltpu.SemaphoreType.DMA((stages(n_rows),)),
    ]
    anywhere = pl.BlockSpec(memory_space=pl.ANY)
    in_vmem = pl.BlockSpec(memory_space=pltpu.VMEM)
    hidden, grad_hidden, grad_cell, total = pl.pallas_call(
        functools.partial(body, n_rows, n_cols),
        out_shape=(
            jax.ShapeDtypeStruct((RD, CD, HC), BF),
            jax.ShapeDtypeStruct((RD, CD, HC), F32),
            jax.ShapeDtypeStruct((RD, CD, HC), F32),
            jax.ShapeDtypeStruct((KIN + 16, GATES), BF),
        ),
        in_specs=[anywhere, anywhere, anywhere, anywhere, in_vmem, anywhere],
        out_specs=(in_vmem, in_vmem, in_vmem, in_vmem),
        scratch_shapes=scratch,
        compiler_params=pltpu.CompilerParams(
            collective_id=0, has_side_effects=True, vmem_limit_bytes=48 * 1024 * 1024
        ),
    )(frames, hidden_start, cell_start, kernel, gate_bias.reshape(1, GATES), cotangent)
    scale = 1.0 / math.sqrt(STEPS * n_rows * RD * n_cols * CD)
    kernel_grad = total[:KIN].astype(F32) * scale
    bias_grad = total[KIN].astype(F32) * scale
    return hidden, grad_hidden, grad_cell, kernel_grad, bias_grad


def stages(n_rows):
    ny = (n_rows // NX) * NYL
    one = (NZ - 1) + (ny - 1) + (NX - 1)
    two = (ny - 1) + (NZ - 1) + (NZ - 1)
    three = (NX - 1) + (NX - 1) + (ny - 1)
    return 2 * PARTS + 2 * one + 2 * two + three


def solution(mesh):
    placed = (
        P(None, "rows", "cols"),
        P("rows", "cols", None),
        P("rows", "cols", None),
        P(),
        P(),
        P(None, "rows", "cols", None),
    )
    return jax.shard_map(
        shards,
        mesh=mesh,
        in_specs=placed,
        out_specs=(
            P("rows", "cols", None),
            P("rows", "cols", None),
            P("rows", "cols", None),
            P(),
            P(),
        ),
        check_vma=False,
    )
```

```python
import functools
import math

import jax
import jax.numpy as jnp
from jax import lax
from jax.experimental import pallas as pl
from jax.experimental.pallas import tpu as pltpu
from jax.sharding import PartitionSpec as P

HC = 128
CI = 32
KS = 3
STEPS = 2
GATES = 512
KIN = 1440
TAPS = 9

NX = 4
NYL = 2
NZ = 8

BF = jnp.bfloat16
F32 = jnp.float32
MESH = pl.DeviceIdType.MESH

RD = 4
CD = 32
WD = 48
EDGE = 8
ROWS_W = 1536
PARTS = 3
PART = ROWS_W // PARTS
HALF = GATES // 2
BIAS_ROW = TAPS * HC + 3 * CI
SIDES = [(dr, dc) for dr in (-1, 0, 1) for dc in (-1, 0, 1) if (dr, dc) != (0, 0)]


def span(step, halo, size):
    if step == 0:
        return (0, size), (halo, size)
    if step > 0:
        return (size - halo, halo), (0, halo)
    return (0, halo), (halo + size, halo)


def place(x, y, z, core):
    return ((y // NYL) * NX + x, ((y % NYL) * NZ + z) * 2 + core)


def body(
    n_rows,
    n_cols,
    frames_ref,
    hidden_ref,
    cell_ref,
    kernel_ref,
    bias_ref,
    cot_ref,
    hid_out,
    gh_out,
    gc_out,
    total_out,
    hown,
    fl,
    cown,
    kown,
    wp,
    ud,
    st,
    co,
    ud_in,
    st_in,
    co_in,
    fs,
    x32,
    xb,
    s1,
    s2,
    hs1,
    hs2,
    ga,
    sv,
    c0s,
    c1s,
    k1s,
    dcs,
    dg2,
    dgo,
    zs,
    cb,
    ud_c,
    lr_c,
    co_c,
    a0,
    o0,
    r0,
    a1,
    r1z,
    r1y,
    r1x,
    a2z,
    a2y,
    a2x,
    r2z,
    r2y,
    r2x,
    r3z,
    r3y,
    r3x,
    gs,
    halo_send,
    halo_recv,
    late_send,
    late_recv,
    loc_sem,
    st_send,
    st_recv,
):
    r = lax.axis_index("rows")
    c = lax.axis_index("cols")
    ny = (n_rows // NX) * NYL
    x = lax.rem(r, NX)
    core = lax.rem(c, 2)
    z = lax.rem(c // 2, NZ)
    y = (r // NX) * NYL + c // (2 * NZ)
    size = {"x": NX, "y": ny, "z": NZ}
    mine = {"x": x, "y": y, "z": z}

    def peer(axis, d):
        at = dict(mine)
        at[axis] = lax.rem(mine[axis] + d, size[axis])
        return place(at["x"], at["y"], at["z"], core)

    sibling = place(x, y, z, 1 - core)

    def neighbour(dr, dc):
        return (lax.rem(r + dr + n_rows, n_rows), lax.rem(c + dc + n_cols, n_cols))

    barrier = pltpu.get_barrier_semaphore()
    greet = [neighbour(dr, dc) for dr, dc in SIDES] + [sibling]
    for axis in ("x", "y", "z"):
        greet += [peer(axis, d) for d in range(1, size[axis])]
    for who in greet:
        pl.semaphore_signal(barrier, inc=1, device_id=who, device_id_type=MESH)

    local = []

    def fetch(src, dst):
        copy = pltpu.make_async_copy(src, dst, loc_sem.at[len(local)])
        copy.start()
        local.append(copy)

    fetch(hidden_ref, hown)
    fetch(cell_ref, cown)
    fetch(cot_ref, kown)
    fetch(frames_ref, fl.at[1, :, :, pl.ds(128, CD * CI)])
    for tap in range(TAPS):
        a, b = divmod(tap, KS)
        fetch(kernel_ref.at[pl.ds(tap * 160 + CI, HC), :], wp.at[pl.ds(tap * HC, HC), :])
        fetch(
            kernel_ref.at[pl.ds(tap * 160, CI), :],
            wp.at[pl.ds(TAPS * HC + a * 128 + b * CI, CI), :],
        )
    for copy in local[:3]:
        copy.wait()
    fields = (
        ([hown[i] for i in range(RD)], 3),
        ([cown[i] for i in range(RD)], 2),
        ([kown[1, i] for i in range(RD)], 1),
    )

    def edge_rows(step, depth):
        if step == 0:
            return range(RD)
        return range(depth) if step < 0 else range(RD - depth, RD)

    def outgoing(dr, dc):
        pieces = []
        for rows, depth in fields:
            for i in edge_rows(dr, depth):
                piece = rows[i].astype(F32)
                if dc != 0:
                    piece = piece[:8, :] if dc < 0 else piece[CD - 8 :, :]
                pieces.append(piece)
        return jnp.concatenate(pieces, axis=0).astype(BF)

    def slot_of(dr, dc, rows_buf, sides_buf, corners_buf):
        if dc == 0:
            return rows_buf.at[(dr + 1) // 2]
        if dr == 0:
            return sides_buf.at[(dc + 1) // 2]
        return corners_buf.at[(dr + 1) + (dc + 1) // 2]

    for dr, dc in SIDES:
        slot_of(dr, dc, ud, st, co)[...] = outgoing(dr, dc)
    pl.semaphore_wait(barrier, len(greet))

    halos = []
    for i, (dr, dc) in enumerate(SIDES):
        who = neighbour(dr, dc)
        (ls, ln), (lt, _) = span(dc, 128, CD * CI)
        for kind, (src, dst) in enumerate(
            (
                (slot_of(dr, dc, ud, st, co), slot_of(dr, dc, ud_in, st_in, co_in)),
                (frames_ref.at[:, :, pl.ds(ls, ln)], fl.at[1 - dr, :, :, pl.ds(lt, ln)]),
            )
        ):
            copy = pltpu.make_async_remote_copy(
                src_ref=src,
                dst_ref=dst,
                send_sem=halo_send.at[i, kind],
                recv_sem=halo_recv.at[i, kind],
                device_id=who,
                device_id_type=MESH,
            )
            copy.start()
            halos.append(copy)

    for a in range(KS):
        wp[pl.ds(TAPS * HC + a * 128 + 96, 32), :] = jnp.zeros((32, GATES), BF)
    x32[...] = jnp.zeros_like(x32)
    edge = jnp.zeros((EDGE, HC), F32)
    s1[pl.ds(0, EDGE), :] = edge
    s1[pl.ds(EDGE + 10 * WD, EDGE), :] = edge
    s2[pl.ds(0, EDGE), :] = edge
    s2[pl.ds(EDGE + 8 * WD, EDGE), :] = edge
    wide = jnp.zeros((EDGE, TAPS * HC), F32)
    zs[pl.ds(0, EDGE), :] = wide
    zs[pl.ds(EDGE + 6 * WD, EDGE), :] = wide
    fs[...] = jnp.zeros_like(fs)

    at_col = lax.broadcasted_iota(jnp.int32, (WD, HC), 0) - 8
    in_raster = (at_col + c * CD >= 0) & (at_col + c * CD < n_cols * CD)
    col_mask = jnp.where(in_raster, 1.0, 0.0).astype(F32)
    own_mask = jnp.where((at_col >= 0) & (at_col < CD), 1.0, 0.0).astype(F32)

    def row_mask(row):
        there = r * RD + row
        inside = (there >= 0) & (there < n_rows * RD)
        return col_mask * jnp.where(inside, 1.0, 0.0).astype(F32)

    lane = lax.broadcasted_iota(jnp.int32, (16, 1280), 1)
    line = lax.broadcasted_iota(jnp.int32, (16, 1280), 0)
    there_col = lane // CI - 4 + c * CD
    there_row = line - 4 + r * RD
    frame_mask = jnp.where(
        (there_col >= 0)
        & (there_col < n_cols * CD)
        & (there_row >= 0)
        & (there_row < n_rows * RD),
        1.0,
        0.0,
    ).astype(F32)

    for copy in local[3:]:
        copy.wait()
    for copy in halos:
        copy.wait_recv()

    def incoming(dr, dc):
        return slot_of(-dr, -dc, ud_in, st_in, co_in)[...].astype(F32)

    around = {side: incoming(*side) for side in SIDES}

    def field_row(which, row):
        rows, depth = fields[which]
        before = [d for _, d in fields[:which]]
        dr = -1 if row < 0 else (1 if row >= RD else 0)
        i = row + depth if row < 0 else (row - RD if row >= RD else row)
        parts = []
        for dc in (-1, 0, 1):
            if (dr, dc) == (0, 0):
                parts.append(rows[row].astype(F32))
                continue
            wide_row = CD if dc == 0 else 8
            skip = (RD * which if dr == 0 else sum(before)) * wide_row
            parts.append(around[dr, dc][skip + i * wide_row : skip + (i + 1) * wide_row, :])
        return jnp.concatenate(parts, axis=0)

    for k in range(10):
        s1[pl.ds(EDGE + k * WD, WD), :] = field_row(0, k - 3) * row_mask(k - 3)
    for k in range(8):
        c0s[pl.ds(k * WD, WD), :] = field_row(1, k - 2)
    for k in range(6):
        k1s[pl.ds(k * WD, WD), :] = field_row(2, k - 1)
    for b in range(KS):
        hs1[b] = s1[pl.ds(EDGE + b - 1, 10 * WD), :].astype(BF)
    low = lax.broadcasted_iota(jnp.int32, (12, HC), 1) < CI
    ones = jnp.where(
        lax.broadcasted_iota(jnp.int32, (WD, HC), 1) == 3 * CI, 1.0, 0.0
    ).astype(F32)
    for t in range(STEPS):
        for k in range(3):
            fs[t, pl.ds(4 * k, 4), :] = fl[k, t].astype(F32)
        for g in range(10):
            vals = fs[t, pl.ds(0, 12), pl.ds(g * 128, 128)] * frame_mask[:12, g * 128 : (g + 1) * 128]
            for j in range(4):
                turned = vals if j == 0 else pltpu.roll(vals, 128 - 32 * j, 1)
                x32[t, pl.ds(EDGE + 4 + 4 * g + j, 12, stride=WD), :] = jnp.where(low, turned, 0.0)
        for row in range(12):
            at = EDGE + row * WD
            joined = (
                x32[t, pl.ds(at - 1, WD), :]
                + pltpu.roll(x32[t, pl.ds(at, WD), :], 32, 1)
                + pltpu.roll(x32[t, pl.ds(at + 1, WD), :], 64, 1)
                + ones
            )
            xb[t, pl.ds(row * WD, WD), :] = joined.astype(BF)

    bias = bias_ref[...]

    def gates_of(hs, t, first, count):
        size_m = count * WD
        blocks = [
            hs[b, pl.ds(a * WD, size_m), :] for a in range(KS) for b in range(KS)
        ] + [xb[t, pl.ds((first + a) * WD, size_m), :] for a in range(KS)]
        lhs = jnp.concatenate(blocks, axis=1)
        ga[pl.ds(0, size_m), :] = jnp.dot(lhs, wp[...], preferred_element_type=F32)

    def sigmoid(v):
        return 0.5 * jnp.tanh(0.5 * v) + 0.5

    def activated(row):
        pre = ga[pl.ds(row * WD, WD), :] + bias
        return (
            sigmoid(pre[:, :HC]),
            sigmoid(pre[:, HC : 2 * HC]),
            jnp.tanh(pre[:, 2 * HC : 3 * HC]),
            sigmoid(pre[:, 3 * HC :]),
        )

    gates_of(hs1, 0, 1, 8)
    for k in range(8):
        row = k - 2
        gi, gf, gg, go = activated(k)
        now = gf * c0s[pl.ds(k * WD, WD), :] + gi * gg
        th = jnp.tanh(now)
        c1s[pl.ds(k * WD, WD), :] = now
        if 0 <= row < RD:
            at = pl.ds(row * WD, WD)
            for q, val in enumerate((gi, gf, gg, go, th)):
                sv[q, at, :] = val
        h = (go * th).astype(BF).astype(F32)
        s2[pl.ds(EDGE + k * WD, WD), :] = h * row_mask(row)
    for b in range(KS):
        hs2[b] = s2[pl.ds(EDGE + b - 1, 8 * WD), :].astype(BF)

    gates_of(hs2, 1, 2, 6)

    def pre_grads(s, dh, gi, gf, gg, go, th, before):
        return (
            s * gg * gi * (1.0 - gi),
            s * before * gf * (1.0 - gf),
            s * gi * (1.0 - gg * gg),
            dh * th * go * (1.0 - go),
        )

    for k in range(6):
        row = k - 1
        gi, gf, gg, go = activated(k)
        before = c1s[pl.ds((k + 1) * WD, WD), :]
        now = gf * before + gi * gg
        th = jnp.tanh(now)
        dh = k1s[pl.ds(k * WD, WD), :]
        s = dh * go * (1.0 - th * th)
        if 0 <= row < RD:
            hid_out[row] = (go * th)[8 : 8 + CD, :].astype(BF)
            dcs[pl.ds(row * WD, WD), :] = s * gf
        mask = row_mask(row)
        for q, pre in enumerate(pre_grads(s, dh, gi, gf, gg, go, th, before)):
            cols = pl.ds(q * HC, HC)
            dg2[pl.ds(k * WD, WD), cols] = (pre * mask).astype(BF)
            if 0 <= row < RD:
                dgo[pl.ds((RD + row) * WD, WD), cols] = (pre * own_mask).astype(BF)

    def adjoint(dg, count):
        size_m = count * WD
        zs[pl.ds(EDGE, size_m), :] = lax.dot_general(
            dg[pl.ds(0, size_m), :],
            wp[pl.ds(0, TAPS * HC), :],
            (((1,), (1,)), ((), ())),
            preferred_element_type=F32,
        )

    def gathered(k, count):
        total = None
        for tap in range(TAPS):
            a, b = divmod(tap, KS)
            row = k + 2 - a
            if not 0 <= row < count:
                continue
            term = zs[pl.ds(EDGE + row * WD - (b - 1), WD), pl.ds(tap * HC, HC)]
            total = term if total is None else total + term
        return total

    adjoint(dg2, 6)
    for row in range(RD):
        at = pl.ds(row * WD, WD)
        gi, gf, gg, go, th = (sv[q, at, :] for q in range(5))
        inner = gathered(row, 6)
        cot = kown[0, row].astype(F32)
        blank = jnp.zeros((8, HC), F32)
        dh = inner + jnp.concatenate([blank, cot, blank], axis=0)
        s = dcs[at, :] + dh * go * (1.0 - th * th)
        gc_out[row] = (s * gf)[8 : 8 + CD, :]
        before = c0s[pl.ds((row + 2) * WD, WD), :]
        for q, pre in enumerate(pre_grads(s, dh, gi, gf, gg, go, th, before)):
            dgo[at, pl.ds(q * HC, HC)] = (pre * own_mask).astype(BF)

    count = [0]

    def copy_to(src, dst, who):
        i = count[0]
        count[0] += 1
        return pltpu.make_async_remote_copy(
            src_ref=src,
            dst_ref=dst,
            send_sem=st_send.at[i],
            recv_sem=st_recv.at[i],
            device_id=who,
            device_id_type=MESH,
        )

    sent = []
    mine_at = pl.multiple_of(core * HALF, HALF)
    other_at = pl.multiple_of((1 - core) * HALF, HALF)

    def weight_blocks(p):
        blocks = []
        for q in range(4 * p, 4 * p + 4):
            if q < TAPS:
                a, b = divmod(q, KS)
                one = hs1[b, pl.ds((2 + a) * WD, RD * WD), :]
                two = hs2[b, pl.ds((1 + a) * WD, RD * WD), :]
            else:
                a = q - TAPS
                one = xb[0, pl.ds((3 + a) * WD, RD * WD), :]
                two = xb[1, pl.ds((3 + a) * WD, RD * WD), :]
            blocks.append(jnp.concatenate([one, two], axis=0))
        return jnp.concatenate(blocks, axis=1)

    swaps = []
    for p in range(PARTS):
        lhs = weight_blocks(p)
        dims = (((0,), (0,)), ((), ()))
        a0[p] = lax.dot_general(
            lhs, dgo[:, pl.ds(other_at, HALF)], dims, preferred_element_type=F32
        ).astype(BF)
        copy = copy_to(a0.at[p], r0.at[p], sibling)
        copy.start()
        swaps.append(copy)
        o0[p] = lax.dot_general(
            lhs, dgo[:, pl.ds(mine_at, HALF)], dims, preferred_element_type=F32
        )
    sent += swaps

    adjoint(dgo, RD)
    zs[pl.ds(EDGE + RD * WD, EDGE), :] = wide
    for k in range(RD + 2):
        cb[k] = gathered(k - 2, RD)
    plans = [
        ("z", "y", "x", r1z, a2z, r2z, r3z),
        ("y", "z", "x", r1y, a2y, r2y, r3y),
        ("x", "z", "y", r1x, a2x, r2x, r3x),
    ]
    state = []
    for p, (ax1, ax2, ax3, r1, a2, r2, r3) in enumerate(plans):
        n1, n2, n3 = size[ax1], size[ax2], size[ax3]
        rows1 = PART // n1
        rows2 = rows1 // n2
        if rows2 >= 16:
            unit = (rows2, HALF)
        else:
            unit = (16, HALF * rows2 // 16)
        across = HALF // unit[1]

        def unit_at(u, unit=unit, across=across):
            return (
                pl.multiple_of((u // across) * unit[0], 16),
                pl.multiple_of(lax.rem(u, across) * unit[1], 128),
            )

        state.append((n1, n2, n3, rows1, unit, unit_at))

    stage1 = []
    for p, (ax1, ax2, ax3, r1, a2, r2, r3) in enumerate(plans):
        n1, n2, n3, rows1, unit, unit_at = state[p]
        swaps[p].wait_recv()
        a1[p] = (o0[p] + r0[p].astype(F32)).astype(BF)
        copies = []
        for d in range(1, n1):
            to = lax.rem(mine[ax1] + d, n1)
            copy = copy_to(
                a1.at[p, pl.ds(pl.multiple_of(to * rows1, 16), rows1), :],
                r1.at[d - 1],
                peer(ax1, d),
            )
            copy.start()
            copies.append(copy)
        stage1.append(copies)
        sent += copies

    stage2 = []
    for p, (ax1, ax2, ax3, r1, a2, r2, r3) in enumerate(plans):
        n1, n2, n3, rows1, unit, unit_at = state[p]
        for copy in stage1[p]:
            copy.wait_recv()
        at = pl.ds(pl.multiple_of(mine[ax1] * rows1, 16), rows1)
        total = a1[p, at, :].astype(F32)
        for d in range(1, n1):
            total = total + r1[d - 1].astype(F32)
        a2[...] = total.astype(BF)
        copies = []
        for d in range(1, n2):
            ur, uc = unit_at(lax.rem(mine[ax2] + d, n2))
            copy = copy_to(
                a2.at[pl.ds(ur, unit[0]), pl.ds(uc, unit[1])], r2.at[d - 1], peer(ax2, d)
            )
            copy.start()
            copies.append(copy)
        stage2.append(copies)
        sent += copies

    late = []
    for i, (dr, dc) in enumerate(SIDES):
        rows_at = pl.ds(0, 1) if dr < 0 else (pl.ds(RD + 1, 1) if dr > 0 else pl.ds(1, RD))
        cols_at = pl.ds(0, 8) if dc < 0 else (pl.ds(8 + CD, 8) if dc > 0 else pl.ds(8, CD))
        copy = pltpu.make_async_remote_copy(
            src_ref=cb.at[rows_at, cols_at, :],
            dst_ref=slot_of(dr, dc, ud_c, lr_c, co_c),
            send_sem=late_send.at[i],
            recv_sem=late_recv.at[i],
            device_id=neighbour(dr, dc),
            device_id_type=MESH,
        )
        copy.start()
        late.append(copy)
    sent += late

    stage3 = []
    for p, (ax1, ax2, ax3, r1, a2, r2, r3) in enumerate(plans):
        n1, n2, n3, rows1, unit, unit_at = state[p]
        for copy in stage2[p]:
            copy.wait_recv()
        ur, uc = unit_at(mine[ax2])
        total = a2[pl.ds(ur, unit[0]), pl.ds(uc, unit[1])].astype(F32)
        for d in range(1, n2):
            total = total + r2[d - 1].astype(F32)
        r3[mine[ax3]] = total.astype(BF)
        copies = []
        for d in range(1, n3):
            copy = copy_to(r3.at[mine[ax3]], r3.at[mine[ax3]], peer(ax3, d))
            copy.start()
            copies.append(copy)
        stage3.append(copies)
        sent += copies

    stage4 = []
    for p, (ax1, ax2, ax3, r1, a2, r2, r3) in enumerate(plans):
        n1, n2, n3, rows1, unit, unit_at = state[p]
        for copy in stage3[p]:
            copy.wait_recv()
        total = r3[0].astype(F32)
        for d in range(1, n3):
            total = total + r3[d].astype(F32)
        ur, uc = unit_at(mine[ax2])
        slot = gs.at[
            pl.ds(pl.multiple_of(p * PART + mine[ax1] * rows1 + ur, 16), unit[0]),
            pl.ds(pl.multiple_of(mine_at + uc, 128), unit[1]),
        ]
        slot[...] = total.astype(BF)
        copies = []
        for d in range(1, n2):
            copy = copy_to(slot, slot, peer(ax2, d))
            copy.start()
            copies.append(copy)
        stage4.append(copies)
        sent += copies

    stage5 = []
    for p, (ax1, ax2, ax3, r1, a2, r2, r3) in enumerate(plans):
        n1, n2, n3, rows1, unit, unit_at = state[p]
        for copy in stage4[p]:
            copy.wait_recv()
        slot = gs.at[
            pl.ds(pl.multiple_of(p * PART + mine[ax1] * rows1, 16), rows1),
            pl.ds(mine_at, HALF),
        ]
        copies = []
        for d in range(1, n1):
            copy = copy_to(slot, slot, peer(ax1, d))
            copy.start()
            copies.append(copy)
        stage5.append(copies)
        sent += copies

    for copy in late:
        copy.wait_recv()
    for row in range(RD):
        gh_out[row] = cb[row + 1, pl.ds(8, CD), :]
    for dr, dc in SIDES:
        inside = (r - dr >= 0) & (r - dr < n_rows) & (c - dc >= 0) & (c - dc < n_cols)
        keep = jnp.where(inside, 1.0, 0.0).astype(F32)
        rows_at = pl.ds(RD - 1, 1) if dr < 0 else (pl.ds(0, 1) if dr > 0 else pl.ds(0, RD))
        cols_at = pl.ds(CD - 8, 8) if dc < 0 else (pl.ds(0, 8) if dc > 0 else pl.ds(0, CD))
        terms = slot_of(dr, dc, ud_c, lr_c, co_c)[...] * keep
        gh_out[rows_at, cols_at, :] = gh_out[rows_at, cols_at, :] + terms

    stage6 = []
    for p in range(PARTS):
        for copy in stage5[p]:
            copy.wait_recv()
        slot = gs.at[pl.ds(p * PART, PART), pl.ds(mine_at, HALF)]
        copy = copy_to(slot, slot, sibling)
        copy.start()
        stage6.append(copy)
    sent += stage6
    for copy in stage6:
        copy.wait_recv()

    total_out[...] = gs[...]

    for copy in halos:
        copy.wait_send()
    for copy in sent:
        copy.wait_send()


def units(n1, n2):
    rows1 = PART // n1
    rows2 = rows1 // n2
    return (rows2, HALF) if rows2 >= 16 else (16, HALF * rows2 // 16)


def shards(frames, hidden_start, cell_start, kernel, gate_bias, cotangent):
    n_rows = lax.axis_size("rows")
    n_cols = lax.axis_size("cols")
    ny = (n_rows // NX) * NYL
    uz = units(NZ, ny)
    uy = units(ny, NZ)
    ux = units(NX, NZ)
    vmem = pltpu.VMEM
    scratch = [
        vmem((RD, CD, HC), BF),
        vmem((3, STEPS, RD, 1280), BF),
        vmem((RD, CD, HC), F32),
        vmem((STEPS, RD, CD, HC), BF),
        vmem((ROWS_W, GATES), BF),
        vmem((2, 6 * CD, HC), BF),
        vmem((2, 3 * RD * 8, HC), BF),
        vmem((4, 6 * 8, HC), BF),
        vmem((2, 6 * CD, HC), BF),
        vmem((2, 3 * RD * 8, HC), BF),
        vmem((4, 6 * 8, HC), BF),
        vmem((STEPS, 16, 1280), F32),
        vmem((STEPS, 12 * WD + 2 * EDGE, HC), F32),
        vmem((STEPS, 12 * WD, HC), BF),
        vmem((10 * WD + 2 * EDGE, HC), F32),
        vmem((8 * WD + 2 * EDGE, HC), F32),
        vmem((KS, 10 * WD, HC), BF),
        vmem((KS, 8 * WD, HC), BF),
        vmem((8 * WD, GATES), F32),
        vmem((5, RD * WD, HC), F32),
        vmem((8 * WD, HC), F32),
        vmem((8 * WD, HC), F32),
        vmem((6 * WD, HC), F32),
        vmem((RD * WD, HC), F32),
        vmem((6 * WD, GATES), BF),
        vmem((2 * RD * WD, GATES), BF),
        vmem((6 * WD + 2 * EDGE, TAPS * HC), F32),
        vmem((RD + 2, WD, HC), F32),
        vmem((2, 1, CD, HC), F32),
        vmem((2, RD, 8, HC), F32),
        vmem((4, 1, 8, HC), F32),
        vmem((PARTS, PART, HALF), BF),
        vmem((PARTS, PART, HALF), F32),
        vmem((PARTS, PART, HALF), BF),
        vmem((PARTS, PART, HALF), BF),
        vmem((NZ - 1, PART // NZ, HALF), BF),
        vmem((ny - 1, PART // ny, HALF), BF),
        vmem((NX - 1, PART // NX, HALF), BF),
        vmem((PART // NZ, HALF), BF),
        vmem((PART // ny, HALF), BF),
        vmem((PART // NX, HALF), BF),
        vmem((ny - 1,) + uz, BF),
        vmem((NZ - 1,) + uy, BF),
        vmem((NZ - 1,) + ux, BF),
        vmem((NX,) + uz, BF),
        vmem((NX,) + uy, BF),
        vmem((ny,) + ux, BF),
        vmem((ROWS_W, GATES), BF),
        pltpu.SemaphoreType.DMA((8, 2)),
        pltpu.SemaphoreType.DMA((8, 2)),
        pltpu.SemaphoreType.DMA((8,)),
        pltpu.SemaphoreType.DMA((8,)),
        pltpu.SemaphoreType.DMA((22,)),
        pltpu.SemaphoreType.DMA((stages(n_rows),)),
        pltpu.SemaphoreType.DMA((stages(n_rows),)),
    ]
    in_hbm = pl.BlockSpec(memory_space=pltpu.HBM)
    in_vmem = pl.BlockSpec(memory_space=pltpu.VMEM)
    hidden, grad_hidden, grad_cell, total = pl.pallas_call(
        functools.partial(body, n_rows, n_cols),
        out_shape=(
            jax.ShapeDtypeStruct((RD, CD, HC), BF),
            jax.ShapeDtypeStruct((RD, CD, HC), F32),
            jax.ShapeDtypeStruct((RD, CD, HC), F32),
            jax.ShapeDtypeStruct((ROWS_W, GATES), BF),
        ),
        in_specs=[in_hbm, in_hbm, in_hbm, in_hbm, in_vmem, in_hbm],
        out_specs=(in_vmem, in_vmem, in_vmem, in_vmem),
        scratch_shapes=scratch,
        compiler_params=pltpu.CompilerParams(
            collective_id=0, has_side_effects=True, vmem_limit_bytes=48 * 1024 * 1024
        ),
    )(frames, hidden_start, cell_start, kernel, gate_bias.reshape(1, GATES), cotangent)
    scale = 1.0 / math.sqrt(STEPS * n_rows * RD * n_cols * CD)
    outs = pl.pallas_call(
        functools.partial(finish, scale),
        out_shape=(
            jax.ShapeDtypeStruct((RD, CD, HC), BF),
            jax.ShapeDtypeStruct((RD, CD, HC), F32),
            jax.ShapeDtypeStruct((RD, CD, HC), F32),
            jax.ShapeDtypeStruct((KIN, GATES), F32),
            jax.ShapeDtypeStruct((1, GATES), F32),
        ),
        in_specs=[in_vmem] * 4,
        out_specs=(in_hbm,) * 5,
        scratch_shapes=[
            vmem((KIN, GATES), F32),
            vmem((1, GATES), F32),
            pltpu.SemaphoreType.DMA((TAPS + 4,)),
        ],
        compiler_params=pltpu.CompilerParams(vmem_limit_bytes=16 * 1024 * 1024),
    )(hidden, grad_hidden, grad_cell, total)
    return outs[0], outs[1], outs[2], outs[3], outs[4].reshape(GATES)


def finish(scale, hid, gh, gc, total, hid_out, gh_out, gc_out, kg_out, bg_out, kg, bg, sem):
    copies = []

    def put(src, dst):
        copy = pltpu.make_async_copy(src, dst, sem.at[len(copies)])
        copy.start()
        copies.append(copy)

    put(hid, hid_out)
    put(gh, gh_out)
    put(gc, gc_out)
    for tap in range(TAPS):
        a, b = divmod(tap, KS)
        first = TAPS * HC + a * 128 + b * CI
        at = tap * 160
        kg[pl.ds(at, CI), :] = total[pl.ds(first, CI), :].astype(F32) * scale
        kg[pl.ds(at + CI, HC), :] = total[pl.ds(tap * HC, HC), :].astype(F32) * scale
        put(kg.at[pl.ds(at, 160), :], kg_out.at[pl.ds(at, 160), :])
    bg[...] = total[pl.ds(BIAS_ROW, 16), :].astype(F32)[:1, :] * scale
    put(bg, bg_out)
    for copy in copies:
        copy.wait()


def stages(n_rows):
    ny = (n_rows // NX) * NYL
    one = (NZ - 1) + (ny - 1) + (NX - 1)
    two = (ny - 1) + (NZ - 1) + (NZ - 1)
    three = (NX - 1) + (NX - 1) + (ny - 1)
    return 2 * PARTS + 2 * one + 2 * two + three


def solution(mesh):
    placed = (
        P(None, "rows", "cols"),
        P("rows", "cols", None),
        P("rows", "cols", None),
        P(),
        P(),
        P(None, "rows", "cols", None),
    )
    return jax.shard_map(
        shards,
        mesh=mesh,
        in_specs=placed,
        out_specs=(
            P("rows", "cols", None),
            P("rows", "cols", None),
            P("rows", "cols", None),
            P(),
            P(),
        ),
        check_vma=False,
    )
```

```python
import functools
import math

import jax
import jax.numpy as jnp
from jax import lax
from jax.experimental import pallas as pl
from jax.experimental.pallas import tpu as pltpu
from jax.sharding import PartitionSpec as P

HC = 128
CI = 32
KS = 3
STEPS = 2
GATES = 512
KIN = 1440
TAPS = 9

NX = 4
NYL = 2
NZ = 8

BF = jnp.bfloat16
F32 = jnp.float32
MESH = pl.DeviceIdType.MESH

RD = 4
CD = 32
WD = 48
EDGE = 8
ROWS_W = 1536
PARTS = 3
PART = ROWS_W // PARTS
HALF = GATES // 2
BIAS_ROW = TAPS * HC + 3 * CI
SIDES = [(dr, dc) for dr in (-1, 0, 1) for dc in (-1, 0, 1) if (dr, dc) != (0, 0)]


def span(step, halo, size):
    if step == 0:
        return (0, size), (halo, size)
    if step > 0:
        return (size - halo, halo), (0, halo)
    return (0, halo), (halo + size, halo)


def place(x, y, z, core):
    return ((y // NYL) * NX + x, ((y % NYL) * NZ + z) * 2 + core)


def body(
    n_rows,
    n_cols,
    frames_ref,
    hidden_ref,
    cell_ref,
    kernel_ref,
    bias_ref,
    cot_ref,
    hid_hbm,
    gh_hbm,
    gc_hbm,
    total_hbm,
    hid_out,
    gh_out,
    gc_out,
    bias_in,
    hown,
    fl,
    cown,
    kown,
    wp,
    ud,
    st,
    co,
    ud_in,
    st_in,
    co_in,
    fs,
    x32,
    xb,
    s1,
    s2,
    hs1,
    hs2,
    ga,
    sv,
    c0s,
    c1s,
    k1s,
    dcs,
    dg2,
    dgo,
    zs,
    cb,
    ud_c,
    lr_c,
    co_c,
    a0,
    o0,
    r0,
    a1,
    r1z,
    r1y,
    r1x,
    a2z,
    a2y,
    a2x,
    r2z,
    r2y,
    r2x,
    r3z,
    r3y,
    r3x,
    gs,
    halo_send,
    halo_recv,
    late_send,
    late_recv,
    loc_sem,
    out_sem,
    st_send,
    st_recv,
):
    r = lax.axis_index("rows")
    c = lax.axis_index("cols")
    ny = (n_rows // NX) * NYL
    x = lax.rem(r, NX)
    core = lax.rem(c, 2)
    z = lax.rem(c // 2, NZ)
    y = (r // NX) * NYL + c // (2 * NZ)
    size = {"x": NX, "y": ny, "z": NZ}
    mine = {"x": x, "y": y, "z": z}

    def peer(axis, d):
        at = dict(mine)
        at[axis] = lax.rem(mine[axis] + d, size[axis])
        return place(at["x"], at["y"], at["z"], core)

    sibling = place(x, y, z, 1 - core)

    def neighbour(dr, dc):
        return (lax.rem(r + dr + n_rows, n_rows), lax.rem(c + dc + n_cols, n_cols))

    barrier = pltpu.get_barrier_semaphore()
    greet = [neighbour(dr, dc) for dr, dc in SIDES] + [sibling]
    for axis in ("x", "y", "z"):
        greet += [peer(axis, d) for d in range(1, size[axis])]
    for who in greet:
        pl.semaphore_signal(barrier, inc=1, device_id=who, device_id_type=MESH)

    local = []

    def fetch(src, dst):
        copy = pltpu.make_async_copy(src, dst, loc_sem.at[len(local)])
        copy.start()
        local.append(copy)

    fetch(hidden_ref, hown)
    fetch(cell_ref, cown)
    fetch(cot_ref, kown)
    fetch(frames_ref, fl.at[1, :, :, pl.ds(128, CD * CI)])
    fetch(bias_ref, bias_in)
    for tap in range(TAPS):
        a, b = divmod(tap, KS)
        fetch(kernel_ref.at[pl.ds(tap * 160 + CI, HC), :], wp.at[pl.ds(tap * HC, HC), :])
        fetch(
            kernel_ref.at[pl.ds(tap * 160, CI), :],
            wp.at[pl.ds(TAPS * HC + a * 128 + b * CI, CI), :],
        )
    for copy in local[:3]:
        copy.wait()
    fields = (
        ([hown[i] for i in range(RD)], 3),
        ([cown[i] for i in range(RD)], 2),
        ([kown[1, i] for i in range(RD)], 1),
    )

    def edge_rows(step, depth):
        if step == 0:
            return range(RD)
        return range(depth) if step < 0 else range(RD - depth, RD)

    def outgoing(dr, dc):
        pieces = []
        for rows, depth in fields:
            for i in edge_rows(dr, depth):
                piece = rows[i].astype(F32)
                if dc != 0:
                    piece = piece[:8, :] if dc < 0 else piece[CD - 8 :, :]
                pieces.append(piece)
        return jnp.concatenate(pieces, axis=0).astype(BF)

    def slot_of(dr, dc, rows_buf, sides_buf, corners_buf):
        if dc == 0:
            return rows_buf.at[(dr + 1) // 2]
        if dr == 0:
            return sides_buf.at[(dc + 1) // 2]
        return corners_buf.at[(dr + 1) + (dc + 1) // 2]

    for dr, dc in SIDES:
        slot_of(dr, dc, ud, st, co)[...] = outgoing(dr, dc)
    pl.semaphore_wait(barrier, len(greet))

    halos = []
    for i, (dr, dc) in enumerate(SIDES):
        who = neighbour(dr, dc)
        (ls, ln), (lt, _) = span(dc, 128, CD * CI)
        for kind, (src, dst) in enumerate(
            (
                (slot_of(dr, dc, ud, st, co), slot_of(dr, dc, ud_in, st_in, co_in)),
                (frames_ref.at[:, :, pl.ds(ls, ln)], fl.at[1 - dr, :, :, pl.ds(lt, ln)]),
            )
        ):
            copy = pltpu.make_async_remote_copy(
                src_ref=src,
                dst_ref=dst,
                send_sem=halo_send.at[i, kind],
                recv_sem=halo_recv.at[i, kind],
                device_id=who,
                device_id_type=MESH,
            )
            copy.start()
            halos.append(copy)

    for a in range(KS):
        wp[pl.ds(TAPS * HC + a * 128 + 96, 32), :] = jnp.zeros((32, GATES), BF)
    x32[...] = jnp.zeros_like(x32)
    edge = jnp.zeros((EDGE, HC), F32)
    s1[pl.ds(0, EDGE), :] = edge
    s1[pl.ds(EDGE + 10 * WD, EDGE), :] = edge
    s2[pl.ds(0, EDGE), :] = edge
    s2[pl.ds(EDGE + 8 * WD, EDGE), :] = edge
    wide = jnp.zeros((EDGE, TAPS * HC), F32)
    zs[pl.ds(0, EDGE), :] = wide
    zs[pl.ds(EDGE + 6 * WD, EDGE), :] = wide
    fs[...] = jnp.zeros_like(fs)

    at_col = lax.broadcasted_iota(jnp.int32, (WD, HC), 0) - 8
    in_raster = (at_col + c * CD >= 0) & (at_col + c * CD < n_cols * CD)
    col_mask = jnp.where(in_raster, 1.0, 0.0).astype(F32)
    own_mask = jnp.where((at_col >= 0) & (at_col < CD), 1.0, 0.0).astype(F32)

    def row_mask(row):
        there = r * RD + row
        inside = (there >= 0) & (there < n_rows * RD)
        return col_mask * jnp.where(inside, 1.0, 0.0).astype(F32)

    lane = lax.broadcasted_iota(jnp.int32, (16, 1280), 1)
    line = lax.broadcasted_iota(jnp.int32, (16, 1280), 0)
    there_col = lane // CI - 4 + c * CD
    there_row = line - 4 + r * RD
    frame_mask = jnp.where(
        (there_col >= 0)
        & (there_col < n_cols * CD)
        & (there_row >= 0)
        & (there_row < n_rows * RD),
        1.0,
        0.0,
    ).astype(F32)

    for copy in local[3:]:
        copy.wait()
    for copy in halos:
        copy.wait_recv()

    def incoming(dr, dc):
        return slot_of(-dr, -dc, ud_in, st_in, co_in)[...].astype(F32)

    around = {side: incoming(*side) for side in SIDES}

    def field_row(which, row):
        rows, depth = fields[which]
        before = [d for _, d in fields[:which]]
        dr = -1 if row < 0 else (1 if row >= RD else 0)
        i = row + depth if row < 0 else (row - RD if row >= RD else row)
        parts = []
        for dc in (-1, 0, 1):
            if (dr, dc) == (0, 0):
                parts.append(rows[row].astype(F32))
                continue
            wide_row = CD if dc == 0 else 8
            skip = (RD * which if dr == 0 else sum(before)) * wide_row
            parts.append(around[dr, dc][skip + i * wide_row : skip + (i + 1) * wide_row, :])
        return jnp.concatenate(parts, axis=0)

    for k in range(10):
        s1[pl.ds(EDGE + k * WD, WD), :] = field_row(0, k - 3) * row_mask(k - 3)
    for k in range(8):
        c0s[pl.ds(k * WD, WD), :] = field_row(1, k - 2)
    for k in range(6):
        k1s[pl.ds(k * WD, WD), :] = field_row(2, k - 1)
    for b in range(KS):
        hs1[b] = s1[pl.ds(EDGE + b - 1, 10 * WD), :].astype(BF)
    low = lax.broadcasted_iota(jnp.int32, (12, HC), 1) < CI
    ones = jnp.where(
        lax.broadcasted_iota(jnp.int32, (WD, HC), 1) == 3 * CI, 1.0, 0.0
    ).astype(F32)
    for t in range(STEPS):
        for k in range(3):
            fs[t, pl.ds(4 * k, 4), :] = fl[k, t].astype(F32)
        for g in range(10):
            vals = fs[t, pl.ds(0, 12), pl.ds(g * 128, 128)] * frame_mask[:12, g * 128 : (g + 1) * 128]
            for j in range(4):
                turned = vals if j == 0 else pltpu.roll(vals, 128 - 32 * j, 1)
                x32[t, pl.ds(EDGE + 4 + 4 * g + j, 12, stride=WD), :] = jnp.where(low, turned, 0.0)
        for row in range(12):
            at = EDGE + row * WD
            joined = (
                x32[t, pl.ds(at - 1, WD), :]
                + pltpu.roll(x32[t, pl.ds(at, WD), :], 32, 1)
                + pltpu.roll(x32[t, pl.ds(at + 1, WD), :], 64, 1)
                + ones
            )
            xb[t, pl.ds(row * WD, WD), :] = joined.astype(BF)

    bias = bias_in[...]

    def gates_of(hs, t, first, count):
        size_m = count * WD
        blocks = [
            hs[b, pl.ds(a * WD, size_m), :] for a in range(KS) for b in range(KS)
        ] + [xb[t, pl.ds((first + a) * WD, size_m), :] for a in range(KS)]
        lhs = jnp.concatenate(blocks, axis=1)
        ga[pl.ds(0, size_m), :] = jnp.dot(lhs, wp[...], preferred_element_type=F32)

    def sigmoid(v):
        return 0.5 * jnp.tanh(0.5 * v) + 0.5

    def activated(row):
        pre = ga[pl.ds(row * WD, WD), :] + bias
        return (
            sigmoid(pre[:, :HC]),
            sigmoid(pre[:, HC : 2 * HC]),
            jnp.tanh(pre[:, 2 * HC : 3 * HC]),
            sigmoid(pre[:, 3 * HC :]),
        )

    gates_of(hs1, 0, 1, 8)
    for k in range(8):
        row = k - 2
        gi, gf, gg, go = activated(k)
        now = gf * c0s[pl.ds(k * WD, WD), :] + gi * gg
        th = jnp.tanh(now)
        c1s[pl.ds(k * WD, WD), :] = now
        if 0 <= row < RD:
            at = pl.ds(row * WD, WD)
            for q, val in enumerate((gi, gf, gg, go, th)):
                sv[q, at, :] = val
        h = (go * th).astype(BF).astype(F32)
        s2[pl.ds(EDGE + k * WD, WD), :] = h * row_mask(row)
    for b in range(KS):
        hs2[b] = s2[pl.ds(EDGE + b - 1, 8 * WD), :].astype(BF)

    gates_of(hs2, 1, 2, 6)

    def pre_grads(s, dh, gi, gf, gg, go, th, before):
        return (
            s * gg * gi * (1.0 - gi),
            s * before * gf * (1.0 - gf),
            s * gi * (1.0 - gg * gg),
            dh * th * go * (1.0 - go),
        )

    for k in range(6):
        row = k - 1
        gi, gf, gg, go = activated(k)
        before = c1s[pl.ds((k + 1) * WD, WD), :]
        now = gf * before + gi * gg
        th = jnp.tanh(now)
        dh = k1s[pl.ds(k * WD, WD), :]
        s = dh * go * (1.0 - th * th)
        if 0 <= row < RD:
            hid_out[row] = (go * th)[8 : 8 + CD, :].astype(BF)
            dcs[pl.ds(row * WD, WD), :] = s * gf
        mask = row_mask(row)
        for q, pre in enumerate(pre_grads(s, dh, gi, gf, gg, go, th, before)):
            cols = pl.ds(q * HC, HC)
            dg2[pl.ds(k * WD, WD), cols] = (pre * mask).astype(BF)
            if 0 <= row < RD:
                dgo[pl.ds((RD + row) * WD, WD), cols] = (pre * own_mask).astype(BF)

    def adjoint(dg, count):
        size_m = count * WD
        zs[pl.ds(EDGE, size_m), :] = lax.dot_general(
            dg[pl.ds(0, size_m), :],
            wp[pl.ds(0, TAPS * HC), :],
            (((1,), (1,)), ((), ())),
            preferred_element_type=F32,
        )

    def gathered(k, count):
        total = None
        for tap in range(TAPS):
            a, b = divmod(tap, KS)
            row = k + 2 - a
            if not 0 <= row < count:
                continue
            term = zs[pl.ds(EDGE + row * WD - (b - 1), WD), pl.ds(tap * HC, HC)]
            total = term if total is None else total + term
        return total

    adjoint(dg2, 6)
    for row in range(RD):
        at = pl.ds(row * WD, WD)
        gi, gf, gg, go, th = (sv[q, at, :] for q in range(5))
        inner = gathered(row, 6)
        cot = kown[0, row].astype(F32)
        blank = jnp.zeros((8, HC), F32)
        dh = inner + jnp.concatenate([blank, cot, blank], axis=0)
        s = dcs[at, :] + dh * go * (1.0 - th * th)
        gc_out[row] = (s * gf)[8 : 8 + CD, :]
        before = c0s[pl.ds((row + 2) * WD, WD), :]
        for q, pre in enumerate(pre_grads(s, dh, gi, gf, gg, go, th, before)):
            dgo[at, pl.ds(q * HC, HC)] = (pre * own_mask).astype(BF)

    written = []

    def write(src, dst):
        copy = pltpu.make_async_copy(src, dst, out_sem.at[len(written)])
        copy.start()
        written.append(copy)

    write(hid_out, hid_hbm)
    write(gc_out, gc_hbm)

    count = [0]

    def copy_to(src, dst, who):
        i = count[0]
        count[0] += 1
        return pltpu.make_async_remote_copy(
            src_ref=src,
            dst_ref=dst,
            send_sem=st_send.at[i],
            recv_sem=st_recv.at[i],
            device_id=who,
            device_id_type=MESH,
        )

    sent = []
    mine_at = pl.multiple_of(core * HALF, HALF)
    other_at = pl.multiple_of((1 - core) * HALF, HALF)

    def weight_blocks(p):
        blocks = []
        for q in range(4 * p, 4 * p + 4):
            if q < TAPS:
                a, b = divmod(q, KS)
                one = hs1[b, pl.ds((2 + a) * WD, RD * WD), :]
                two = hs2[b, pl.ds((1 + a) * WD, RD * WD), :]
            else:
                a = q - TAPS
                one = xb[0, pl.ds((3 + a) * WD, RD * WD), :]
                two = xb[1, pl.ds((3 + a) * WD, RD * WD), :]
            blocks.append(jnp.concatenate([one, two], axis=0))
        return jnp.concatenate(blocks, axis=1)

    swaps = []
    dims = (((0,), (0,)), ((), ()))
    for p in range(PARTS):
        a0[p] = lax.dot_general(
            weight_blocks(p), dgo[:, pl.ds(other_at, HALF)], dims, preferred_element_type=F32
        ).astype(BF)
        copy = copy_to(a0.at[p], r0.at[p], sibling)
        copy.start()
        swaps.append(copy)
    for p in range(PARTS):
        o0[p] = lax.dot_general(
            weight_blocks(p), dgo[:, pl.ds(mine_at, HALF)], dims, preferred_element_type=F32
        )
    sent += swaps

    plans = [
        ("z", "y", "x", r1z, a2z, r2z, r3z),
        ("y", "z", "x", r1y, a2y, r2y, r3y),
        ("x", "z", "y", r1x, a2x, r2x, r3x),
    ]
    state = []
    for p, (ax1, ax2, ax3, r1, a2, r2, r3) in enumerate(plans):
        n1, n2, n3 = size[ax1], size[ax2], size[ax3]
        rows1 = PART // n1
        rows2 = rows1 // n2
        if rows2 >= 16:
            unit = (rows2, HALF)
        else:
            unit = (16, HALF * rows2 // 16)
        across = HALF // unit[1]

        def unit_at(u, unit=unit, across=across):
            return (
                pl.multiple_of((u // across) * unit[0], 16),
                pl.multiple_of(lax.rem(u, across) * unit[1], 128),
            )

        state.append((n1, n2, n3, rows1, unit, unit_at))

    stage1 = []
    for p, (ax1, ax2, ax3, r1, a2, r2, r3) in enumerate(plans):
        n1, n2, n3, rows1, unit, unit_at = state[p]
        swaps[p].wait_recv()
        a1[p] = (o0[p] + r0[p].astype(F32)).astype(BF)
        copies = []
        for d in range(1, n1):
            to = lax.rem(mine[ax1] + d, n1)
            copy = copy_to(
                a1.at[p, pl.ds(pl.multiple_of(to * rows1, 16), rows1), :],
                r1.at[d - 1],
                peer(ax1, d),
            )
            copy.start()
            copies.append(copy)
        stage1.append(copies)
        sent += copies

    adjoint(dgo, RD)
    zs[pl.ds(EDGE + RD * WD, EDGE), :] = wide
    for k in range(RD + 2):
        cb[k] = gathered(k - 2, RD)
    stage2 = []
    for p, (ax1, ax2, ax3, r1, a2, r2, r3) in enumerate(plans):
        n1, n2, n3, rows1, unit, unit_at = state[p]
        for copy in stage1[p]:
            copy.wait_recv()
        at = pl.ds(pl.multiple_of(mine[ax1] * rows1, 16), rows1)
        total = a1[p, at, :].astype(F32)
        for d in range(1, n1):
            total = total + r1[d - 1].astype(F32)
        a2[...] = total.astype(BF)
        copies = []
        for d in range(1, n2):
            ur, uc = unit_at(lax.rem(mine[ax2] + d, n2))
            copy = copy_to(
                a2.at[pl.ds(ur, unit[0]), pl.ds(uc, unit[1])], r2.at[d - 1], peer(ax2, d)
            )
            copy.start()
            copies.append(copy)
        stage2.append(copies)
        sent += copies

    late = []
    for i, (dr, dc) in enumerate(SIDES):
        rows_at = pl.ds(0, 1) if dr < 0 else (pl.ds(RD + 1, 1) if dr > 0 else pl.ds(1, RD))
        cols_at = pl.ds(0, 8) if dc < 0 else (pl.ds(8 + CD, 8) if dc > 0 else pl.ds(8, CD))
        copy = pltpu.make_async_remote_copy(
            src_ref=cb.at[rows_at, cols_at, :],
            dst_ref=slot_of(dr, dc, ud_c, lr_c, co_c),
            send_sem=late_send.at[i],
            recv_sem=late_recv.at[i],
            device_id=neighbour(dr, dc),
            device_id_type=MESH,
        )
        copy.start()
        late.append(copy)
    sent += late

    stage3 = []
    for p, (ax1, ax2, ax3, r1, a2, r2, r3) in enumerate(plans):
        n1, n2, n3, rows1, unit, unit_at = state[p]
        for copy in stage2[p]:
            copy.wait_recv()
        ur, uc = unit_at(mine[ax2])
        total = a2[pl.ds(ur, unit[0]), pl.ds(uc, unit[1])].astype(F32)
        for d in range(1, n2):
            total = total + r2[d - 1].astype(F32)
        r3[mine[ax3]] = total.astype(BF)
        copies = []
        for d in range(1, n3):
            copy = copy_to(r3.at[mine[ax3]], r3.at[mine[ax3]], peer(ax3, d))
            copy.start()
            copies.append(copy)
        stage3.append(copies)
        sent += copies

    stage4 = []
    for p, (ax1, ax2, ax3, r1, a2, r2, r3) in enumerate(plans):
        n1, n2, n3, rows1, unit, unit_at = state[p]
        for copy in stage3[p]:
            copy.wait_recv()
        total = r3[0].astype(F32)
        for d in range(1, n3):
            total = total + r3[d].astype(F32)
        ur, uc = unit_at(mine[ax2])
        slot = gs.at[
            pl.ds(pl.multiple_of(p * PART + mine[ax1] * rows1 + ur, 16), unit[0]),
            pl.ds(pl.multiple_of(mine_at + uc, 128), unit[1]),
        ]
        slot[...] = total.astype(BF)
        copies = []
        for d in range(1, n2):
            copy = copy_to(slot, slot, peer(ax2, d))
            copy.start()
            copies.append(copy)
        stage4.append(copies)
        sent += copies

    stage5 = []
    for p, (ax1, ax2, ax3, r1, a2, r2, r3) in enumerate(plans):
        n1, n2, n3, rows1, unit, unit_at = state[p]
        for copy in stage4[p]:
            copy.wait_recv()
        slot = gs.at[
            pl.ds(pl.multiple_of(p * PART + mine[ax1] * rows1, 16), rows1),
            pl.ds(mine_at, HALF),
        ]
        copies = []
        for d in range(1, n1):
            copy = copy_to(slot, slot, peer(ax1, d))
            copy.start()
            copies.append(copy)
        stage5.append(copies)
        sent += copies

    for copy in late:
        copy.wait_recv()
    for row in range(RD):
        gh_out[row] = cb[row + 1, pl.ds(8, CD), :]
    for dr, dc in SIDES:
        inside = (r - dr >= 0) & (r - dr < n_rows) & (c - dc >= 0) & (c - dc < n_cols)
        keep = jnp.where(inside, 1.0, 0.0).astype(F32)
        rows_at = pl.ds(RD - 1, 1) if dr < 0 else (pl.ds(0, 1) if dr > 0 else pl.ds(0, RD))
        cols_at = pl.ds(CD - 8, 8) if dc < 0 else (pl.ds(0, 8) if dc > 0 else pl.ds(0, CD))
        terms = slot_of(dr, dc, ud_c, lr_c, co_c)[...] * keep
        gh_out[rows_at, cols_at, :] = gh_out[rows_at, cols_at, :] + terms

    write(gh_out, gh_hbm)

    stage6 = []
    for p in range(PARTS):
        for copy in stage5[p]:
            copy.wait_recv()
        rows_at = pl.ds(p * PART, PART)
        slot = gs.at[rows_at, pl.ds(mine_at, HALF)]
        copy = copy_to(slot, slot, sibling)
        copy.start()
        stage6.append(copy)
        write(slot, total_hbm.at[rows_at, pl.ds(mine_at, HALF)])
    sent += stage6
    for p, copy in enumerate(stage6):
        copy.wait_recv()
        rows_at = pl.ds(p * PART, PART)
        write(
            gs.at[rows_at, pl.ds(other_at, HALF)], total_hbm.at[rows_at, pl.ds(other_at, HALF)]
        )

    for copy in written:
        copy.wait()
    for copy in halos:
        copy.wait_send()
    for copy in sent:
        copy.wait_send()


def units(n1, n2):
    rows1 = PART // n1
    rows2 = rows1 // n2
    return (rows2, HALF) if rows2 >= 16 else (16, HALF * rows2 // 16)


def shards(frames, hidden_start, cell_start, kernel, gate_bias, cotangent):
    n_rows = lax.axis_size("rows")
    n_cols = lax.axis_size("cols")
    ny = (n_rows // NX) * NYL
    uz = units(NZ, ny)
    uy = units(ny, NZ)
    ux = units(NX, NZ)
    vmem = pltpu.VMEM
    scratch = [
        vmem((RD, CD, HC), BF),
        vmem((RD, CD, HC), F32),
        vmem((RD, CD, HC), F32),
        vmem((1, GATES), F32),
        vmem((RD, CD, HC), BF),
        vmem((3, STEPS, RD, 1280), BF),
        vmem((RD, CD, HC), F32),
        vmem((STEPS, RD, CD, HC), BF),
        vmem((ROWS_W, GATES), BF),
        vmem((2, 6 * CD, HC), BF),
        vmem((2, 3 * RD * 8, HC), BF),
        vmem((4, 6 * 8, HC), BF),
        vmem((2, 6 * CD, HC), BF),
        vmem((2, 3 * RD * 8, HC), BF),
        vmem((4, 6 * 8, HC), BF),
        vmem((STEPS, 16, 1280), F32),
        vmem((STEPS, 12 * WD + 2 * EDGE, HC), F32),
        vmem((STEPS, 12 * WD, HC), BF),
        vmem((10 * WD + 2 * EDGE, HC), F32),
        vmem((8 * WD + 2 * EDGE, HC), F32),
        vmem((KS, 10 * WD, HC), BF),
        vmem((KS, 8 * WD, HC), BF),
        vmem((8 * WD, GATES), F32),
        vmem((5, RD * WD, HC), F32),
        vmem((8 * WD, HC), F32),
        vmem((8 * WD, HC), F32),
        vmem((6 * WD, HC), F32),
        vmem((RD * WD, HC), F32),
        vmem((6 * WD, GATES), BF),
        vmem((2 * RD * WD, GATES), BF),
        vmem((6 * WD + 2 * EDGE, TAPS * HC), F32),
        vmem((RD + 2, WD, HC), F32),
        vmem((2, 1, CD, HC), F32),
        vmem((2, RD, 8, HC), F32),
        vmem((4, 1, 8, HC), F32),
        vmem((PARTS, PART, HALF), BF),
        vmem((PARTS, PART, HALF), F32),
        vmem((PARTS, PART, HALF), BF),
        vmem((PARTS, PART, HALF), BF),
        vmem((NZ - 1, PART // NZ, HALF), BF),
        vmem((ny - 1, PART // ny, HALF), BF),
        vmem((NX - 1, PART // NX, HALF), BF),
        vmem((PART // NZ, HALF), BF),
        vmem((PART // ny, HALF), BF),
        vmem((PART // NX, HALF), BF),
        vmem((ny - 1,) + uz, BF),
        vmem((NZ - 1,) + uy, BF),
        vmem((NZ - 1,) + ux, BF),
        vmem((NX,) + uz, BF),
        vmem((NX,) + uy, BF),
        vmem((ny,) + ux, BF),
        vmem((ROWS_W, GATES), BF),
        pltpu.SemaphoreType.DMA((8, 2)),
        pltpu.SemaphoreType.DMA((8, 2)),
        pltpu.SemaphoreType.DMA((8,)),
        pltpu.SemaphoreType.DMA((8,)),
        pltpu.SemaphoreType.DMA((5 + 2 * TAPS,)),
        pltpu.SemaphoreType.DMA((3 + 2 * PARTS,)),
        pltpu.SemaphoreType.DMA((stages(n_rows),)),
        pltpu.SemaphoreType.DMA((stages(n_rows),)),
    ]
    in_hbm = pl.BlockSpec(memory_space=pltpu.HBM)
    hidden, grad_hidden, grad_cell, total = pl.pallas_call(
        functools.partial(body, n_rows, n_cols),
        out_shape=(
            jax.ShapeDtypeStruct((RD, CD, HC), BF),
            jax.ShapeDtypeStruct((RD, CD, HC), F32),
            jax.ShapeDtypeStruct((RD, CD, HC), F32),
            jax.ShapeDtypeStruct((ROWS_W, GATES), BF),
        ),
        in_specs=[in_hbm] * 6,
        out_specs=(in_hbm,) * 4,
        scratch_shapes=scratch,
        compiler_params=pltpu.CompilerParams(
            collective_id=0, has_side_effects=True, vmem_limit_bytes=63 * 1024 * 1024
        ),
    )(frames, hidden_start, cell_start, kernel, gate_bias.reshape(1, GATES), cotangent)
    scale = 1.0 / math.sqrt(STEPS * n_rows * RD * n_cols * CD)
    outs = pl.pallas_call(
        functools.partial(finish, scale),
        out_shape=(
            jax.ShapeDtypeStruct((RD, CD, HC), BF),
            jax.ShapeDtypeStruct((RD, CD, HC), F32),
            jax.ShapeDtypeStruct((RD, CD, HC), F32),
            jax.ShapeDtypeStruct((KIN, GATES), F32),
            jax.ShapeDtypeStruct((1, GATES), F32),
        ),
        in_specs=[in_hbm] * 4,
        out_specs=(in_hbm,) * 5,
        scratch_shapes=[
            vmem((ROWS_W, GATES), BF),
            vmem((KIN, GATES), F32),
            vmem((1, GATES), F32),
            pltpu.SemaphoreType.DMA((1 + KS,)),
            pltpu.SemaphoreType.DMA((TAPS + 4,)),
        ],
        compiler_params=pltpu.CompilerParams(vmem_limit_bytes=63 * 1024 * 1024),
    )(hidden, grad_hidden, grad_cell, total)
    return outs[0], outs[1], outs[2], outs[3], outs[4].reshape(GATES)


def finish(
    scale, hid, gh, gc, total_hbm, hid_out, gh_out, gc_out, kg_out, bg_out, total, kg, bg, in_sem, sem
):
    copies = []

    def put(src, dst):
        copy = pltpu.make_async_copy(src, dst, sem.at[len(copies)])
        copy.start()
        copies.append(copy)

    fetched = []
    step = KS * HC
    for i in range(1 + KS):
        at = pl.ds(TAPS * HC if i == 0 else (i - 1) * step, step)
        copy = pltpu.make_async_copy(total_hbm.at[at, :], total.at[at, :], in_sem.at[i])
        copy.start()
        fetched.append(copy)
    put(hid, hid_out)
    put(gh, gh_out)
    put(gc, gc_out)
    fetched[0].wait()
    for tap in range(TAPS):
        a, b = divmod(tap, KS)
        if b == 0:
            fetched[1 + a].wait()
        first = TAPS * HC + a * 128 + b * CI
        at = tap * 160
        kg[pl.ds(at, CI), :] = total[pl.ds(first, CI), :].astype(F32) * scale
        kg[pl.ds(at + CI, HC), :] = total[pl.ds(tap * HC, HC), :].astype(F32) * scale
        put(kg.at[pl.ds(at, 160), :], kg_out.at[pl.ds(at, 160), :])
    bg[...] = total[pl.ds(BIAS_ROW, 16), :].astype(F32)[:1, :] * scale
    put(bg, bg_out)
    for copy in copies:
        copy.wait()


def stages(n_rows):
    ny = (n_rows // NX) * NYL
    one = (NZ - 1) + (ny - 1) + (NX - 1)
    two = (ny - 1) + (NZ - 1) + (NZ - 1)
    three = (NX - 1) + (NX - 1) + (ny - 1)
    return 2 * PARTS + 2 * one + 2 * two + three


def solution(mesh):
    placed = (
        P(None, "rows", "cols"),
        P("rows", "cols", None),
        P("rows", "cols", None),
        P(),
        P(),
        P(None, "rows", "cols", None),
    )
    return jax.shard_map(
        shards,
        mesh=mesh,
        in_specs=placed,
        out_specs=(
            P("rows", "cols", None),
            P("rows", "cols", None),
            P("rows", "cols", None),
            P(),
            P(),
        ),
        check_vma=False,
    )
```

```python
import functools
import math

import jax
import jax.numpy as jnp
from jax import lax
from jax.experimental import pallas as pl
from jax.experimental.pallas import tpu as pltpu
from jax.sharding import PartitionSpec as P

HC = 128
CI = 32
KS = 3
STEPS = 2
GATES = 512
KIN = 1440
TAPS = 9

NX = 4
NYL = 2
NZ = 8

BF = jnp.bfloat16
F32 = jnp.float32
MESH = pl.DeviceIdType.MESH

RD = 4
CD = 32
WD = 48
EDGE = 8
ROWS_W = 1536
PARTS = 3
HALF = GATES // 2
FRAME_ROWS = ((0, 112), (112, 96), (208, 96))
AREAS = ((0, 384), (768, 384), (1536, 704))
LINES = 2944
BIAS_ROW = 384 + 3 * CI
SIDES = [(dr, dc) for dr in (-1, 0, 1) for dc in (-1, 0, 1) if (dr, dc) != (0, 0)]


def span(step, halo, size):
    if step == 0:
        return (0, size), (halo, size)
    if step > 0:
        return (size - halo, halo), (0, halo)
    return (0, halo), (halo + size, halo)


def place(x, y, z, core):
    return ((y // NYL) * NX + x, ((y % NYL) * NZ + z) * 2 + core)


def body(
    n_rows,
    n_cols,
    frames_ref,
    hidden_ref,
    cell_ref,
    kernel_ref,
    bias_ref,
    cot_ref,
    hid_hbm,
    gh_hbm,
    gc_hbm,
    total_hbm,
    hid_out,
    gh_out,
    gc_out,
    bias_in,
    hown,
    fl,
    cown,
    kown,
    wp,
    ud,
    st,
    co,
    ud_in,
    st_in,
    co_in,
    fs,
    x32,
    xb,
    s1,
    s2,
    hs1,
    hs2,
    ga,
    sv,
    c0s,
    c1s,
    k1s,
    dcs,
    dg2,
    dgo,
    zs,
    cb,
    ud_c,
    lr_c,
    co_c,
    a0,
    o0,
    r0,
    a1,
    r1z,
    r1y,
    r1x,
    a2z,
    a2y,
    a2x,
    r2z,
    r2y,
    r2x,
    r3z,
    r3y,
    r3x,
    g4z,
    g4y,
    g4x,
    gs,
    halo_send,
    halo_recv,
    late_send,
    late_recv,
    loc_sem,
    out_sem,
    st_send,
    st_recv,
):
    r = lax.axis_index("rows")
    c = lax.axis_index("cols")
    ny = (n_rows // NX) * NYL
    x = lax.rem(r, NX)
    core = lax.rem(c, 2)
    z = lax.rem(c // 2, NZ)
    y = (r // NX) * NYL + c // (2 * NZ)
    size = {"x": NX, "y": ny, "z": NZ}
    mine = {"x": x, "y": y, "z": z}

    def peer(axis, d):
        at = dict(mine)
        at[axis] = lax.rem(mine[axis] + d, size[axis])
        return place(at["x"], at["y"], at["z"], core)

    sibling = place(x, y, z, 1 - core)

    def neighbour(dr, dc):
        return (lax.rem(r + dr + n_rows, n_rows), lax.rem(c + dc + n_cols, n_cols))

    barrier = pltpu.get_barrier_semaphore()
    greet = [neighbour(dr, dc) for dr, dc in SIDES] + [sibling]
    for axis in ("x", "y", "z"):
        greet += [peer(axis, d) for d in range(1, size[axis])]
    for who in greet:
        pl.semaphore_signal(barrier, inc=1, device_id=who, device_id_type=MESH)

    local = []

    def fetch(src, dst):
        copy = pltpu.make_async_copy(src, dst, loc_sem.at[len(local)])
        copy.start()
        local.append(copy)

    fetch(hidden_ref, hown)
    fetch(cell_ref, cown)
    fetch(cot_ref, kown)
    fetch(frames_ref, fl.at[1, :, :, pl.ds(128, CD * CI)])
    fetch(bias_ref, bias_in)
    for tap in range(TAPS):
        a, b = divmod(tap, KS)
        fetch(kernel_ref.at[pl.ds(tap * 160 + CI, HC), :], wp.at[pl.ds(tap * HC, HC), :])
        fetch(
            kernel_ref.at[pl.ds(tap * 160, CI), :],
            wp.at[pl.ds(TAPS * HC + a * 128 + b * CI, CI), :],
        )
    for copy in local[:3]:
        copy.wait()
    fields = (
        ([hown[i] for i in range(RD)], 3),
        ([cown[i] for i in range(RD)], 2),
        ([kown[1, i] for i in range(RD)], 1),
    )

    def edge_rows(step, depth):
        if step == 0:
            return range(RD)
        return range(depth) if step < 0 else range(RD - depth, RD)

    def outgoing(dr, dc):
        pieces = []
        for rows, depth in fields:
            for i in edge_rows(dr, depth):
                piece = rows[i].astype(F32)
                if dc != 0:
                    piece = piece[:8, :] if dc < 0 else piece[CD - 8 :, :]
                pieces.append(piece)
        return jnp.concatenate(pieces, axis=0).astype(BF)

    def slot_of(dr, dc, rows_buf, sides_buf, corners_buf):
        if dc == 0:
            return rows_buf.at[(dr + 1) // 2]
        if dr == 0:
            return sides_buf.at[(dc + 1) // 2]
        return corners_buf.at[(dr + 1) + (dc + 1) // 2]

    for dr, dc in SIDES:
        slot_of(dr, dc, ud, st, co)[...] = outgoing(dr, dc)
    pl.semaphore_wait(barrier, len(greet))

    halos = []
    for i, (dr, dc) in enumerate(SIDES):
        who = neighbour(dr, dc)
        (ls, ln), (lt, _) = span(dc, 128, CD * CI)
        for kind, (src, dst) in enumerate(
            (
                (slot_of(dr, dc, ud, st, co), slot_of(dr, dc, ud_in, st_in, co_in)),
                (frames_ref.at[:, :, pl.ds(ls, ln)], fl.at[1 - dr, :, :, pl.ds(lt, ln)]),
            )
        ):
            copy = pltpu.make_async_remote_copy(
                src_ref=src,
                dst_ref=dst,
                send_sem=halo_send.at[i, kind],
                recv_sem=halo_recv.at[i, kind],
                device_id=who,
                device_id_type=MESH,
            )
            copy.start()
            halos.append(copy)

    for a in range(KS):
        wp[pl.ds(TAPS * HC + a * 128 + 96, 32), :] = jnp.zeros((32, GATES), BF)
    x32[...] = jnp.zeros_like(x32)
    edge = jnp.zeros((EDGE, HC), F32)
    s1[pl.ds(0, EDGE), :] = edge
    s1[pl.ds(EDGE + 10 * WD, EDGE), :] = edge
    s2[pl.ds(0, EDGE), :] = edge
    s2[pl.ds(EDGE + 8 * WD, EDGE), :] = edge
    wide = jnp.zeros((EDGE, TAPS * HC), F32)
    zs[pl.ds(0, EDGE), :] = wide
    zs[pl.ds(EDGE + 6 * WD, EDGE), :] = wide
    fs[...] = jnp.zeros_like(fs)
    for spare in (a2z, a2y, a2x):
        spare[...] = jnp.zeros_like(spare)

    at_col = lax.broadcasted_iota(jnp.int32, (WD, HC), 0) - 8
    in_raster = (at_col + c * CD >= 0) & (at_col + c * CD < n_cols * CD)
    col_mask = jnp.where(in_raster, 1.0, 0.0).astype(F32)
    own_mask = jnp.where((at_col >= 0) & (at_col < CD), 1.0, 0.0).astype(F32)

    def row_mask(row):
        there = r * RD + row
        inside = (there >= 0) & (there < n_rows * RD)
        return col_mask * jnp.where(inside, 1.0, 0.0).astype(F32)

    lane = lax.broadcasted_iota(jnp.int32, (16, 1280), 1)
    line = lax.broadcasted_iota(jnp.int32, (16, 1280), 0)
    there_col = lane // CI - 4 + c * CD
    there_row = line - 4 + r * RD
    frame_mask = jnp.where(
        (there_col >= 0)
        & (there_col < n_cols * CD)
        & (there_row >= 0)
        & (there_row < n_rows * RD),
        1.0,
        0.0,
    ).astype(F32)

    for copy in local[3:]:
        copy.wait()
    for copy in halos:
        copy.wait_recv()

    def incoming(dr, dc):
        return slot_of(-dr, -dc, ud_in, st_in, co_in)[...].astype(F32)

    around = {side: incoming(*side) for side in SIDES}

    def field_row(which, row):
        rows, depth = fields[which]
        before = [d for _, d in fields[:which]]
        dr = -1 if row < 0 else (1 if row >= RD else 0)
        i = row + depth if row < 0 else (row - RD if row >= RD else row)
        parts = []
        for dc in (-1, 0, 1):
            if (dr, dc) == (0, 0):
                parts.append(rows[row].astype(F32))
                continue
            wide_row = CD if dc == 0 else 8
            skip = (RD * which if dr == 0 else sum(before)) * wide_row
            parts.append(around[dr, dc][skip + i * wide_row : skip + (i + 1) * wide_row, :])
        return jnp.concatenate(parts, axis=0)

    for k in range(10):
        s1[pl.ds(EDGE + k * WD, WD), :] = field_row(0, k - 3) * row_mask(k - 3)
    for k in range(8):
        c0s[pl.ds(k * WD, WD), :] = field_row(1, k - 2)
    for k in range(6):
        k1s[pl.ds(k * WD, WD), :] = field_row(2, k - 1)
    for b in range(KS):
        hs1[b] = s1[pl.ds(EDGE + b - 1, 10 * WD), :].astype(BF)
    low = lax.broadcasted_iota(jnp.int32, (12, HC), 1) < CI
    ones = jnp.where(
        lax.broadcasted_iota(jnp.int32, (WD, HC), 1) == 3 * CI, 1.0, 0.0
    ).astype(F32)
    for t in range(STEPS):
        for k in range(3):
            fs[t, pl.ds(4 * k, 4), :] = fl[k, t].astype(F32)
        for g in range(10):
            vals = fs[t, pl.ds(0, 12), pl.ds(g * 128, 128)] * frame_mask[:12, g * 128 : (g + 1) * 128]
            for j in range(4):
                turned = vals if j == 0 else pltpu.roll(vals, 128 - 32 * j, 1)
                x32[t, pl.ds(EDGE + 4 + 4 * g + j, 12, stride=WD), :] = jnp.where(low, turned, 0.0)
        for row in range(12):
            at = EDGE + row * WD
            joined = (
                x32[t, pl.ds(at - 1, WD), :]
                + pltpu.roll(x32[t, pl.ds(at, WD), :], 32, 1)
                + pltpu.roll(x32[t, pl.ds(at + 1, WD), :], 64, 1)
                + ones
            )
            xb[t, pl.ds(row * WD, WD), :] = joined.astype(BF)

    bias = bias_in[...]

    def gates_of(hs, t, first, count):
        size_m = count * WD
        blocks = [
            hs[b, pl.ds(a * WD, size_m), :] for a in range(KS) for b in range(KS)
        ] + [xb[t, pl.ds((first + a) * WD, size_m), :] for a in range(KS)]
        lhs = jnp.concatenate(blocks, axis=1)
        ga[pl.ds(0, size_m), :] = jnp.dot(lhs, wp[...], preferred_element_type=F32)

    def sigmoid(v):
        return 0.5 * jnp.tanh(0.5 * v) + 0.5

    def activated(row):
        pre = ga[pl.ds(row * WD, WD), :] + bias
        return (
            sigmoid(pre[:, :HC]),
            sigmoid(pre[:, HC : 2 * HC]),
            jnp.tanh(pre[:, 2 * HC : 3 * HC]),
            sigmoid(pre[:, 3 * HC :]),
        )

    gates_of(hs1, 0, 1, 8)
    for k in range(8):
        row = k - 2
        gi, gf, gg, go = activated(k)
        now = gf * c0s[pl.ds(k * WD, WD), :] + gi * gg
        th = jnp.tanh(now)
        c1s[pl.ds(k * WD, WD), :] = now
        if 0 <= row < RD:
            at = pl.ds(row * WD, WD)
            for q, val in enumerate((gi, gf, gg, go, th)):
                sv[q, at, :] = val
        h = (go * th).astype(BF).astype(F32)
        s2[pl.ds(EDGE + k * WD, WD), :] = h * row_mask(row)
    for b in range(KS):
        hs2[b] = s2[pl.ds(EDGE + b - 1, 8 * WD), :].astype(BF)

    gates_of(hs2, 1, 2, 6)

    def pre_grads(s, dh, gi, gf, gg, go, th, before):
        return (
            s * gg * gi * (1.0 - gi),
            s * before * gf * (1.0 - gf),
            s * gi * (1.0 - gg * gg),
            dh * th * go * (1.0 - go),
        )

    for k in range(6):
        row = k - 1
        gi, gf, gg, go = activated(k)
        before = c1s[pl.ds((k + 1) * WD, WD), :]
        now = gf * before + gi * gg
        th = jnp.tanh(now)
        dh = k1s[pl.ds(k * WD, WD), :]
        s = dh * go * (1.0 - th * th)
        if 0 <= row < RD:
            hid_out[row] = (go * th)[8 : 8 + CD, :].astype(BF)
            dcs[pl.ds(row * WD, WD), :] = s * gf
        mask = row_mask(row)
        for q, pre in enumerate(pre_grads(s, dh, gi, gf, gg, go, th, before)):
            cols = pl.ds(q * HC, HC)
            dg2[pl.ds(k * WD, WD), cols] = (pre * mask).astype(BF)
            if 0 <= row < RD:
                dgo[pl.ds((RD + row) * WD, WD), cols] = (pre * own_mask).astype(BF)

    def adjoint(dg, count):
        size_m = count * WD
        zs[pl.ds(EDGE, size_m), :] = lax.dot_general(
            dg[pl.ds(0, size_m), :],
            wp[pl.ds(0, TAPS * HC), :],
            (((1,), (1,)), ((), ())),
            preferred_element_type=F32,
        )

    def gathered(k, count):
        total = None
        for tap in range(TAPS):
            a, b = divmod(tap, KS)
            row = k + 2 - a
            if not 0 <= row < count:
                continue
            term = zs[pl.ds(EDGE + row * WD - (b - 1), WD), pl.ds(tap * HC, HC)]
            total = term if total is None else total + term
        return total

    adjoint(dg2, 6)
    for row in range(RD):
        at = pl.ds(row * WD, WD)
        gi, gf, gg, go, th = (sv[q, at, :] for q in range(5))
        inner = gathered(row, 6)
        cot = kown[0, row].astype(F32)
        blank = jnp.zeros((8, HC), F32)
        dh = inner + jnp.concatenate([blank, cot, blank], axis=0)
        s = dcs[at, :] + dh * go * (1.0 - th * th)
        gc_out[row] = (s * gf)[8 : 8 + CD, :]
        before = c0s[pl.ds((row + 2) * WD, WD), :]
        for q, pre in enumerate(pre_grads(s, dh, gi, gf, gg, go, th, before)):
            dgo[at, pl.ds(q * HC, HC)] = (pre * own_mask).astype(BF)

    written = []

    def write(src, dst):
        copy = pltpu.make_async_copy(src, dst, out_sem.at[len(written)])
        copy.start()
        written.append(copy)

    write(hid_out, hid_hbm)
    write(gc_out, gc_hbm)

    count = [0]

    def copy_to(src, dst, who):
        i = count[0]
        count[0] += 1
        return pltpu.make_async_remote_copy(
            src_ref=src,
            dst_ref=dst,
            send_sem=st_send.at[i],
            recv_sem=st_recv.at[i],
            device_id=who,
            device_id_type=MESH,
        )

    sent = []
    mine_at = pl.multiple_of(core * HALF, HALF)
    other_at = pl.multiple_of((1 - core) * HALF, HALF)

    def weight_blocks(p):
        blocks = []
        for q in range(KS * p, KS * p + (KS if p < 2 else 2 * KS)):
            if q < TAPS:
                a, b = divmod(q, KS)
                one = hs1[b, pl.ds((2 + a) * WD, RD * WD), :]
                two = hs2[b, pl.ds((1 + a) * WD, RD * WD), :]
            else:
                a = q - TAPS
                one = xb[0, pl.ds((3 + a) * WD, RD * WD), :]
                two = xb[1, pl.ds((3 + a) * WD, RD * WD), :]
            blocks.append(jnp.concatenate([one, two], axis=0))
        return jnp.concatenate(blocks, axis=1)

    def weight_grad(p, cols_at, out):
        val = lax.dot_general(
            weight_blocks(p),
            dgo[:, pl.ds(cols_at, HALF)],
            (((0,), (0,)), ((), ())),
            preferred_element_type=F32,
        ).astype(out.dtype)
        base, lines = AREAS[p]
        for panel in range(2):
            cut = val[:, panel * 128 : (panel + 1) * 128]
            at = base + panel * lines
            out[pl.ds(at, KS * HC), :] = cut[: KS * HC, :]
            if p == 2:
                for a, (first, size_a) in enumerate(FRAME_ROWS):
                    start = (KS + a) * HC
                    out[pl.ds(at + KS * HC + first, size_a), :] = cut[start : start + size_a, :]
                out[pl.ds(at + lines - 16, 16), :] = jnp.zeros((16, 128), out.dtype)

    swaps = []
    for p, (base, lines) in enumerate(AREAS):
        weight_grad(p, other_at, a0)
        area = pl.ds(base, 2 * lines)
        copy = copy_to(a0.at[area, :], r0.at[area, :], sibling)
        copy.start()
        swaps.append(copy)
    for p in range(PARTS):
        weight_grad(p, mine_at, o0)
    sent += swaps

    plans = [
        ("z", "y", "x", r1z, a2z, r2z, r3z, g4z),
        ("y", "z", "x", r1y, a2y, r2y, r3y, g4y),
        ("x", "z", "y", r1x, a2x, r2x, r3x, g4x),
    ]

    stage1 = []
    for p, (ax1, ax2, ax3, r1, a2, r2, r3, g4) in enumerate(plans):
        base, lines = AREAS[p]
        n1, chunk = size[ax1], r1.shape[1]
        swaps[p].wait_recv()
        area = pl.ds(base, 2 * lines)
        a1[area, :] = (o0[area, :] + r0[area, :].astype(F32)).astype(BF)
        copies = []
        for d in range(1, n1):
            to = pl.multiple_of(base + lax.rem(mine[ax1] + d, n1) * chunk, 16)
            copy = copy_to(a1.at[pl.ds(to, chunk), :], r1.at[d - 1], peer(ax1, d))
            copy.start()
            copies.append(copy)
        stage1.append(copies)
        sent += copies

    adjoint(dgo, RD)
    zs[pl.ds(EDGE + RD * WD, EDGE), :] = wide
    for k in range(RD + 2):
        cb[k] = gathered(k - 2, RD)
    stage2 = []
    for p, (ax1, ax2, ax3, r1, a2, r2, r3, g4) in enumerate(plans):
        base, lines = AREAS[p]
        n1, chunk = size[ax1], r1.shape[1]
        n2, unit = size[ax2], r2.shape[1]
        for copy in stage1[p]:
            copy.wait_recv()
        at = pl.multiple_of(base + mine[ax1] * chunk, 16)
        total = a1[pl.ds(at, chunk), :].astype(F32)
        for d in range(1, n1):
            total = total + r1[d - 1].astype(F32)
        a2[pl.ds(0, chunk), :] = total.astype(BF)
        copies = []
        for d in range(1, n2):
            to = pl.multiple_of(lax.rem(mine[ax2] + d, n2) * unit, 16)
            copy = copy_to(a2.at[pl.ds(to, unit), :], r2.at[d - 1], peer(ax2, d))
            copy.start()
            copies.append(copy)
        stage2.append(copies)
        sent += copies

    late = []
    for i, (dr, dc) in enumerate(SIDES):
        rows_at = pl.ds(0, 1) if dr < 0 else (pl.ds(RD + 1, 1) if dr > 0 else pl.ds(1, RD))
        cols_at = pl.ds(0, 8) if dc < 0 else (pl.ds(8 + CD, 8) if dc > 0 else pl.ds(8, CD))
        copy = pltpu.make_async_remote_copy(
            src_ref=cb.at[rows_at, cols_at, :],
            dst_ref=slot_of(dr, dc, ud_c, lr_c, co_c),
            send_sem=late_send.at[i],
            recv_sem=late_recv.at[i],
            device_id=neighbour(dr, dc),
            device_id_type=MESH,
        )
        copy.start()
        late.append(copy)
    sent += late

    stage3 = []
    for p, (ax1, ax2, ax3, r1, a2, r2, r3, g4) in enumerate(plans):
        n2, n3, unit = size[ax2], size[ax3], r2.shape[1]
        for copy in stage2[p]:
            copy.wait_recv()
        total = a2[pl.ds(pl.multiple_of(mine[ax2] * unit, 16), unit), :].astype(F32)
        for d in range(1, n2):
            total = total + r2[d - 1].astype(F32)
        r3[mine[ax3]] = total.astype(BF)
        copies = []
        for d in range(1, n3):
            copy = copy_to(r3.at[mine[ax3]], r3.at[mine[ax3]], peer(ax3, d))
            copy.start()
            copies.append(copy)
        stage3.append(copies)
        sent += copies

    stage4 = []
    for p, (ax1, ax2, ax3, r1, a2, r2, r3, g4) in enumerate(plans):
        n2, n3, unit = size[ax2], size[ax3], r2.shape[1]
        for copy in stage3[p]:
            copy.wait_recv()
        total = r3[0].astype(F32)
        for d in range(1, n3):
            total = total + r3[d].astype(F32)
        slot = g4.at[pl.ds(pl.multiple_of(mine[ax2] * unit, 16), unit), :]
        slot[...] = total.astype(BF)
        copies = []
        for d in range(1, n2):
            copy = copy_to(slot, slot, peer(ax2, d))
            copy.start()
            copies.append(copy)
        stage4.append(copies)
        sent += copies

    stage5 = []
    for p, (ax1, ax2, ax3, r1, a2, r2, r3, g4) in enumerate(plans):
        base, lines = AREAS[p]
        n1, chunk = size[ax1], r1.shape[1]
        for copy in stage4[p]:
            copy.wait_recv()
        at = pl.ds(pl.multiple_of(base + mine[ax1] * chunk, 16), chunk)
        copies = []
        for d in range(1, n1):
            copy = copy_to(g4.at[pl.ds(0, chunk), :], gs.at[core, at, :], peer(ax1, d))
            copy.start()
            copies.append(copy)
        gs[core, at, :] = g4[pl.ds(0, chunk), :]
        stage5.append(copies)
        sent += copies

    for copy in late:
        copy.wait_recv()
    for row in range(RD):
        gh_out[row] = cb[row + 1, pl.ds(8, CD), :]
    for dr, dc in SIDES:
        inside = (r - dr >= 0) & (r - dr < n_rows) & (c - dc >= 0) & (c - dc < n_cols)
        keep = jnp.where(inside, 1.0, 0.0).astype(F32)
        rows_at = pl.ds(RD - 1, 1) if dr < 0 else (pl.ds(0, 1) if dr > 0 else pl.ds(0, RD))
        cols_at = pl.ds(CD - 8, 8) if dc < 0 else (pl.ds(0, 8) if dc > 0 else pl.ds(0, CD))
        terms = slot_of(dr, dc, ud_c, lr_c, co_c)[...] * keep
        gh_out[rows_at, cols_at, :] = gh_out[rows_at, cols_at, :] + terms

    write(gh_out, gh_hbm)

    stage6 = []
    for p, (base, lines) in enumerate(AREAS):
        for copy in stage5[p]:
            copy.wait_recv()
        slot = gs.at[core, pl.ds(base, 2 * lines), :]
        copy = copy_to(slot, slot, sibling)
        copy.start()
        stage6.append(copy)
        write(slot, total_hbm.at[core, pl.ds(base, 2 * lines), :])
    sent += stage6
    for p, copy in enumerate(stage6):
        base, lines = AREAS[p]
        copy.wait_recv()
        area = pl.ds(base, 2 * lines)
        write(gs.at[1 - core, area, :], total_hbm.at[1 - core, area, :])

    for copy in written:
        copy.wait()
    for copy in halos:
        copy.wait_send()
    for copy in sent:
        copy.wait_send()


def sizes(p, n1, n2):
    chunk = 2 * AREAS[p][1] // n1
    return chunk, -(-chunk // (16 * n2)) * 16


def shards(frames, hidden_start, cell_start, kernel, gate_bias, cotangent):
    n_rows = lax.axis_size("rows")
    n_cols = lax.axis_size("cols")
    ny = (n_rows // NX) * NYL
    (cz, uz), (cy, uy), (cx, ux) = sizes(0, NZ, ny), sizes(1, ny, NZ), sizes(2, NX, NZ)
    vmem = pltpu.VMEM
    scratch = [
        vmem((RD, CD, HC), BF),
        vmem((RD, CD, HC), F32),
        vmem((RD, CD, HC), F32),
        vmem((1, GATES), F32),
        vmem((RD, CD, HC), BF),
        vmem((3, STEPS, RD, 1280), BF),
        vmem((RD, CD, HC), F32),
        vmem((STEPS, RD, CD, HC), BF),
        vmem((ROWS_W, GATES), BF),
        vmem((2, 6 * CD, HC), BF),
        vmem((2, 3 * RD * 8, HC), BF),
        vmem((4, 6 * 8, HC), BF),
        vmem((2, 6 * CD, HC), BF),
        vmem((2, 3 * RD * 8, HC), BF),
        vmem((4, 6 * 8, HC), BF),
        vmem((STEPS, 16, 1280), F32),
        vmem((STEPS, 12 * WD + 2 * EDGE, HC), F32),
        vmem((STEPS, 12 * WD, HC), BF),
        vmem((10 * WD + 2 * EDGE, HC), F32),
        vmem((8 * WD + 2 * EDGE, HC), F32),
        vmem((KS, 10 * WD, HC), BF),
        vmem((KS, 8 * WD, HC), BF),
        vmem((8 * WD, GATES), F32),
        vmem((5, RD * WD, HC), F32),
        vmem((8 * WD, HC), F32),
        vmem((8 * WD, HC), F32),
        vmem((6 * WD, HC), F32),
        vmem((RD * WD, HC), F32),
        vmem((6 * WD, GATES), BF),
        vmem((2 * RD * WD, GATES), BF),
        vmem((6 * WD + 2 * EDGE, TAPS * HC), F32),
        vmem((RD + 2, WD, HC), F32),
        vmem((2, 1, CD, HC), F32),
        vmem((2, RD, 8, HC), F32),
        vmem((4, 1, 8, HC), F32),
        vmem((LINES, 128), BF),
        vmem((LINES, 128), F32),
        vmem((LINES, 128), BF),
        vmem((LINES, 128), BF),
        vmem((NZ - 1, cz, 128), BF),
        vmem((ny - 1, cy, 128), BF),
        vmem((NX - 1, cx, 128), BF),
        vmem((ny * uz, 128), BF),
        vmem((NZ * uy, 128), BF),
        vmem((NZ * ux, 128), BF),
        vmem((ny - 1, uz, 128), BF),
        vmem((NZ - 1, uy, 128), BF),
        vmem((NZ - 1, ux, 128), BF),
        vmem((NX, uz, 128), BF),
        vmem((NX, uy, 128), BF),
        vmem((ny, ux, 128), BF),
        vmem((ny * uz, 128), BF),
        vmem((NZ * uy, 128), BF),
        vmem((NZ * ux, 128), BF),
        vmem((2, LINES, 128), BF),
        pltpu.SemaphoreType.DMA((8, 2)),
        pltpu.SemaphoreType.DMA((8, 2)),
        pltpu.SemaphoreType.DMA((8,)),
        pltpu.SemaphoreType.DMA((8,)),
        pltpu.SemaphoreType.DMA((5 + 2 * TAPS,)),
        pltpu.SemaphoreType.DMA((3 + 2 * PARTS,)),
        pltpu.SemaphoreType.DMA((stages(n_rows),)),
        pltpu.SemaphoreType.DMA((stages(n_rows),)),
    ]
    in_hbm = pl.BlockSpec(memory_space=pltpu.HBM)
    hidden, grad_hidden, grad_cell, total = pl.pallas_call(
        functools.partial(body, n_rows, n_cols),
        out_shape=(
            jax.ShapeDtypeStruct((RD, CD, HC), BF),
            jax.ShapeDtypeStruct((RD, CD, HC), F32),
            jax.ShapeDtypeStruct((RD, CD, HC), F32),
            jax.ShapeDtypeStruct((2, LINES, 128), BF),
        ),
        in_specs=[in_hbm] * 6,
        out_specs=(in_hbm,) * 4,
        scratch_shapes=scratch,
        compiler_params=pltpu.CompilerParams(
            collective_id=0, has_side_effects=True, vmem_limit_bytes=63 * 1024 * 1024
        ),
    )(frames, hidden_start, cell_start, kernel, gate_bias.reshape(1, GATES), cotangent)
    scale = 1.0 / math.sqrt(STEPS * n_rows * RD * n_cols * CD)
    outs = pl.pallas_call(
        functools.partial(finish, scale),
        out_shape=(
            jax.ShapeDtypeStruct((RD, CD, HC), BF),
            jax.ShapeDtypeStruct((RD, CD, HC), F32),
            jax.ShapeDtypeStruct((RD, CD, HC), F32),
            jax.ShapeDtypeStruct((KIN, GATES), F32),
            jax.ShapeDtypeStruct((1, GATES), F32),
        ),
        in_specs=[in_hbm] * 4,
        out_specs=(in_hbm,) * 5,
        scratch_shapes=[
            vmem((2, LINES, 128), BF),
            vmem((RD, CD, HC), BF),
            vmem((RD, CD, HC), F32),
            vmem((RD, CD, HC), F32),
            vmem((KIN, GATES), F32),
            vmem((1, GATES), F32),
            pltpu.SemaphoreType.DMA((PARTS + 3,)),
            pltpu.SemaphoreType.DMA((TAPS + 4,)),
        ],
        compiler_params=pltpu.CompilerParams(vmem_limit_bytes=63 * 1024 * 1024),
    )(hidden, grad_hidden, grad_cell, total)
    return outs[0], outs[1], outs[2], outs[3], outs[4].reshape(GATES)


def finish(
    scale,
    hid_in,
    gh_in,
    gc_in,
    total_in,
    hid_out,
    gh_out,
    gc_out,
    kg_out,
    bg_out,
    total,
    hid,
    gh,
    gc,
    kg,
    bg,
    in_sem,
    sem,
):
    copies = []

    def put(src, dst):
        copy = pltpu.make_async_copy(src, dst, sem.at[len(copies)])
        copy.start()
        copies.append(copy)

    fetched = []

    def fetch(src, dst):
        copy = pltpu.make_async_copy(src, dst, in_sem.at[len(fetched)])
        copy.start()
        fetched.append(copy)

    for base, lines in AREAS[::-1]:
        area = pl.ds(base, 2 * lines)
        fetch(total_in.at[:, area, :], total.at[:, area, :])
    for src, dst in ((hid_in, hid), (gh_in, gh), (gc_in, gc)):
        fetch(src, dst)

    def take(core, panel, p, row, count):
        base, lines = AREAS[p]
        return total[core, pl.ds(base + panel * lines + row, count), :].astype(F32) * scale

    for p in (2, 1, 0):
        fetched[2 - p].wait()
        for b in range(KS):
            at = (p * KS + b) * 160
            for core in range(2):
                for panel in range(2):
                    cols = pl.ds((2 * core + panel) * 128, 128)
                    kg[pl.ds(at, CI), cols] = take(
                        core, panel, 2, KS * HC + FRAME_ROWS[p][0] + b * CI, CI
                    )
                    kg[pl.ds(at + CI, HC), cols] = take(core, panel, p, b * HC, HC)
            put(kg.at[pl.ds(at, 160), :], kg_out.at[pl.ds(at, 160), :])
    for core in range(2):
        for panel in range(2):
            bg[:, pl.ds((2 * core + panel) * 128, 128)] = take(core, panel, 2, BIAS_ROW, 16)[:1, :]
    put(bg, bg_out)
    for i, (src, dst) in enumerate(((hid, hid_out), (gh, gh_out), (gc, gc_out))):
        fetched[PARTS + i].wait()
        put(src, dst)
    for copy in copies:
        copy.wait()


def stages(n_rows):
    ny = (n_rows // NX) * NYL
    one = (NZ - 1) + (ny - 1) + (NX - 1)
    two = (ny - 1) + (NZ - 1) + (NZ - 1)
    three = (NX - 1) + (NX - 1) + (ny - 1)
    return 2 * PARTS + 2 * one + 2 * two + three


def solution(mesh):
    placed = (
        P(None, "rows", "cols"),
        P("rows", "cols", None),
        P("rows", "cols", None),
        P(),
        P(),
        P(None, "rows", "cols", None),
    )
    return jax.shard_map(
        shards,
        mesh=mesh,
        in_specs=placed,
        out_specs=(
            P("rows", "cols", None),
            P("rows", "cols", None),
            P("rows", "cols", None),
            P(),
            P(),
        ),
        check_vma=False,
    )
```

```python
import functools
import math

import jax
import jax.numpy as jnp
from jax import lax
from jax.experimental import pallas as pl
from jax.experimental.pallas import tpu as pltpu
from jax.sharding import PartitionSpec as P

HC = 128
CI = 32
KS = 3
STEPS = 2
GATES = 512
KIN = 1440
TAPS = 9

NX = 4
NYL = 2
NZ = 8

BF = jnp.bfloat16
F32 = jnp.float32
MESH = pl.DeviceIdType.MESH

RD = 4
CD = 32
WD = 48
EDGE = 8
ROWS_W = 1536
PARTS = 3
HALF = GATES // 2
FRAME_ROWS = ((0, 112), (112, 96), (208, 96))
AREAS = ((0, 384), (768, 384), (1536, 704))
LINES = 2944
ORDER = (2, 0, 1)
BIAS_ROW = 384 + 3 * CI
SIDES = [(dr, dc) for dr in (-1, 0, 1) for dc in (-1, 0, 1) if (dr, dc) != (0, 0)]


def span(step, halo, size):
    if step == 0:
        return (0, size), (halo, size)
    if step > 0:
        return (size - halo, halo), (0, halo)
    return (0, halo), (halo + size, halo)


def far_first(n):
    return sorted(range(1, n), key=lambda d: (-min(d, n - d), d))


def place(x, y, z, core):
    return ((y // NYL) * NX + x, ((y % NYL) * NZ + z) * 2 + core)


def body(
    n_rows,
    n_cols,
    frames_ref,
    hidden_ref,
    cell_ref,
    kernel_ref,
    bias_ref,
    cot_ref,
    hid_hbm,
    gh_hbm,
    gc_hbm,
    total_hbm,
    hid_out,
    gh_out,
    gc_out,
    bias_in,
    hown,
    fl,
    cown,
    kown,
    wp,
    ud,
    st,
    co,
    ud_in,
    st_in,
    co_in,
    fs,
    x32,
    xb,
    s1,
    s2,
    hs1,
    hs2,
    ga,
    sv,
    c0s,
    c1s,
    k1s,
    dcs,
    dg2,
    dgo,
    zs,
    cb,
    ud_c,
    lr_c,
    co_c,
    a0,
    o0,
    r0,
    a1,
    r1z,
    r1y,
    r1x,
    a2z,
    a2y,
    a2x,
    r2z,
    r2y,
    r2x,
    r3z,
    r3y,
    r3x,
    g4z,
    g4y,
    g4x,
    gs,
    halo_send,
    halo_recv,
    late_send,
    late_recv,
    loc_sem,
    out_sem,
    st_send,
    st_recv,
):
    r = lax.axis_index("rows")
    c = lax.axis_index("cols")
    ny = (n_rows // NX) * NYL
    x = lax.rem(r, NX)
    core = lax.rem(c, 2)
    z = lax.rem(c // 2, NZ)
    y = (r // NX) * NYL + c // (2 * NZ)
    size = {"x": NX, "y": ny, "z": NZ}
    mine = {"x": x, "y": y, "z": z}

    def peer(axis, d):
        at = dict(mine)
        at[axis] = lax.rem(mine[axis] + d, size[axis])
        return place(at["x"], at["y"], at["z"], core)

    sibling = place(x, y, z, 1 - core)

    def neighbour(dr, dc):
        return (lax.rem(r + dr + n_rows, n_rows), lax.rem(c + dc + n_cols, n_cols))

    barrier = pltpu.get_barrier_semaphore()
    greet = [neighbour(dr, dc) for dr, dc in SIDES] + [sibling]
    for axis in ("x", "y", "z"):
        greet += [peer(axis, d) for d in range(1, size[axis])]
    for who in greet:
        pl.semaphore_signal(barrier, inc=1, device_id=who, device_id_type=MESH)

    local = []

    def fetch(src, dst):
        copy = pltpu.make_async_copy(src, dst, loc_sem.at[len(local)])
        copy.start()
        local.append(copy)

    fetch(hidden_ref, hown)
    fetch(cell_ref, cown)
    fetch(cot_ref, kown)
    fetch(frames_ref, fl.at[1, :, :, pl.ds(128, CD * CI)])
    fetch(bias_ref, bias_in)
    for tap in range(TAPS):
        a, b = divmod(tap, KS)
        fetch(kernel_ref.at[pl.ds(tap * 160 + CI, HC), :], wp.at[pl.ds(tap * HC, HC), :])
        fetch(
            kernel_ref.at[pl.ds(tap * 160, CI), :],
            wp.at[pl.ds(TAPS * HC + a * 128 + b * CI, CI), :],
        )
    for copy in local[:3]:
        copy.wait()
    fields = (
        ([hown[i] for i in range(RD)], 3),
        ([cown[i] for i in range(RD)], 2),
        ([kown[1, i] for i in range(RD)], 1),
    )

    def edge_rows(step, depth):
        if step == 0:
            return range(RD)
        return range(depth) if step < 0 else range(RD - depth, RD)

    def outgoing(dr, dc):
        pieces = []
        for rows, depth in fields:
            for i in edge_rows(dr, depth):
                piece = rows[i].astype(F32)
                if dc != 0:
                    piece = piece[:8, :] if dc < 0 else piece[CD - 8 :, :]
                pieces.append(piece)
        return jnp.concatenate(pieces, axis=0).astype(BF)

    def slot_of(dr, dc, rows_buf, sides_buf, corners_buf):
        if dc == 0:
            return rows_buf.at[(dr + 1) // 2]
        if dr == 0:
            return sides_buf.at[(dc + 1) // 2]
        return corners_buf.at[(dr + 1) + (dc + 1) // 2]

    for dr, dc in SIDES:
        slot_of(dr, dc, ud, st, co)[...] = outgoing(dr, dc)
    pl.semaphore_wait(barrier, len(greet))

    halos = []
    for i, (dr, dc) in enumerate(SIDES):
        who = neighbour(dr, dc)
        (ls, ln), (lt, _) = span(dc, 128, CD * CI)
        for kind, (src, dst) in enumerate(
            (
                (slot_of(dr, dc, ud, st, co), slot_of(dr, dc, ud_in, st_in, co_in)),
                (frames_ref.at[:, :, pl.ds(ls, ln)], fl.at[1 - dr, :, :, pl.ds(lt, ln)]),
            )
        ):
            copy = pltpu.make_async_remote_copy(
                src_ref=src,
                dst_ref=dst,
                send_sem=halo_send.at[i, kind],
                recv_sem=halo_recv.at[i, kind],
                device_id=who,
                device_id_type=MESH,
            )
            copy.start()
            halos.append(copy)

    for a in range(KS):
        wp[pl.ds(TAPS * HC + a * 128 + 96, 32), :] = jnp.zeros((32, GATES), BF)
    x32[...] = jnp.zeros_like(x32)
    edge = jnp.zeros((EDGE, HC), F32)
    s1[pl.ds(0, EDGE), :] = edge
    s1[pl.ds(EDGE + 10 * WD, EDGE), :] = edge
    s2[pl.ds(0, EDGE), :] = edge
    s2[pl.ds(EDGE + 8 * WD, EDGE), :] = edge
    wide = jnp.zeros((EDGE, TAPS * HC), F32)
    zs[pl.ds(0, EDGE), :] = wide
    zs[pl.ds(EDGE + 6 * WD, EDGE), :] = wide
    fs[...] = jnp.zeros_like(fs)
    for spare in (a2z, a2y, a2x):
        spare[...] = jnp.zeros_like(spare)

    at_col = lax.broadcasted_iota(jnp.int32, (WD, HC), 0) - 8
    in_raster = (at_col + c * CD >= 0) & (at_col + c * CD < n_cols * CD)
    col_mask = jnp.where(in_raster, 1.0, 0.0).astype(F32)
    own_mask = jnp.where((at_col >= 0) & (at_col < CD), 1.0, 0.0).astype(F32)

    def row_mask(row):
        there = r * RD + row
        inside = (there >= 0) & (there < n_rows * RD)
        return col_mask * jnp.where(inside, 1.0, 0.0).astype(F32)

    lane = lax.broadcasted_iota(jnp.int32, (16, 1280), 1)
    line = lax.broadcasted_iota(jnp.int32, (16, 1280), 0)
    there_col = lane // CI - 4 + c * CD
    there_row = line - 4 + r * RD
    frame_mask = jnp.where(
        (there_col >= 0)
        & (there_col < n_cols * CD)
        & (there_row >= 0)
        & (there_row < n_rows * RD),
        1.0,
        0.0,
    ).astype(F32)

    for copy in local[3:]:
        copy.wait()
    for copy in halos:
        copy.wait_recv()

    def incoming(dr, dc):
        return slot_of(-dr, -dc, ud_in, st_in, co_in)[...].astype(F32)

    around = {side: incoming(*side) for side in SIDES}

    def field_row(which, row):
        rows, depth = fields[which]
        before = [d for _, d in fields[:which]]
        dr = -1 if row < 0 else (1 if row >= RD else 0)
        i = row + depth if row < 0 else (row - RD if row >= RD else row)
        parts = []
        for dc in (-1, 0, 1):
            if (dr, dc) == (0, 0):
                parts.append(rows[row].astype(F32))
                continue
            wide_row = CD if dc == 0 else 8
            skip = (RD * which if dr == 0 else sum(before)) * wide_row
            parts.append(around[dr, dc][skip + i * wide_row : skip + (i + 1) * wide_row, :])
        return jnp.concatenate(parts, axis=0)

    for k in range(10):
        s1[pl.ds(EDGE + k * WD, WD), :] = field_row(0, k - 3) * row_mask(k - 3)
    for k in range(8):
        c0s[pl.ds(k * WD, WD), :] = field_row(1, k - 2)
    for k in range(6):
        k1s[pl.ds(k * WD, WD), :] = field_row(2, k - 1)
    for b in range(KS):
        hs1[b] = s1[pl.ds(EDGE + b - 1, 10 * WD), :].astype(BF)
    low = lax.broadcasted_iota(jnp.int32, (12, HC), 1) < CI
    ones = jnp.where(
        lax.broadcasted_iota(jnp.int32, (WD, HC), 1) == 3 * CI, 1.0, 0.0
    ).astype(F32)
    for t in range(STEPS):
        for k in range(3):
            fs[t, pl.ds(4 * k, 4), :] = fl[k, t].astype(F32)
        for g in range(10):
            vals = fs[t, pl.ds(0, 12), pl.ds(g * 128, 128)] * frame_mask[:12, g * 128 : (g + 1) * 128]
            for j in range(4):
                turned = vals if j == 0 else pltpu.roll(vals, 128 - 32 * j, 1)
                x32[t, pl.ds(EDGE + 4 + 4 * g + j, 12, stride=WD), :] = jnp.where(low, turned, 0.0)
        for row in range(12):
            at = EDGE + row * WD
            joined = (
                x32[t, pl.ds(at - 1, WD), :]
                + pltpu.roll(x32[t, pl.ds(at, WD), :], 32, 1)
                + pltpu.roll(x32[t, pl.ds(at + 1, WD), :], 64, 1)
                + ones
            )
            xb[t, pl.ds(row * WD, WD), :] = joined.astype(BF)

    bias = bias_in[...]

    def gates_of(hs, t, first, count):
        size_m = count * WD
        blocks = [
            hs[b, pl.ds(a * WD, size_m), :] for a in range(KS) for b in range(KS)
        ] + [xb[t, pl.ds((first + a) * WD, size_m), :] for a in range(KS)]
        lhs = jnp.concatenate(blocks, axis=1)
        ga[pl.ds(0, size_m), :] = jnp.dot(lhs, wp[...], preferred_element_type=F32)

    def sigmoid(v):
        return 0.5 * jnp.tanh(0.5 * v) + 0.5

    def activated(row):
        pre = ga[pl.ds(row * WD, WD), :] + bias
        return (
            sigmoid(pre[:, :HC]),
            sigmoid(pre[:, HC : 2 * HC]),
            jnp.tanh(pre[:, 2 * HC : 3 * HC]),
            sigmoid(pre[:, 3 * HC :]),
        )

    gates_of(hs1, 0, 1, 8)
    for k in range(8):
        row = k - 2
        gi, gf, gg, go = activated(k)
        now = gf * c0s[pl.ds(k * WD, WD), :] + gi * gg
        th = jnp.tanh(now)
        c1s[pl.ds(k * WD, WD), :] = now
        if 0 <= row < RD:
            at = pl.ds(row * WD, WD)
            for q, val in enumerate((gi, gf, gg, go, th)):
                sv[q, at, :] = val
        h = (go * th).astype(BF).astype(F32)
        s2[pl.ds(EDGE + k * WD, WD), :] = h * row_mask(row)
    for b in range(KS):
        hs2[b] = s2[pl.ds(EDGE + b - 1, 8 * WD), :].astype(BF)

    gates_of(hs2, 1, 2, 6)

    def pre_grads(s, dh, gi, gf, gg, go, th, before):
        return (
            s * gg * gi * (1.0 - gi),
            s * before * gf * (1.0 - gf),
            s * gi * (1.0 - gg * gg),
            dh * th * go * (1.0 - go),
        )

    for k in range(6):
        row = k - 1
        gi, gf, gg, go = activated(k)
        before = c1s[pl.ds((k + 1) * WD, WD), :]
        now = gf * before + gi * gg
        th = jnp.tanh(now)
        dh = k1s[pl.ds(k * WD, WD), :]
        s = dh * go * (1.0 - th * th)
        if 0 <= row < RD:
            hid_out[row] = (go * th)[8 : 8 + CD, :].astype(BF)
            dcs[pl.ds(row * WD, WD), :] = s * gf
        mask = row_mask(row)
        for q, pre in enumerate(pre_grads(s, dh, gi, gf, gg, go, th, before)):
            cols = pl.ds(q * HC, HC)
            dg2[pl.ds(k * WD, WD), cols] = (pre * mask).astype(BF)
            if 0 <= row < RD:
                dgo[pl.ds((RD + row) * WD, WD), cols] = (pre * own_mask).astype(BF)

    def adjoint(dg, count):
        size_m = count * WD
        zs[pl.ds(EDGE, size_m), :] = lax.dot_general(
            dg[pl.ds(0, size_m), :],
            wp[pl.ds(0, TAPS * HC), :],
            (((1,), (1,)), ((), ())),
            preferred_element_type=F32,
        )

    def gathered(k, count):
        total = None
        for tap in range(TAPS):
            a, b = divmod(tap, KS)
            row = k + 2 - a
            if not 0 <= row < count:
                continue
            term = zs[pl.ds(EDGE + row * WD - (b - 1), WD), pl.ds(tap * HC, HC)]
            total = term if total is None else total + term
        return total

    adjoint(dg2, 6)
    for row in range(RD):
        at = pl.ds(row * WD, WD)
        gi, gf, gg, go, th = (sv[q, at, :] for q in range(5))
        inner = gathered(row, 6)
        cot = kown[0, row].astype(F32)
        blank = jnp.zeros((8, HC), F32)
        dh = inner + jnp.concatenate([blank, cot, blank], axis=0)
        s = dcs[at, :] + dh * go * (1.0 - th * th)
        gc_out[row] = (s * gf)[8 : 8 + CD, :]
        before = c0s[pl.ds((row + 2) * WD, WD), :]
        for q, pre in enumerate(pre_grads(s, dh, gi, gf, gg, go, th, before)):
            dgo[at, pl.ds(q * HC, HC)] = (pre * own_mask).astype(BF)

    written = []

    def write(src, dst):
        copy = pltpu.make_async_copy(src, dst, out_sem.at[len(written)])
        copy.start()
        written.append(copy)

    write(hid_out, hid_hbm)
    write(gc_out, gc_hbm)

    count = [0]

    def copy_to(src, dst, who):
        i = count[0]
        count[0] += 1
        return pltpu.make_async_remote_copy(
            src_ref=src,
            dst_ref=dst,
            send_sem=st_send.at[i],
            recv_sem=st_recv.at[i],
            device_id=who,
            device_id_type=MESH,
        )

    sent = []
    mine_at = pl.multiple_of(core * HALF, HALF)
    other_at = pl.multiple_of((1 - core) * HALF, HALF)

    def weight_blocks(p):
        blocks = []
        for q in range(KS * p, KS * p + (KS if p < 2 else 2 * KS)):
            if q < TAPS:
                a, b = divmod(q, KS)
                one = hs1[b, pl.ds((2 + a) * WD, RD * WD), :]
                two = hs2[b, pl.ds((1 + a) * WD, RD * WD), :]
            else:
                a = q - TAPS
                one = xb[0, pl.ds((3 + a) * WD, RD * WD), :]
                two = xb[1, pl.ds((3 + a) * WD, RD * WD), :]
            blocks.append(jnp.concatenate([one, two], axis=0))
        return jnp.concatenate(blocks, axis=1)

    def weight_grad(p, cols_at, out):
        val = lax.dot_general(
            weight_blocks(p),
            dgo[:, pl.ds(cols_at, HALF)],
            (((0,), (0,)), ((), ())),
            preferred_element_type=F32,
        ).astype(out.dtype)
        base, lines = AREAS[p]
        for panel in range(2):
            cut = val[:, panel * 128 : (panel + 1) * 128]
            at = base + panel * lines
            out[pl.ds(at, KS * HC), :] = cut[: KS * HC, :]
            if p == 2:
                for a, (first, size_a) in enumerate(FRAME_ROWS):
                    start = (KS + a) * HC
                    out[pl.ds(at + KS * HC + first, size_a), :] = cut[start : start + size_a, :]
                out[pl.ds(at + lines - 16, 16), :] = jnp.zeros((16, 128), out.dtype)

    swaps = [None] * PARTS
    for p in ORDER:
        base, lines = AREAS[p]
        weight_grad(p, other_at, a0)
        area = pl.ds(base, 2 * lines)
        copy = copy_to(a0.at[area, :], r0.at[area, :], sibling)
        copy.start()
        swaps[p] = copy
    for p in ORDER:
        weight_grad(p, mine_at, o0)
    sent += swaps

    plans = [
        ("z", "y", "x", r1z, a2z, r2z, r3z, g4z),
        ("y", "z", "x", r1y, a2y, r2y, r3y, g4y),
        ("x", "z", "y", r1x, a2x, r2x, r3x, g4x),
    ]

    stage1 = [None] * PARTS
    for p in ORDER:
        ax1, ax2, ax3, r1, a2, r2, r3, g4 = plans[p]
        base, lines = AREAS[p]
        n1, chunk = size[ax1], r1.shape[1]
        swaps[p].wait_recv()
        area = pl.ds(base, 2 * lines)
        a1[area, :] = (o0[area, :] + r0[area, :].astype(F32)).astype(BF)
        copies = []
        for d in far_first(n1):
            to = pl.multiple_of(base + lax.rem(mine[ax1] + d, n1) * chunk, 16)
            copy = copy_to(a1.at[pl.ds(to, chunk), :], r1.at[d - 1], peer(ax1, d))
            copy.start()
            copies.append(copy)
        stage1[p] = copies
        sent += copies

    adjoint(dgo, RD)
    zs[pl.ds(EDGE + RD * WD, EDGE), :] = wide
    for k in range(RD + 2):
        cb[k] = gathered(k - 2, RD)
    stage2 = [None] * PARTS
    for p in ORDER:
        ax1, ax2, ax3, r1, a2, r2, r3, g4 = plans[p]
        base, lines = AREAS[p]
        n1, chunk = size[ax1], r1.shape[1]
        n2, unit = size[ax2], r2.shape[1]
        for copy in stage1[p]:
            copy.wait_recv()
        at = pl.multiple_of(base + mine[ax1] * chunk, 16)
        total = a1[pl.ds(at, chunk), :].astype(F32)
        for d in range(1, n1):
            total = total + r1[d - 1].astype(F32)
        a2[pl.ds(0, chunk), :] = total.astype(BF)
        copies = []
        for d in far_first(n2):
            to = pl.multiple_of(lax.rem(mine[ax2] + d, n2) * unit, 16)
            copy = copy_to(a2.at[pl.ds(to, unit), :], r2.at[d - 1], peer(ax2, d))
            copy.start()
            copies.append(copy)
        stage2[p] = copies
        sent += copies

    late = []
    for i, (dr, dc) in enumerate(SIDES):
        rows_at = pl.ds(0, 1) if dr < 0 else (pl.ds(RD + 1, 1) if dr > 0 else pl.ds(1, RD))
        cols_at = pl.ds(0, 8) if dc < 0 else (pl.ds(8 + CD, 8) if dc > 0 else pl.ds(8, CD))
        copy = pltpu.make_async_remote_copy(
            src_ref=cb.at[rows_at, cols_at, :],
            dst_ref=slot_of(dr, dc, ud_c, lr_c, co_c),
            send_sem=late_send.at[i],
            recv_sem=late_recv.at[i],
            device_id=neighbour(dr, dc),
            device_id_type=MESH,
        )
        copy.start()
        late.append(copy)
    sent += late

    stage3 = [None] * PARTS
    for p in ORDER:
        ax1, ax2, ax3, r1, a2, r2, r3, g4 = plans[p]
        n2, n3, unit = size[ax2], size[ax3], r2.shape[1]
        for copy in stage2[p]:
            copy.wait_recv()
        total = a2[pl.ds(pl.multiple_of(mine[ax2] * unit, 16), unit), :].astype(F32)
        for d in range(1, n2):
            total = total + r2[d - 1].astype(F32)
        r3[mine[ax3]] = total.astype(BF)
        copies = []
        for d in far_first(n3):
            copy = copy_to(r3.at[mine[ax3]], r3.at[mine[ax3]], peer(ax3, d))
            copy.start()
            copies.append(copy)
        stage3[p] = copies
        sent += copies

    stage4 = [None] * PARTS
    for p in ORDER:
        ax1, ax2, ax3, r1, a2, r2, r3, g4 = plans[p]
        n2, n3, unit = size[ax2], size[ax3], r2.shape[1]
        for copy in stage3[p]:
            copy.wait_recv()
        total = r3[0].astype(F32)
        for d in range(1, n3):
            total = total + r3[d].astype(F32)
        slot = g4.at[pl.ds(pl.multiple_of(mine[ax2] * unit, 16), unit), :]
        slot[...] = total.astype(BF)
        copies = []
        for d in far_first(n2):
            copy = copy_to(slot, slot, peer(ax2, d))
            copy.start()
            copies.append(copy)
        stage4[p] = copies
        sent += copies

    stage5 = [None] * PARTS
    for p in ORDER:
        ax1, ax2, ax3, r1, a2, r2, r3, g4 = plans[p]
        base, lines = AREAS[p]
        n1, chunk = size[ax1], r1.shape[1]
        for copy in stage4[p]:
            copy.wait_recv()
        at = pl.ds(pl.multiple_of(base + mine[ax1] * chunk, 16), chunk)
        copies = []
        for d in far_first(n1):
            copy = copy_to(g4.at[pl.ds(0, chunk), :], gs.at[core, at, :], peer(ax1, d))
            copy.start()
            copies.append(copy)
        gs[core, at, :] = g4[pl.ds(0, chunk), :]
        stage5[p] = copies
        sent += copies

    for copy in late:
        copy.wait_recv()
    for row in range(RD):
        gh_out[row] = cb[row + 1, pl.ds(8, CD), :]
    for dr, dc in SIDES:
        inside = (r - dr >= 0) & (r - dr < n_rows) & (c - dc >= 0) & (c - dc < n_cols)
        keep = jnp.where(inside, 1.0, 0.0).astype(F32)
        rows_at = pl.ds(RD - 1, 1) if dr < 0 else (pl.ds(0, 1) if dr > 0 else pl.ds(0, RD))
        cols_at = pl.ds(CD - 8, 8) if dc < 0 else (pl.ds(0, 8) if dc > 0 else pl.ds(0, CD))
        terms = slot_of(dr, dc, ud_c, lr_c, co_c)[...] * keep
        gh_out[rows_at, cols_at, :] = gh_out[rows_at, cols_at, :] + terms

    write(gh_out, gh_hbm)

    stage6 = [None] * PARTS
    for p in ORDER:
        base, lines = AREAS[p]
        for copy in stage5[p]:
            copy.wait_recv()
        slot = gs.at[core, pl.ds(base, 2 * lines), :]
        copy = copy_to(slot, slot, sibling)
        copy.start()
        stage6[p] = copy
        write(slot, total_hbm.at[core, pl.ds(base, 2 * lines), :])
    sent += stage6
    for p in ORDER:
        base, lines = AREAS[p]
        copy = stage6[p]
        copy.wait_recv()
        area = pl.ds(base, 2 * lines)
        write(gs.at[1 - core, area, :], total_hbm.at[1 - core, area, :])

    for copy in written:
        copy.wait()
    for copy in halos:
        copy.wait_send()
    for copy in sent:
        copy.wait_send()


def sizes(p, n1, n2):
    chunk = 2 * AREAS[p][1] // n1
    return chunk, -(-chunk // (16 * n2)) * 16


def shards(frames, hidden_start, cell_start, kernel, gate_bias, cotangent):
    n_rows = lax.axis_size("rows")
    n_cols = lax.axis_size("cols")
    ny = (n_rows // NX) * NYL
    (cz, uz), (cy, uy), (cx, ux) = sizes(0, NZ, ny), sizes(1, ny, NZ), sizes(2, NX, NZ)
    vmem = pltpu.VMEM
    scratch = [
        vmem((RD, CD, HC), BF),
        vmem((RD, CD, HC), F32),
        vmem((RD, CD, HC), F32),
        vmem((1, GATES), F32),
        vmem((RD, CD, HC), BF),
        vmem((3, STEPS, RD, 1280), BF),
        vmem((RD, CD, HC), F32),
        vmem((STEPS, RD, CD, HC), BF),
        vmem((ROWS_W, GATES), BF),
        vmem((2, 6 * CD, HC), BF),
        vmem((2, 3 * RD * 8, HC), BF),
        vmem((4, 6 * 8, HC), BF),
        vmem((2, 6 * CD, HC), BF),
        vmem((2, 3 * RD * 8, HC), BF),
        vmem((4, 6 * 8, HC), BF),
        vmem((STEPS, 16, 1280), F32),
        vmem((STEPS, 12 * WD + 2 * EDGE, HC), F32),
        vmem((STEPS, 12 * WD, HC), BF),
        vmem((10 * WD + 2 * EDGE, HC), F32),
        vmem((8 * WD + 2 * EDGE, HC), F32),
        vmem((KS, 10 * WD, HC), BF),
        vmem((KS, 8 * WD, HC), BF),
        vmem((8 * WD, GATES), F32),
        vmem((5, RD * WD, HC), F32),
        vmem((8 * WD, HC), F32),
        vmem((8 * WD, HC), F32),
        vmem((6 * WD, HC), F32),
        vmem((RD * WD, HC), F32),
        vmem((6 * WD, GATES), BF),
        vmem((2 * RD * WD, GATES), BF),
        vmem((6 * WD + 2 * EDGE, TAPS * HC), F32),
        vmem((RD + 2, WD, HC), F32),
        vmem((2, 1, CD, HC), F32),
        vmem((2, RD, 8, HC), F32),
        vmem((4, 1, 8, HC), F32),
        vmem((LINES, 128), BF),
        vmem((LINES, 128), F32),
        vmem((LINES, 128), BF),
        vmem((LINES, 128), BF),
        vmem((NZ - 1, cz, 128), BF),
        vmem((ny - 1, cy, 128), BF),
        vmem((NX - 1, cx, 128), BF),
        vmem((ny * uz, 128), BF),
        vmem((NZ * uy, 128), BF),
        vmem((NZ * ux, 128), BF),
        vmem((ny - 1, uz, 128), BF),
        vmem((NZ - 1, uy, 128), BF),
        vmem((NZ - 1, ux, 128), BF),
        vmem((NX, uz, 128), BF),
        vmem((NX, uy, 128), BF),
        vmem((ny, ux, 128), BF),
        vmem((ny * uz, 128), BF),
        vmem((NZ * uy, 128), BF),
        vmem((NZ * ux, 128), BF),
        vmem((2, LINES, 128), BF),
        pltpu.SemaphoreType.DMA((8, 2)),
        pltpu.SemaphoreType.DMA((8, 2)),
        pltpu.SemaphoreType.DMA((8,)),
        pltpu.SemaphoreType.DMA((8,)),
        pltpu.SemaphoreType.DMA((5 + 2 * TAPS,)),
        pltpu.SemaphoreType.DMA((3 + 2 * PARTS,)),
        pltpu.SemaphoreType.DMA((stages(n_rows),)),
        pltpu.SemaphoreType.DMA((stages(n_rows),)),
    ]
    in_hbm = pl.BlockSpec(memory_space=pltpu.HBM)
    hidden, grad_hidden, grad_cell, total = pl.pallas_call(
        functools.partial(body, n_rows, n_cols),
        out_shape=(
            jax.ShapeDtypeStruct((RD, CD, HC), BF),
            jax.ShapeDtypeStruct((RD, CD, HC), F32),
            jax.ShapeDtypeStruct((RD, CD, HC), F32),
            jax.ShapeDtypeStruct((2, LINES, 128), BF),
        ),
        in_specs=[in_hbm] * 6,
        out_specs=(in_hbm,) * 4,
        scratch_shapes=scratch,
        compiler_params=pltpu.CompilerParams(
            collective_id=0, has_side_effects=True, vmem_limit_bytes=63 * 1024 * 1024
        ),
    )(frames, hidden_start, cell_start, kernel, gate_bias.reshape(1, GATES), cotangent)
    scale = 1.0 / math.sqrt(STEPS * n_rows * RD * n_cols * CD)
    outs = pl.pallas_call(
        functools.partial(finish, scale),
        out_shape=(
            jax.ShapeDtypeStruct((RD, CD, HC), BF),
            jax.ShapeDtypeStruct((RD, CD, HC), F32),
            jax.ShapeDtypeStruct((RD, CD, HC), F32),
            jax.ShapeDtypeStruct((KIN, GATES), F32),
            jax.ShapeDtypeStruct((1, GATES), F32),
        ),
        in_specs=[in_hbm] * 4,
        out_specs=(in_hbm,) * 5,
        scratch_shapes=[
            vmem((2, LINES, 128), BF),
            vmem((RD, CD, HC), BF),
            vmem((RD, CD, HC), F32),
            vmem((RD, CD, HC), F32),
            vmem((KIN, GATES), F32),
            vmem((1, GATES), F32),
            pltpu.SemaphoreType.DMA((PARTS + 3,)),
            pltpu.SemaphoreType.DMA((TAPS + 4,)),
        ],
        compiler_params=pltpu.CompilerParams(vmem_limit_bytes=63 * 1024 * 1024),
    )(hidden, grad_hidden, grad_cell, total)
    return outs[0], outs[1], outs[2], outs[3], outs[4].reshape(GATES)


def finish(
    scale,
    hid_in,
    gh_in,
    gc_in,
    total_in,
    hid_out,
    gh_out,
    gc_out,
    kg_out,
    bg_out,
    total,
    hid,
    gh,
    gc,
    kg,
    bg,
    in_sem,
    sem,
):
    copies = []

    def put(src, dst):
        copy = pltpu.make_async_copy(src, dst, sem.at[len(copies)])
        copy.start()
        copies.append(copy)

    fetched = []

    def fetch(src, dst):
        copy = pltpu.make_async_copy(src, dst, in_sem.at[len(fetched)])
        copy.start()
        fetched.append(copy)

    for base, lines in AREAS[::-1]:
        area = pl.ds(base, 2 * lines)
        fetch(total_in.at[:, area, :], total.at[:, area, :])
    for src, dst in ((hid_in, hid), (gh_in, gh), (gc_in, gc)):
        fetch(src, dst)

    def take(core, panel, p, row, count):
        base, lines = AREAS[p]
        return total[core, pl.ds(base + panel * lines + row, count), :].astype(F32) * scale

    for p in (2, 1, 0):
        fetched[2 - p].wait()
        for b in range(KS):
            at = (p * KS + b) * 160
            for core in range(2):
                for panel in range(2):
                    cols = pl.ds((2 * core + panel) * 128, 128)
                    kg[pl.ds(at, CI), cols] = take(
                        core, panel, 2, KS * HC + FRAME_ROWS[p][0] + b * CI, CI
                    )
                    kg[pl.ds(at + CI, HC), cols] = take(core, panel, p, b * HC, HC)
            put(kg.at[pl.ds(at, 160), :], kg_out.at[pl.ds(at, 160), :])
    for core in range(2):
        for panel in range(2):
            bg[:, pl.ds((2 * core + panel) * 128, 128)] = take(core, panel, 2, BIAS_ROW, 16)[:1, :]
    put(bg, bg_out)
    for i, (src, dst) in enumerate(((hid, hid_out), (gh, gh_out), (gc, gc_out))):
        fetched[PARTS + i].wait()
        put(src, dst)
    for copy in copies:
        copy.wait()


def stages(n_rows):
    ny = (n_rows // NX) * NYL
    one = (NZ - 1) + (ny - 1) + (NX - 1)
    two = (ny - 1) + (NZ - 1) + (NZ - 1)
    three = (NX - 1) + (NX - 1) + (ny - 1)
    return 2 * PARTS + 2 * one + 2 * two + three


def solution(mesh):
    placed = (
        P(None, "rows", "cols"),
        P("rows", "cols", None),
        P("rows", "cols", None),
        P(),
        P(),
        P(None, "rows", "cols", None),
    )
    return jax.shard_map(
        shards,
        mesh=mesh,
        in_specs=placed,
        out_specs=(
            P("rows", "cols", None),
            P("rows", "cols", None),
            P("rows", "cols", None),
            P(),
            P(),
        ),
        check_vma=False,
    )
```

```python
import functools
import math

import jax
import jax.numpy as jnp
from jax import lax
from jax.experimental import pallas as pl
from jax.experimental.pallas import tpu as pltpu
from jax.sharding import PartitionSpec as P

HC = 128
CI = 32
KS = 3
STEPS = 2
GATES = 512
KIN = 1440
TAPS = 9

NX = 4
NYL = 2
NZ = 8

BF = jnp.bfloat16
F32 = jnp.float32
MESH = pl.DeviceIdType.MESH

RD = 4
CD = 32
WD = 48
EDGE = 8
ROWS_W = 1536
PARTS = 3
HALF = GATES // 2
FRAME_ROWS = ((0, 112), (112, 96), (208, 96))
AREAS = ((0, 384), (768, 384), (1536, 704))
LINES = 2944
ORDER = (2, 0, 1)
BIAS_ROW = 384 + 3 * CI
SIDES = [(dr, dc) for dr in (-1, 0, 1) for dc in (-1, 0, 1) if (dr, dc) != (0, 0)]


def span(step, halo, size):
    if step == 0:
        return (0, size), (halo, size)
    if step > 0:
        return (size - halo, halo), (0, halo)
    return (0, halo), (halo + size, halo)


def far_first(n):
    return sorted(range(1, n), key=lambda d: (-min(d, n - d), d))


def place(x, y, z, core):
    return ((y // NYL) * NX + x, ((y % NYL) * NZ + z) * 2 + core)


def body(
    n_rows,
    n_cols,
    frames_ref,
    hidden_ref,
    cell_ref,
    kernel_ref,
    bias_ref,
    cot_ref,
    hid_hbm,
    gh_hbm,
    gc_hbm,
    total_hbm,
    hid_out,
    gh_out,
    gc_out,
    bias_in,
    hown,
    fl,
    cown,
    kown,
    wp,
    ud,
    st,
    co,
    ud_in,
    st_in,
    co_in,
    fs,
    x32,
    xb,
    s1,
    s2,
    hs1,
    hs2,
    ga,
    sv,
    c0s,
    c1s,
    k1s,
    dcs,
    dg2,
    dgo,
    zs,
    cb,
    ud_c,
    lr_c,
    co_c,
    a0,
    o0,
    r0,
    a1,
    r1z,
    r1y,
    r1x,
    a2z,
    a2y,
    a2x,
    r2z,
    r2y,
    r2x,
    r3z,
    r3y,
    r3x,
    g4z,
    g4y,
    g4x,
    gs,
    halo_send,
    halo_recv,
    late_send,
    late_recv,
    loc_sem,
    out_sem,
    st_send,
    st_recv,
):
    r = lax.axis_index("rows")
    c = lax.axis_index("cols")
    ny = (n_rows // NX) * NYL
    x = lax.rem(r, NX)
    core = lax.rem(c, 2)
    z = lax.rem(c // 2, NZ)
    y = (r // NX) * NYL + c // (2 * NZ)
    size = {"x": NX, "y": ny, "z": NZ}
    mine = {"x": x, "y": y, "z": z}

    def peer(axis, d):
        at = dict(mine)
        at[axis] = lax.rem(mine[axis] + d, size[axis])
        return place(at["x"], at["y"], at["z"], core)

    sibling = place(x, y, z, 1 - core)

    def neighbour(dr, dc):
        return (lax.rem(r + dr + n_rows, n_rows), lax.rem(c + dc + n_cols, n_cols))

    barrier = pltpu.get_barrier_semaphore()
    greet = [neighbour(dr, dc) for dr, dc in SIDES] + [sibling]
    for axis in ("x", "y", "z"):
        greet += [peer(axis, d) for d in range(1, size[axis])]
    for who in greet:
        pl.semaphore_signal(barrier, inc=1, device_id=who, device_id_type=MESH)

    local = []

    def fetch(src, dst):
        copy = pltpu.make_async_copy(src, dst, loc_sem.at[len(local)])
        copy.start()
        local.append(copy)

    fetch(hidden_ref, hown)
    fetch(cell_ref, cown)
    fetch(cot_ref, kown)
    fetch(frames_ref, fl.at[1, :, :, pl.ds(128, CD * CI)])
    fetch(bias_ref, bias_in)
    for tap in range(TAPS):
        a, b = divmod(tap, KS)
        fetch(kernel_ref.at[pl.ds(tap * 160 + CI, HC), :], wp.at[pl.ds(tap * HC, HC), :])
        fetch(
            kernel_ref.at[pl.ds(tap * 160, CI), :],
            wp.at[pl.ds(TAPS * HC + a * 128 + b * CI, CI), :],
        )
    for copy in local[:3]:
        copy.wait()
    fields = (
        ([hown[i] for i in range(RD)], 3),
        ([cown[i] for i in range(RD)], 2),
        ([kown[1, i] for i in range(RD)], 1),
    )

    def edge_rows(step, depth):
        if step == 0:
            return range(RD)
        return range(depth) if step < 0 else range(RD - depth, RD)

    def outgoing(dr, dc):
        pieces = []
        for rows, depth in fields:
            for i in edge_rows(dr, depth):
                piece = rows[i].astype(F32)
                if dc != 0:
                    piece = piece[:8, :] if dc < 0 else piece[CD - 8 :, :]
                pieces.append(piece)
        return jnp.concatenate(pieces, axis=0).astype(BF)

    def slot_of(dr, dc, rows_buf, sides_buf, corners_buf):
        if dc == 0:
            return rows_buf.at[(dr + 1) // 2]
        if dr == 0:
            return sides_buf.at[(dc + 1) // 2]
        return corners_buf.at[(dr + 1) + (dc + 1) // 2]

    for dr, dc in SIDES:
        slot_of(dr, dc, ud, st, co)[...] = outgoing(dr, dc)
    pl.semaphore_wait(barrier, len(greet))

    halos = []
    for i, (dr, dc) in enumerate(SIDES):
        who = neighbour(dr, dc)
        (ls, ln), (lt, _) = span(dc, 128, CD * CI)
        for kind, (src, dst) in enumerate(
            (
                (slot_of(dr, dc, ud, st, co), slot_of(dr, dc, ud_in, st_in, co_in)),
                (frames_ref.at[:, :, pl.ds(ls, ln)], fl.at[1 - dr, :, :, pl.ds(lt, ln)]),
            )
        ):
            copy = pltpu.make_async_remote_copy(
                src_ref=src,
                dst_ref=dst,
                send_sem=halo_send.at[i, kind],
                recv_sem=halo_recv.at[i, kind],
                device_id=who,
                device_id_type=MESH,
            )
            copy.start()
            halos.append(copy)

    for a in range(KS):
        wp[pl.ds(TAPS * HC + a * 128 + 96, 32), :] = jnp.zeros((32, GATES), BF)
    x32[...] = jnp.zeros_like(x32)
    edge = jnp.zeros((EDGE, HC), F32)
    s1[pl.ds(0, EDGE), :] = edge
    s1[pl.ds(EDGE + 10 * WD, EDGE), :] = edge
    s2[pl.ds(0, EDGE), :] = edge
    s2[pl.ds(EDGE + 8 * WD, EDGE), :] = edge
    wide = jnp.zeros((EDGE, TAPS * HC), F32)
    zs[pl.ds(0, EDGE), :] = wide
    zs[pl.ds(EDGE + 6 * WD, EDGE), :] = wide
    fs[...] = jnp.zeros_like(fs)
    for spare in (a2z, a2y, a2x):
        spare[...] = jnp.zeros_like(spare)

    at_col = lax.broadcasted_iota(jnp.int32, (WD, HC), 0) - 8
    in_raster = (at_col + c * CD >= 0) & (at_col + c * CD < n_cols * CD)
    col_mask = jnp.where(in_raster, 1.0, 0.0).astype(F32)
    own_mask = jnp.where((at_col >= 0) & (at_col < CD), 1.0, 0.0).astype(F32)

    def row_mask(row):
        there = r * RD + row
        inside = (there >= 0) & (there < n_rows * RD)
        return col_mask * jnp.where(inside, 1.0, 0.0).astype(F32)

    lane = lax.broadcasted_iota(jnp.int32, (16, 1280), 1)
    line = lax.broadcasted_iota(jnp.int32, (16, 1280), 0)
    there_col = lane // CI - 4 + c * CD
    there_row = line - 4 + r * RD
    frame_mask = jnp.where(
        (there_col >= 0)
        & (there_col < n_cols * CD)
        & (there_row >= 0)
        & (there_row < n_rows * RD),
        1.0,
        0.0,
    ).astype(F32)

    for copy in local[3:]:
        copy.wait()
    for copy in halos:
        copy.wait_recv()

    def incoming(dr, dc):
        return slot_of(-dr, -dc, ud_in, st_in, co_in)[...].astype(F32)

    around = {side: incoming(*side) for side in SIDES}

    def field_row(which, row):
        rows, depth = fields[which]
        before = [d for _, d in fields[:which]]
        dr = -1 if row < 0 else (1 if row >= RD else 0)
        i = row + depth if row < 0 else (row - RD if row >= RD else row)
        parts = []
        for dc in (-1, 0, 1):
            if (dr, dc) == (0, 0):
                parts.append(rows[row].astype(F32))
                continue
            wide_row = CD if dc == 0 else 8
            skip = (RD * which if dr == 0 else sum(before)) * wide_row
            parts.append(around[dr, dc][skip + i * wide_row : skip + (i + 1) * wide_row, :])
        return jnp.concatenate(parts, axis=0)

    for k in range(10):
        s1[pl.ds(EDGE + k * WD, WD), :] = field_row(0, k - 3) * row_mask(k - 3)
    for k in range(8):
        c0s[pl.ds(k * WD, WD), :] = field_row(1, k - 2)
    for k in range(6):
        k1s[pl.ds(k * WD, WD), :] = field_row(2, k - 1)
    for b in range(KS):
        hs1[b] = s1[pl.ds(EDGE + b - 1, 10 * WD), :].astype(BF)
    low = lax.broadcasted_iota(jnp.int32, (12, HC), 1) < CI
    ones = jnp.where(
        lax.broadcasted_iota(jnp.int32, (WD, HC), 1) == 3 * CI, 1.0, 0.0
    ).astype(F32)
    for t in range(STEPS):
        for k in range(3):
            fs[t, pl.ds(4 * k, 4), :] = fl[k, t].astype(F32)
        for g in range(10):
            vals = fs[t, pl.ds(0, 12), pl.ds(g * 128, 128)] * frame_mask[:12, g * 128 : (g + 1) * 128]
            for j in range(4):
                turned = vals if j == 0 else pltpu.roll(vals, 128 - 32 * j, 1)
                x32[t, pl.ds(EDGE + 4 + 4 * g + j, 12, stride=WD), :] = jnp.where(low, turned, 0.0)
        for row in range(12):
            at = EDGE + row * WD
            joined = (
                x32[t, pl.ds(at - 1, WD), :]
                + pltpu.roll(x32[t, pl.ds(at, WD), :], 32, 1)
                + pltpu.roll(x32[t, pl.ds(at + 1, WD), :], 64, 1)
                + ones
            )
            xb[t, pl.ds(row * WD, WD), :] = joined.astype(BF)

    bias = bias_in[...]

    def gates_of(hs, t, first, count):
        size_m = count * WD
        blocks = [
            hs[b, pl.ds(a * WD, size_m), :] for a in range(KS) for b in range(KS)
        ] + [xb[t, pl.ds((first + a) * WD, size_m), :] for a in range(KS)]
        lhs = jnp.concatenate(blocks, axis=1)
        ga[pl.ds(0, size_m), :] = jnp.dot(lhs, wp[...], preferred_element_type=F32)

    def sigmoid(v):
        return 0.5 * jnp.tanh(0.5 * v) + 0.5

    def activated(row):
        pre = ga[pl.ds(row * WD, WD), :] + bias
        return (
            sigmoid(pre[:, :HC]),
            sigmoid(pre[:, HC : 2 * HC]),
            jnp.tanh(pre[:, 2 * HC : 3 * HC]),
            sigmoid(pre[:, 3 * HC :]),
        )

    gates_of(hs1, 0, 1, 8)
    for k in range(8):
        row = k - 2
        gi, gf, gg, go = activated(k)
        now = gf * c0s[pl.ds(k * WD, WD), :] + gi * gg
        th = jnp.tanh(now)
        c1s[pl.ds(k * WD, WD), :] = now
        if 0 <= row < RD:
            at = pl.ds(row * WD, WD)
            for q, val in enumerate((gi, gf, gg, go, th)):
                sv[q, at, :] = val
        h = (go * th).astype(BF).astype(F32)
        s2[pl.ds(EDGE + k * WD, WD), :] = h * row_mask(row)
    for b in range(KS):
        hs2[b] = s2[pl.ds(EDGE + b - 1, 8 * WD), :].astype(BF)

    gates_of(hs2, 1, 2, 6)

    def pre_grads(s, dh, gi, gf, gg, go, th, before):
        return (
            s * gg * gi * (1.0 - gi),
            s * before * gf * (1.0 - gf),
            s * gi * (1.0 - gg * gg),
            dh * th * go * (1.0 - go),
        )

    for k in range(6):
        row = k - 1
        gi, gf, gg, go = activated(k)
        before = c1s[pl.ds((k + 1) * WD, WD), :]
        now = gf * before + gi * gg
        th = jnp.tanh(now)
        dh = k1s[pl.ds(k * WD, WD), :]
        s = dh * go * (1.0 - th * th)
        if 0 <= row < RD:
            hid_out[row] = (go * th)[8 : 8 + CD, :].astype(BF)
            dcs[pl.ds(row * WD, WD), :] = s * gf
        mask = row_mask(row)
        for q, pre in enumerate(pre_grads(s, dh, gi, gf, gg, go, th, before)):
            cols = pl.ds(q * HC, HC)
            dg2[pl.ds(k * WD, WD), cols] = (pre * mask).astype(BF)
            if 0 <= row < RD:
                dgo[pl.ds((RD + row) * WD, WD), cols] = (pre * own_mask).astype(BF)

    def adjoint(dg, count):
        size_m = count * WD
        zs[pl.ds(EDGE, size_m), :] = lax.dot_general(
            dg[pl.ds(0, size_m), :],
            wp[pl.ds(0, TAPS * HC), :],
            (((1,), (1,)), ((), ())),
            preferred_element_type=F32,
        )

    def gathered(k, count):
        total = None
        for tap in range(TAPS):
            a, b = divmod(tap, KS)
            row = k + 2 - a
            if not 0 <= row < count:
                continue
            term = zs[pl.ds(EDGE + row * WD - (b - 1), WD), pl.ds(tap * HC, HC)]
            total = term if total is None else total + term
        return total

    adjoint(dg2, 6)
    for row in range(RD):
        at = pl.ds(row * WD, WD)
        gi, gf, gg, go, th = (sv[q, at, :] for q in range(5))
        inner = gathered(row, 6)
        cot = kown[0, row].astype(F32)
        blank = jnp.zeros((8, HC), F32)
        dh = inner + jnp.concatenate([blank, cot, blank], axis=0)
        s = dcs[at, :] + dh * go * (1.0 - th * th)
        gc_out[row] = (s * gf)[8 : 8 + CD, :]
        before = c0s[pl.ds((row + 2) * WD, WD), :]
        for q, pre in enumerate(pre_grads(s, dh, gi, gf, gg, go, th, before)):
            dgo[at, pl.ds(q * HC, HC)] = (pre * own_mask).astype(BF)

    written = []

    def write(src, dst):
        copy = pltpu.make_async_copy(src, dst, out_sem.at[len(written)])
        copy.start()
        written.append(copy)

    write(hid_out, hid_hbm)
    write(gc_out, gc_hbm)

    count = [0]

    def copy_to(src, dst, who):
        i = count[0]
        count[0] += 1
        return pltpu.make_async_remote_copy(
            src_ref=src,
            dst_ref=dst,
            send_sem=st_send.at[i],
            recv_sem=st_recv.at[i],
            device_id=who,
            device_id_type=MESH,
        )

    sent = []
    mine_at = pl.multiple_of(core * HALF, HALF)
    other_at = pl.multiple_of((1 - core) * HALF, HALF)

    def weight_blocks(p):
        blocks = []
        for q in range(KS * p, KS * p + (KS if p < 2 else 2 * KS)):
            if q < TAPS:
                a, b = divmod(q, KS)
                one = hs1[b, pl.ds((2 + a) * WD, RD * WD), :]
                two = hs2[b, pl.ds((1 + a) * WD, RD * WD), :]
            else:
                a = q - TAPS
                one = xb[0, pl.ds((3 + a) * WD, RD * WD), :]
                two = xb[1, pl.ds((3 + a) * WD, RD * WD), :]
            blocks.append(jnp.concatenate([one, two], axis=0))
        return jnp.concatenate(blocks, axis=1)

    def weight_grad(p, cols_at, out):
        val = lax.dot_general(
            weight_blocks(p),
            dgo[:, pl.ds(cols_at, HALF)],
            (((0,), (0,)), ((), ())),
            preferred_element_type=F32,
        ).astype(out.dtype)
        base, lines = AREAS[p]
        for panel in range(2):
            cut = val[:, panel * 128 : (panel + 1) * 128]
            at = base + panel * lines
            out[pl.ds(at, KS * HC), :] = cut[: KS * HC, :]
            if p == 2:
                for a, (first, size_a) in enumerate(FRAME_ROWS):
                    start = (KS + a) * HC
                    out[pl.ds(at + KS * HC + first, size_a), :] = cut[start : start + size_a, :]
                out[pl.ds(at + lines - 16, 16), :] = jnp.zeros((16, 128), out.dtype)

    swaps = [None] * PARTS
    for p in ORDER:
        base, lines = AREAS[p]
        weight_grad(p, other_at, a0)
        area = pl.ds(base, 2 * lines)
        copy = copy_to(a0.at[area, :], r0.at[area, :], sibling)
        copy.start()
        swaps[p] = copy
    for p in ORDER:
        weight_grad(p, mine_at, o0)
    sent += swaps

    plans = [
        ("z", "y", "x", r1z, a2z, r2z, r3z, g4z),
        ("y", "z", "x", r1y, a2y, r2y, r3y, g4y),
        ("x", "z", "y", r1x, a2x, r2x, r3x, g4x),
    ]

    stage1 = [None] * PARTS
    for p in ORDER:
        ax1, ax2, ax3, r1, a2, r2, r3, g4 = plans[p]
        base, lines = AREAS[p]
        n1, chunk = size[ax1], r1.shape[1]
        swaps[p].wait_recv()
        copies = []
        for d in far_first(n1) + [0]:
            to = pl.multiple_of(base + lax.rem(mine[ax1] + d, n1) * chunk, 16)
            at = pl.ds(to, chunk)
            a1[at, :] = (o0[at, :] + r0[at, :].astype(F32)).astype(BF)
            if d > 0:
                copy = copy_to(a1.at[at, :], r1.at[d - 1], peer(ax1, d))
                copy.start()
                copies.append(copy)
        stage1[p] = copies
        sent += copies

    adjoint(dgo, RD)
    zs[pl.ds(EDGE + RD * WD, EDGE), :] = wide
    for k in range(RD + 2):
        cb[k] = gathered(k - 2, RD)
    stage2 = [None] * PARTS
    for p in ORDER:
        ax1, ax2, ax3, r1, a2, r2, r3, g4 = plans[p]
        base, lines = AREAS[p]
        n1, chunk = size[ax1], r1.shape[1]
        n2, unit = size[ax2], r2.shape[1]
        for copy in stage1[p]:
            copy.wait_recv()
        at = pl.multiple_of(base + mine[ax1] * chunk, 16)
        total = a1[pl.ds(at, chunk), :].astype(F32)
        for d in range(1, n1):
            total = total + r1[d - 1].astype(F32)
        a2[pl.ds(0, chunk), :] = total.astype(BF)
        copies = []
        for d in far_first(n2):
            to = pl.multiple_of(lax.rem(mine[ax2] + d, n2) * unit, 16)
            copy = copy_to(a2.at[pl.ds(to, unit), :], r2.at[d - 1], peer(ax2, d))
            copy.start()
            copies.append(copy)
        stage2[p] = copies
        sent += copies

    late = []
    for i, (dr, dc) in enumerate(SIDES):
        rows_at = pl.ds(0, 1) if dr < 0 else (pl.ds(RD + 1, 1) if dr > 0 else pl.ds(1, RD))
        cols_at = pl.ds(0, 8) if dc < 0 else (pl.ds(8 + CD, 8) if dc > 0 else pl.ds(8, CD))
        copy = pltpu.make_async_remote_copy(
            src_ref=cb.at[rows_at, cols_at, :],
            dst_ref=slot_of(dr, dc, ud_c, lr_c, co_c),
            send_sem=late_send.at[i],
            recv_sem=late_recv.at[i],
            device_id=neighbour(dr, dc),
            device_id_type=MESH,
        )
        copy.start()
        late.append(copy)
    sent += late

    stage3 = [None] * PARTS
    for p in ORDER:
        ax1, ax2, ax3, r1, a2, r2, r3, g4 = plans[p]
        n2, n3, unit = size[ax2], size[ax3], r2.shape[1]
        for copy in stage2[p]:
            copy.wait_recv()
        total = a2[pl.ds(pl.multiple_of(mine[ax2] * unit, 16), unit), :].astype(F32)
        for d in range(1, n2):
            total = total + r2[d - 1].astype(F32)
        r3[mine[ax3]] = total.astype(BF)
        copies = []
        for d in far_first(n3):
            copy = copy_to(r3.at[mine[ax3]], r3.at[mine[ax3]], peer(ax3, d))
            copy.start()
            copies.append(copy)
        stage3[p] = copies
        sent += copies

    stage4 = [None] * PARTS
    for p in ORDER:
        ax1, ax2, ax3, r1, a2, r2, r3, g4 = plans[p]
        n2, n3, unit = size[ax2], size[ax3], r2.shape[1]
        for copy in stage3[p]:
            copy.wait_recv()
        total = r3[0].astype(F32)
        for d in range(1, n3):
            total = total + r3[d].astype(F32)
        slot = g4.at[pl.ds(pl.multiple_of(mine[ax2] * unit, 16), unit), :]
        slot[...] = total.astype(BF)
        copies = []
        for d in far_first(n2):
            copy = copy_to(slot, slot, peer(ax2, d))
            copy.start()
            copies.append(copy)
        stage4[p] = copies
        sent += copies

    stage5 = [None] * PARTS
    for p in ORDER:
        ax1, ax2, ax3, r1, a2, r2, r3, g4 = plans[p]
        base, lines = AREAS[p]
        n1, chunk = size[ax1], r1.shape[1]
        for copy in stage4[p]:
            copy.wait_recv()
        at = pl.ds(pl.multiple_of(base + mine[ax1] * chunk, 16), chunk)
        copies = []
        for d in far_first(n1):
            copy = copy_to(g4.at[pl.ds(0, chunk), :], gs.at[core, at, :], peer(ax1, d))
            copy.start()
            copies.append(copy)
        gs[core, at, :] = g4[pl.ds(0, chunk), :]
        stage5[p] = copies
        sent += copies

    for copy in late:
        copy.wait_recv()
    for row in range(RD):
        gh_out[row] = cb[row + 1, pl.ds(8, CD), :]
    for dr, dc in SIDES:
        inside = (r - dr >= 0) & (r - dr < n_rows) & (c - dc >= 0) & (c - dc < n_cols)
        keep = jnp.where(inside, 1.0, 0.0).astype(F32)
        rows_at = pl.ds(RD - 1, 1) if dr < 0 else (pl.ds(0, 1) if dr > 0 else pl.ds(0, RD))
        cols_at = pl.ds(CD - 8, 8) if dc < 0 else (pl.ds(0, 8) if dc > 0 else pl.ds(0, CD))
        terms = slot_of(dr, dc, ud_c, lr_c, co_c)[...] * keep
        gh_out[rows_at, cols_at, :] = gh_out[rows_at, cols_at, :] + terms

    write(gh_out, gh_hbm)

    stage6 = [None] * PARTS
    for p in ORDER:
        base, lines = AREAS[p]
        for copy in stage5[p]:
            copy.wait_recv()
        slot = gs.at[core, pl.ds(base, 2 * lines), :]
        copy = copy_to(slot, slot, sibling)
        copy.start()
        stage6[p] = copy
        write(slot, total_hbm.at[core, pl.ds(base, 2 * lines), :])
    for copy in halos + sent:
        copy.wait_send()
    for p in ORDER:
        base, lines = AREAS[p]
        copy = stage6[p]
        copy.wait_recv()
        area = pl.ds(base, 2 * lines)
        write(gs.at[1 - core, area, :], total_hbm.at[1 - core, area, :])

    for copy in stage6:
        copy.wait_send()
    for copy in written:
        copy.wait()


def sizes(p, n1, n2):
    chunk = 2 * AREAS[p][1] // n1
    return chunk, -(-chunk // (16 * n2)) * 16


def shards(frames, hidden_start, cell_start, kernel, gate_bias, cotangent):
    n_rows = lax.axis_size("rows")
    n_cols = lax.axis_size("cols")
    ny = (n_rows // NX) * NYL
    (cz, uz), (cy, uy), (cx, ux) = sizes(0, NZ, ny), sizes(1, ny, NZ), sizes(2, NX, NZ)
    vmem = pltpu.VMEM
    scratch = [
        vmem((RD, CD, HC), BF),
        vmem((RD, CD, HC), F32),
        vmem((RD, CD, HC), F32),
        vmem((1, GATES), F32),
        vmem((RD, CD, HC), BF),
        vmem((3, STEPS, RD, 1280), BF),
        vmem((RD, CD, HC), F32),
        vmem((STEPS, RD, CD, HC), BF),
        vmem((ROWS_W, GATES), BF),
        vmem((2, 6 * CD, HC), BF),
        vmem((2, 3 * RD * 8, HC), BF),
        vmem((4, 6 * 8, HC), BF),
        vmem((2, 6 * CD, HC), BF),
        vmem((2, 3 * RD * 8, HC), BF),
        vmem((4, 6 * 8, HC), BF),
        vmem((STEPS, 16, 1280), F32),
        vmem((STEPS, 12 * WD + 2 * EDGE, HC), F32),
        vmem((STEPS, 12 * WD, HC), BF),
        vmem((10 * WD + 2 * EDGE, HC), F32),
        vmem((8 * WD + 2 * EDGE, HC), F32),
        vmem((KS, 10 * WD, HC), BF),
        vmem((KS, 8 * WD, HC), BF),
        vmem((8 * WD, GATES), F32),
        vmem((5, RD * WD, HC), F32),
        vmem((8 * WD, HC), F32),
        vmem((8 * WD, HC), F32),
        vmem((6 * WD, HC), F32),
        vmem((RD * WD, HC), F32),
        vmem((6 * WD, GATES), BF),
        vmem((2 * RD * WD, GATES), BF),
        vmem((6 * WD + 2 * EDGE, TAPS * HC), F32),
        vmem((RD + 2, WD, HC), F32),
        vmem((2, 1, CD, HC), F32),
        vmem((2, RD, 8, HC), F32),
        vmem((4, 1, 8, HC), F32),
        vmem((LINES, 128), BF),
        vmem((LINES, 128), F32),
        vmem((LINES, 128), BF),
        vmem((LINES, 128), BF),
        vmem((NZ - 1, cz, 128), BF),
        vmem((ny - 1, cy, 128), BF),
        vmem((NX - 1, cx, 128), BF),
        vmem((ny * uz, 128), BF),
        vmem((NZ * uy, 128), BF),
        vmem((NZ * ux, 128), BF),
        vmem((ny - 1, uz, 128), BF),
        vmem((NZ - 1, uy, 128), BF),
        vmem((NZ - 1, ux, 128), BF),
        vmem((NX, uz, 128), BF),
        vmem((NX, uy, 128), BF),
        vmem((ny, ux, 128), BF),
        vmem((ny * uz, 128), BF),
        vmem((NZ * uy, 128), BF),
        vmem((NZ * ux, 128), BF),
        vmem((2, LINES, 128), BF),
        pltpu.SemaphoreType.DMA((8, 2)),
        pltpu.SemaphoreType.DMA((8, 2)),
        pltpu.SemaphoreType.DMA((8,)),
        pltpu.SemaphoreType.DMA((8,)),
        pltpu.SemaphoreType.DMA((5 + 2 * TAPS,)),
        pltpu.SemaphoreType.DMA((3 + 2 * PARTS,)),
        pltpu.SemaphoreType.DMA((stages(n_rows),)),
        pltpu.SemaphoreType.DMA((stages(n_rows),)),
    ]
    in_hbm = pl.BlockSpec(memory_space=pltpu.HBM)
    hidden, grad_hidden, grad_cell, total = pl.pallas_call(
        functools.partial(body, n_rows, n_cols),
        out_shape=(
            jax.ShapeDtypeStruct((RD, CD, HC), BF),
            jax.ShapeDtypeStruct((RD, CD, HC), F32),
            jax.ShapeDtypeStruct((RD, CD, HC), F32),
            jax.ShapeDtypeStruct((2, LINES, 128), BF),
        ),
        in_specs=[in_hbm] * 6,
        out_specs=(in_hbm,) * 4,
        scratch_shapes=scratch,
        compiler_params=pltpu.CompilerParams(
            collective_id=0, has_side_effects=True, vmem_limit_bytes=63 * 1024 * 1024
        ),
    )(frames, hidden_start, cell_start, kernel, gate_bias.reshape(1, GATES), cotangent)
    scale = 1.0 / math.sqrt(STEPS * n_rows * RD * n_cols * CD)
    outs = pl.pallas_call(
        functools.partial(finish, scale),
        out_shape=(
            jax.ShapeDtypeStruct((RD, CD, HC), BF),
            jax.ShapeDtypeStruct((RD, CD, HC), F32),
            jax.ShapeDtypeStruct((RD, CD, HC), F32),
            jax.ShapeDtypeStruct((KIN, GATES), F32),
            jax.ShapeDtypeStruct((1, GATES), F32),
        ),
        in_specs=[in_hbm] * 4,
        out_specs=(in_hbm,) * 5,
        scratch_shapes=[
            vmem((2, LINES, 128), BF),
            vmem((RD, CD, HC), BF),
            vmem((RD, CD, HC), F32),
            vmem((RD, CD, HC), F32),
            vmem((KIN, GATES), F32),
            vmem((1, GATES), F32),
            pltpu.SemaphoreType.DMA((PARTS + 3,)),
            pltpu.SemaphoreType.DMA((TAPS + 4,)),
        ],
        compiler_params=pltpu.CompilerParams(vmem_limit_bytes=63 * 1024 * 1024),
    )(hidden, grad_hidden, grad_cell, total)
    return outs[0], outs[1], outs[2], outs[3], outs[4].reshape(GATES)


def finish(
    scale,
    hid_in,
    gh_in,
    gc_in,
    total_in,
    hid_out,
    gh_out,
    gc_out,
    kg_out,
    bg_out,
    total,
    hid,
    gh,
    gc,
    kg,
    bg,
    in_sem,
    sem,
):
    copies = []

    def put(src, dst):
        copy = pltpu.make_async_copy(src, dst, sem.at[len(copies)])
        copy.start()
        copies.append(copy)

    fetched = []

    def fetch(src, dst):
        copy = pltpu.make_async_copy(src, dst, in_sem.at[len(fetched)])
        copy.start()
        fetched.append(copy)

    for base, lines in AREAS[::-1]:
        area = pl.ds(base, 2 * lines)
        fetch(total_in.at[:, area, :], total.at[:, area, :])
    for src, dst in ((hid_in, hid), (gh_in, gh), (gc_in, gc)):
        fetch(src, dst)

    def take(core, panel, p, row, count):
        base, lines = AREAS[p]
        return total[core, pl.ds(base + panel * lines + row, count), :].astype(F32) * scale

    for p in (2, 1, 0):
        fetched[2 - p].wait()
        for b in range(KS):
            at = (p * KS + b) * 160
            for core in range(2):
                for panel in range(2):
                    cols = pl.ds((2 * core + panel) * 128, 128)
                    kg[pl.ds(at, CI), cols] = take(
                        core, panel, 2, KS * HC + FRAME_ROWS[p][0] + b * CI, CI
                    )
                    kg[pl.ds(at + CI, HC), cols] = take(core, panel, p, b * HC, HC)
            put(kg.at[pl.ds(at, 160), :], kg_out.at[pl.ds(at, 160), :])
    for core in range(2):
        for panel in range(2):
            bg[:, pl.ds((2 * core + panel) * 128, 128)] = take(core, panel, 2, BIAS_ROW, 16)[:1, :]
    put(bg, bg_out)
    for i, (src, dst) in enumerate(((hid, hid_out), (gh, gh_out), (gc, gc_out))):
        fetched[PARTS + i].wait()
        put(src, dst)
    for copy in copies:
        copy.wait()


def stages(n_rows):
    ny = (n_rows // NX) * NYL
    one = (NZ - 1) + (ny - 1) + (NX - 1)
    two = (ny - 1) + (NZ - 1) + (NZ - 1)
    three = (NX - 1) + (NX - 1) + (ny - 1)
    return 2 * PARTS + 2 * one + 2 * two + three


def solution(mesh):
    placed = (
        P(None, "rows", "cols"),
        P("rows", "cols", None),
        P("rows", "cols", None),
        P(),
        P(),
        P(None, "rows", "cols", None),
    )
    return jax.shard_map(
        shards,
        mesh=mesh,
        in_specs=placed,
        out_specs=(
            P("rows", "cols", None),
            P("rows", "cols", None),
            P("rows", "cols", None),
            P(),
            P(),
        ),
        check_vma=False,
    )
```

```python
import functools
import math

import jax
import jax.numpy as jnp
from jax import lax
from jax.experimental import pallas as pl
from jax.experimental.pallas import tpu as pltpu
from jax.sharding import PartitionSpec as P

HC = 128
CI = 32
KS = 3
STEPS = 2
GATES = 512
KIN = 1440
TAPS = 9

NX = 4
NYL = 2
NZ = 8

BF = jnp.bfloat16
F32 = jnp.float32
MESH = pl.DeviceIdType.MESH

RD = 4
CD = 32
WD = 48
EDGE = 8
ROWS_W = 1536
PARTS = 3
HALF = GATES // 2
FRAME_ROWS = ((0, 112), (112, 96), (208, 96))
AREAS = ((0, 384), (768, 384), (1536, 704))
LINES = 2944
ORDER = (2, 0, 1)
BIAS_ROW = 384 + 3 * CI
SIDES = [(dr, dc) for dr in (-1, 0, 1) for dc in (-1, 0, 1) if (dr, dc) != (0, 0)]


def span(step, halo, size):
    if step == 0:
        return (0, size), (halo, size)
    if step > 0:
        return (size - halo, halo), (0, halo)
    return (0, halo), (halo + size, halo)


def far_first(n):
    return sorted(range(1, n), key=lambda d: (-min(d, n - d), d))


def place(x, y, z, core):
    return ((y // NYL) * NX + x, ((y % NYL) * NZ + z) * 2 + core)


def body(
    n_rows,
    n_cols,
    frames_ref,
    hidden_ref,
    cell_ref,
    kernel_ref,
    bias_ref,
    cot_ref,
    hid_hbm,
    gh_hbm,
    gc_hbm,
    total_hbm,
    hid_out,
    gh_out,
    gc_out,
    bias_in,
    hown,
    fl,
    cown,
    kown,
    wp,
    ud,
    st,
    co,
    ud_in,
    st_in,
    co_in,
    fs,
    x32,
    xb,
    s1,
    s2,
    hs1,
    hs2,
    ga,
    sv,
    c0s,
    c1s,
    k1s,
    dcs,
    dg2,
    dgo,
    zs,
    cb,
    ud_c,
    lr_c,
    co_c,
    a0,
    o0,
    r0,
    a1,
    r1z,
    r1y,
    r1x,
    a2z,
    a2y,
    a2x,
    r2z,
    r2y,
    r2x,
    r3z,
    r3y,
    r3x,
    g4z,
    g4y,
    g4x,
    gs,
    halo_send,
    halo_recv,
    late_send,
    late_recv,
    loc_sem,
    out_sem,
    st_send,
    st_recv,
):
    r = lax.axis_index("rows")
    c = lax.axis_index("cols")
    ny = (n_rows // NX) * NYL
    x = lax.rem(r, NX)
    core = lax.rem(c, 2)
    z = lax.rem(c // 2, NZ)
    y = (r // NX) * NYL + c // (2 * NZ)
    size = {"x": NX, "y": ny, "z": NZ}
    mine = {"x": x, "y": y, "z": z}

    def peer(axis, d):
        at = dict(mine)
        at[axis] = lax.rem(mine[axis] + d, size[axis])
        return place(at["x"], at["y"], at["z"], core)

    sibling = place(x, y, z, 1 - core)

    def neighbour(dr, dc):
        return (lax.rem(r + dr + n_rows, n_rows), lax.rem(c + dc + n_cols, n_cols))

    barrier = pltpu.get_barrier_semaphore()
    greet = [neighbour(dr, dc) for dr, dc in SIDES] + [sibling]
    for axis in ("x", "y", "z"):
        greet += [peer(axis, d) for d in range(1, size[axis])]
    for who in greet[: len(SIDES)]:
        pl.semaphore_signal(barrier, inc=1, device_id=who, device_id_type=MESH)

    local = []

    def fetch(src, dst):
        copy = pltpu.make_async_copy(src, dst, loc_sem.at[len(local)])
        copy.start()
        local.append(copy)

    fetch(hidden_ref, hown)
    fetch(cell_ref, cown)
    fetch(cot_ref, kown)
    fetch(frames_ref, fl.at[1, :, :, pl.ds(128, CD * CI)])
    for who in greet[len(SIDES) :]:
        pl.semaphore_signal(barrier, inc=1, device_id=who, device_id_type=MESH)
    for copy in local[:3]:
        copy.wait()
    fields = (
        ([hown[i] for i in range(RD)], 3),
        ([cown[i] for i in range(RD)], 2),
        ([kown[1, i] for i in range(RD)], 1),
    )

    def edge_rows(step, depth):
        if step == 0:
            return range(RD)
        return range(depth) if step < 0 else range(RD - depth, RD)

    def outgoing(dr, dc):
        pieces = []
        for rows, depth in fields:
            for i in edge_rows(dr, depth):
                piece = rows[i].astype(F32)
                if dc != 0:
                    piece = piece[:8, :] if dc < 0 else piece[CD - 8 :, :]
                pieces.append(piece)
        return jnp.concatenate(pieces, axis=0).astype(BF)

    def slot_of(dr, dc, rows_buf, sides_buf, corners_buf):
        if dc == 0:
            return rows_buf.at[(dr + 1) // 2]
        if dr == 0:
            return sides_buf.at[(dc + 1) // 2]
        return corners_buf.at[(dr + 1) + (dc + 1) // 2]

    for dr, dc in SIDES:
        slot_of(dr, dc, ud, st, co)[...] = outgoing(dr, dc)
    pl.semaphore_wait(barrier, len(greet))

    halos = []
    for i, (dr, dc) in enumerate(SIDES):
        who = neighbour(dr, dc)
        (ls, ln), (lt, _) = span(dc, 128, CD * CI)
        for kind, (src, dst) in enumerate(
            (
                (slot_of(dr, dc, ud, st, co), slot_of(dr, dc, ud_in, st_in, co_in)),
                (frames_ref.at[:, :, pl.ds(ls, ln)], fl.at[1 - dr, :, :, pl.ds(lt, ln)]),
            )
        ):
            copy = pltpu.make_async_remote_copy(
                src_ref=src,
                dst_ref=dst,
                send_sem=halo_send.at[i, kind],
                recv_sem=halo_recv.at[i, kind],
                device_id=who,
                device_id_type=MESH,
            )
            copy.start()
            halos.append(copy)

    fetch(bias_ref, bias_in)
    for tap in range(TAPS):
        a, b = divmod(tap, KS)
        fetch(kernel_ref.at[pl.ds(tap * 160 + CI, HC), :], wp.at[pl.ds(tap * HC, HC), :])
        fetch(
            kernel_ref.at[pl.ds(tap * 160, CI), :],
            wp.at[pl.ds(TAPS * HC + a * 128 + b * CI, CI), :],
        )
    for a in range(KS):
        wp[pl.ds(TAPS * HC + a * 128 + 96, 32), :] = jnp.zeros((32, GATES), BF)
    x32[...] = jnp.zeros_like(x32)
    edge = jnp.zeros((EDGE, HC), F32)
    s1[pl.ds(0, EDGE), :] = edge
    s1[pl.ds(EDGE + 10 * WD, EDGE), :] = edge
    s2[pl.ds(0, EDGE), :] = edge
    s2[pl.ds(EDGE + 8 * WD, EDGE), :] = edge
    wide = jnp.zeros((EDGE, TAPS * HC), F32)
    zs[pl.ds(0, EDGE), :] = wide
    zs[pl.ds(EDGE + 6 * WD, EDGE), :] = wide
    fs[...] = jnp.zeros_like(fs)
    for spare in (a2z, a2y, a2x):
        spare[...] = jnp.zeros_like(spare)

    at_col = lax.broadcasted_iota(jnp.int32, (WD, HC), 0) - 8
    in_raster = (at_col + c * CD >= 0) & (at_col + c * CD < n_cols * CD)
    col_mask = jnp.where(in_raster, 1.0, 0.0).astype(F32)
    own_mask = jnp.where((at_col >= 0) & (at_col < CD), 1.0, 0.0).astype(F32)

    def row_mask(row):
        there = r * RD + row
        inside = (there >= 0) & (there < n_rows * RD)
        return col_mask * jnp.where(inside, 1.0, 0.0).astype(F32)

    lane = lax.broadcasted_iota(jnp.int32, (16, 1280), 1)
    line = lax.broadcasted_iota(jnp.int32, (16, 1280), 0)
    there_col = lane // CI - 4 + c * CD
    there_row = line - 4 + r * RD
    frame_mask = jnp.where(
        (there_col >= 0)
        & (there_col < n_cols * CD)
        & (there_row >= 0)
        & (there_row < n_rows * RD),
        1.0,
        0.0,
    ).astype(F32)

    for copy in local[3:]:
        copy.wait()
    for copy in halos:
        copy.wait_recv()

    def incoming(dr, dc):
        return slot_of(-dr, -dc, ud_in, st_in, co_in)[...].astype(F32)

    around = {side: incoming(*side) for side in SIDES}

    def field_row(which, row):
        rows, depth = fields[which]
        before = [d for _, d in fields[:which]]
        dr = -1 if row < 0 else (1 if row >= RD else 0)
        i = row + depth if row < 0 else (row - RD if row >= RD else row)
        parts = []
        for dc in (-1, 0, 1):
            if (dr, dc) == (0, 0):
                parts.append(rows[row].astype(F32))
                continue
            wide_row = CD if dc == 0 else 8
            skip = (RD * which if dr == 0 else sum(before)) * wide_row
            parts.append(around[dr, dc][skip + i * wide_row : skip + (i + 1) * wide_row, :])
        return jnp.concatenate(parts, axis=0)

    for k in range(10):
        s1[pl.ds(EDGE + k * WD, WD), :] = field_row(0, k - 3) * row_mask(k - 3)
    for k in range(8):
        c0s[pl.ds(k * WD, WD), :] = field_row(1, k - 2)
    for k in range(6):
        k1s[pl.ds(k * WD, WD), :] = field_row(2, k - 1)
    for b in range(KS):
        hs1[b] = s1[pl.ds(EDGE + b - 1, 10 * WD), :].astype(BF)
    low = lax.broadcasted_iota(jnp.int32, (12, HC), 1) < CI
    ones = jnp.where(
        lax.broadcasted_iota(jnp.int32, (WD, HC), 1) == 3 * CI, 1.0, 0.0
    ).astype(F32)
    for t in range(STEPS):
        for k in range(3):
            fs[t, pl.ds(4 * k, 4), :] = fl[k, t].astype(F32)
        for g in range(10):
            vals = fs[t, pl.ds(0, 12), pl.ds(g * 128, 128)] * frame_mask[:12, g * 128 : (g + 1) * 128]
            for j in range(4):
                turned = vals if j == 0 else pltpu.roll(vals, 128 - 32 * j, 1)
                x32[t, pl.ds(EDGE + 4 + 4 * g + j, 12, stride=WD), :] = jnp.where(low, turned, 0.0)
        for row in range(12):
            at = EDGE + row * WD
            joined = (
                x32[t, pl.ds(at - 1, WD), :]
                + pltpu.roll(x32[t, pl.ds(at, WD), :], 32, 1)
                + pltpu.roll(x32[t, pl.ds(at + 1, WD), :], 64, 1)
                + ones
            )
            xb[t, pl.ds(row * WD, WD), :] = joined.astype(BF)

    bias = bias_in[...]

    def gates_of(hs, t, first, count):
        size_m = count * WD
        blocks = [
            hs[b, pl.ds(a * WD, size_m), :] for a in range(KS) for b in range(KS)
        ] + [xb[t, pl.ds((first + a) * WD, size_m), :] for a in range(KS)]
        lhs = jnp.concatenate(blocks, axis=1)
        ga[pl.ds(0, size_m), :] = jnp.dot(lhs, wp[...], preferred_element_type=F32)

    def sigmoid(v):
        return 0.5 * jnp.tanh(0.5 * v) + 0.5

    def activated(row):
        pre = ga[pl.ds(row * WD, WD), :] + bias
        return (
            sigmoid(pre[:, :HC]),
            sigmoid(pre[:, HC : 2 * HC]),
            jnp.tanh(pre[:, 2 * HC : 3 * HC]),
            sigmoid(pre[:, 3 * HC :]),
        )

    gates_of(hs1, 0, 1, 8)
    for k in range(8):
        row = k - 2
        gi, gf, gg, go = activated(k)
        now = gf * c0s[pl.ds(k * WD, WD), :] + gi * gg
        th = jnp.tanh(now)
        c1s[pl.ds(k * WD, WD), :] = now
        if 0 <= row < RD:
            at = pl.ds(row * WD, WD)
            for q, val in enumerate((gi, gf, gg, go, th)):
                sv[q, at, :] = val
        h = (go * th).astype(BF).astype(F32)
        s2[pl.ds(EDGE + k * WD, WD), :] = h * row_mask(row)
    for b in range(KS):
        hs2[b] = s2[pl.ds(EDGE + b - 1, 8 * WD), :].astype(BF)

    gates_of(hs2, 1, 2, 6)

    def pre_grads(s, dh, gi, gf, gg, go, th, before):
        return (
            s * gg * gi * (1.0 - gi),
            s * before * gf * (1.0 - gf),
            s * gi * (1.0 - gg * gg),
            dh * th * go * (1.0 - go),
        )

    for k in range(6):
        row = k - 1
        gi, gf, gg, go = activated(k)
        before = c1s[pl.ds((k + 1) * WD, WD), :]
        now = gf * before + gi * gg
        th = jnp.tanh(now)
        dh = k1s[pl.ds(k * WD, WD), :]
        s = dh * go * (1.0 - th * th)
        if 0 <= row < RD:
            hid_out[row] = (go * th)[8 : 8 + CD, :].astype(BF)
            dcs[pl.ds(row * WD, WD), :] = s * gf
        mask = row_mask(row)
        for q, pre in enumerate(pre_grads(s, dh, gi, gf, gg, go, th, before)):
            cols = pl.ds(q * HC, HC)
            dg2[pl.ds(k * WD, WD), cols] = (pre * mask).astype(BF)
            if 0 <= row < RD:
                dgo[pl.ds((RD + row) * WD, WD), cols] = (pre * own_mask).astype(BF)

    def adjoint(dg, count):
        size_m = count * WD
        zs[pl.ds(EDGE, size_m), :] = lax.dot_general(
            dg[pl.ds(0, size_m), :],
            wp[pl.ds(0, TAPS * HC), :],
            (((1,), (1,)), ((), ())),
            preferred_element_type=F32,
        )

    def gathered(k, count):
        total = None
        for tap in range(TAPS):
            a, b = divmod(tap, KS)
            row = k + 2 - a
            if not 0 <= row < count:
                continue
            term = zs[pl.ds(EDGE + row * WD - (b - 1), WD), pl.ds(tap * HC, HC)]
            total = term if total is None else total + term
        return total

    adjoint(dg2, 6)
    for row in range(RD):
        at = pl.ds(row * WD, WD)
        gi, gf, gg, go, th = (sv[q, at, :] for q in range(5))
        inner = gathered(row, 6)
        cot = kown[0, row].astype(F32)
        blank = jnp.zeros((8, HC), F32)
        dh = inner + jnp.concatenate([blank, cot, blank], axis=0)
        s = dcs[at, :] + dh * go * (1.0 - th * th)
        gc_out[row] = (s * gf)[8 : 8 + CD, :]
        before = c0s[pl.ds((row + 2) * WD, WD), :]
        for q, pre in enumerate(pre_grads(s, dh, gi, gf, gg, go, th, before)):
            dgo[at, pl.ds(q * HC, HC)] = (pre * own_mask).astype(BF)

    written = []

    def write(src, dst):
        copy = pltpu.make_async_copy(src, dst, out_sem.at[len(written)])
        copy.start()
        written.append(copy)

    write(hid_out, hid_hbm)
    write(gc_out, gc_hbm)

    count = [0]

    def copy_to(src, dst, who):
        i = count[0]
        count[0] += 1
        return pltpu.make_async_remote_copy(
            src_ref=src,
            dst_ref=dst,
            send_sem=st_send.at[i],
            recv_sem=st_recv.at[i],
            device_id=who,
            device_id_type=MESH,
        )

    sent = []
    mine_at = pl.multiple_of(core * HALF, HALF)
    other_at = pl.multiple_of((1 - core) * HALF, HALF)

    def weight_blocks(p):
        blocks = []
        for q in range(KS * p, KS * p + (KS if p < 2 else 2 * KS)):
            if q < TAPS:
                a, b = divmod(q, KS)
                one = hs1[b, pl.ds((2 + a) * WD, RD * WD), :]
                two = hs2[b, pl.ds((1 + a) * WD, RD * WD), :]
            else:
                a = q - TAPS
                one = xb[0, pl.ds((3 + a) * WD, RD * WD), :]
                two = xb[1, pl.ds((3 + a) * WD, RD * WD), :]
            blocks.append(jnp.concatenate([one, two], axis=0))
        return jnp.concatenate(blocks, axis=1)

    def weight_grad(p, cols_at, out):
        val = lax.dot_general(
            weight_blocks(p),
            dgo[:, pl.ds(cols_at, HALF)],
            (((0,), (0,)), ((), ())),
            preferred_element_type=F32,
        ).astype(out.dtype)
        base, lines = AREAS[p]
        for panel in range(2):
            cut = val[:, panel * 128 : (panel + 1) * 128]
            at = base + panel * lines
            out[pl.ds(at, KS * HC), :] = cut[: KS * HC, :]
            if p == 2:
                for a, (first, size_a) in enumerate(FRAME_ROWS):
                    start = (KS + a) * HC
                    out[pl.ds(at + KS * HC + first, size_a), :] = cut[start : start + size_a, :]
                out[pl.ds(at + lines - 16, 16), :] = jnp.zeros((16, 128), out.dtype)

    swaps = [None] * PARTS
    for p in ORDER:
        base, lines = AREAS[p]
        weight_grad(p, other_at, a0)
        area = pl.ds(base, 2 * lines)
        copy = copy_to(a0.at[area, :], r0.at[area, :], sibling)
        copy.start()
        swaps[p] = copy
    for p in ORDER:
        weight_grad(p, mine_at, o0)
    sent += swaps

    plans = [
        ("z", "y", "x", r1z, a2z, r2z, r3z, g4z),
        ("y", "z", "x", r1y, a2y, r2y, r3y, g4y),
        ("x", "z", "y", r1x, a2x, r2x, r3x, g4x),
    ]

    stage1 = [None] * PARTS
    for p in ORDER:
        ax1, ax2, ax3, r1, a2, r2, r3, g4 = plans[p]
        base, lines = AREAS[p]
        n1, chunk = size[ax1], r1.shape[1]
        swaps[p].wait_recv()
        copies = []
        for d in far_first(n1) + [0]:
            to = pl.multiple_of(base + lax.rem(mine[ax1] + d, n1) * chunk, 16)
            at = pl.ds(to, chunk)
            a1[at, :] = (o0[at, :] + r0[at, :].astype(F32)).astype(BF)
            if d > 0:
                copy = copy_to(a1.at[at, :], r1.at[d - 1], peer(ax1, d))
                copy.start()
                copies.append(copy)
        stage1[p] = copies
        sent += copies

    adjoint(dgo, RD)
    zs[pl.ds(EDGE + RD * WD, EDGE), :] = wide
    for k in range(RD + 2):
        cb[k] = gathered(k - 2, RD)
    stage2 = [None] * PARTS
    for p in ORDER:
        ax1, ax2, ax3, r1, a2, r2, r3, g4 = plans[p]
        base, lines = AREAS[p]
        n1, chunk = size[ax1], r1.shape[1]
        n2, unit = size[ax2], r2.shape[1]
        for copy in stage1[p]:
            copy.wait_recv()
        at = pl.multiple_of(base + mine[ax1] * chunk, 16)
        total = a1[pl.ds(at, chunk), :].astype(F32)
        for d in range(1, n1):
            total = total + r1[d - 1].astype(F32)
        a2[pl.ds(0, chunk), :] = total.astype(BF)
        copies = []
        for d in far_first(n2):
            to = pl.multiple_of(lax.rem(mine[ax2] + d, n2) * unit, 16)
            copy = copy_to(a2.at[pl.ds(to, unit), :], r2.at[d - 1], peer(ax2, d))
            copy.start()
            copies.append(copy)
        stage2[p] = copies
        sent += copies

    late = []
    for i, (dr, dc) in enumerate(SIDES):
        rows_at = pl.ds(0, 1) if dr < 0 else (pl.ds(RD + 1, 1) if dr > 0 else pl.ds(1, RD))
        cols_at = pl.ds(0, 8) if dc < 0 else (pl.ds(8 + CD, 8) if dc > 0 else pl.ds(8, CD))
        copy = pltpu.make_async_remote_copy(
            src_ref=cb.at[rows_at, cols_at, :],
            dst_ref=slot_of(dr, dc, ud_c, lr_c, co_c),
            send_sem=late_send.at[i],
            recv_sem=late_recv.at[i],
            device_id=neighbour(dr, dc),
            device_id_type=MESH,
        )
        copy.start()
        late.append(copy)
    sent += late

    stage3 = [None] * PARTS
    for p in ORDER:
        ax1, ax2, ax3, r1, a2, r2, r3, g4 = plans[p]
        n2, n3, unit = size[ax2], size[ax3], r2.shape[1]
        for copy in stage2[p]:
            copy.wait_recv()
        total = a2[pl.ds(pl.multiple_of(mine[ax2] * unit, 16), unit), :].astype(F32)
        for d in range(1, n2):
            total = total + r2[d - 1].astype(F32)
        r3[mine[ax3]] = total.astype(BF)
        copies = []
        for d in far_first(n3):
            copy = copy_to(r3.at[mine[ax3]], r3.at[mine[ax3]], peer(ax3, d))
            copy.start()
            copies.append(copy)
        stage3[p] = copies
        sent += copies

    stage4 = [None] * PARTS
    for p in ORDER:
        ax1, ax2, ax3, r1, a2, r2, r3, g4 = plans[p]
        n2, n3, unit = size[ax2], size[ax3], r2.shape[1]
        for copy in stage3[p]:
            copy.wait_recv()
        total = r3[0].astype(F32)
        for d in range(1, n3):
            total = total + r3[d].astype(F32)
        slot = g4.at[pl.ds(pl.multiple_of(mine[ax2] * unit, 16), unit), :]
        slot[...] = total.astype(BF)
        copies = []
        for d in far_first(n2):
            copy = copy_to(slot, slot, peer(ax2, d))
            copy.start()
            copies.append(copy)
        stage4[p] = copies
        sent += copies

    stage5 = [None] * PARTS
    for p in ORDER:
        ax1, ax2, ax3, r1, a2, r2, r3, g4 = plans[p]
        base, lines = AREAS[p]
        n1, chunk = size[ax1], r1.shape[1]
        for copy in stage4[p]:
            copy.wait_recv()
        at = pl.ds(pl.multiple_of(base + mine[ax1] * chunk, 16), chunk)
        copies = []
        for d in far_first(n1):
            copy = copy_to(g4.at[pl.ds(0, chunk), :], gs.at[core, at, :], peer(ax1, d))
            copy.start()
            copies.append(copy)
        gs[core, at, :] = g4[pl.ds(0, chunk), :]
        stage5[p] = copies
        sent += copies

    for copy in late:
        copy.wait_recv()
    for row in range(RD):
        gh_out[row] = cb[row + 1, pl.ds(8, CD), :]
    for dr, dc in SIDES:
        inside = (r - dr >= 0) & (r - dr < n_rows) & (c - dc >= 0) & (c - dc < n_cols)
        keep = jnp.where(inside, 1.0, 0.0).astype(F32)
        rows_at = pl.ds(RD - 1, 1) if dr < 0 else (pl.ds(0, 1) if dr > 0 else pl.ds(0, RD))
        cols_at = pl.ds(CD - 8, 8) if dc < 0 else (pl.ds(0, 8) if dc > 0 else pl.ds(0, CD))
        terms = slot_of(dr, dc, ud_c, lr_c, co_c)[...] * keep
        gh_out[rows_at, cols_at, :] = gh_out[rows_at, cols_at, :] + terms

    write(gh_out, gh_hbm)

    stage6 = [None] * PARTS
    for p in ORDER:
        base, lines = AREAS[p]
        for copy in stage5[p]:
            copy.wait_recv()
        slot = gs.at[core, pl.ds(base, 2 * lines), :]
        copy = copy_to(slot, slot, sibling)
        copy.start()
        stage6[p] = copy
        write(slot, total_hbm.at[core, pl.ds(base, 2 * lines), :])
    for copy in halos + sent:
        copy.wait_send()
    for p in ORDER:
        base, lines = AREAS[p]
        copy = stage6[p]
        copy.wait_recv()
        area = pl.ds(base, 2 * lines)
        write(gs.at[1 - core, area, :], total_hbm.at[1 - core, area, :])

    for copy in stage6:
        copy.wait_send()
    for copy in written:
        copy.wait()


def sizes(p, n1, n2):
    chunk = 2 * AREAS[p][1] // n1
    return chunk, -(-chunk // (16 * n2)) * 16


def shards(frames, hidden_start, cell_start, kernel, gate_bias, cotangent):
    n_rows = lax.axis_size("rows")
    n_cols = lax.axis_size("cols")
    ny = (n_rows // NX) * NYL
    (cz, uz), (cy, uy), (cx, ux) = sizes(0, NZ, ny), sizes(1, ny, NZ), sizes(2, NX, NZ)
    vmem = pltpu.VMEM
    scratch = [
        vmem((RD, CD, HC), BF),
        vmem((RD, CD, HC), F32),
        vmem((RD, CD, HC), F32),
        vmem((1, GATES), F32),
        vmem((RD, CD, HC), BF),
        vmem((3, STEPS, RD, 1280), BF),
        vmem((RD, CD, HC), F32),
        vmem((STEPS, RD, CD, HC), BF),
        vmem((ROWS_W, GATES), BF),
        vmem((2, 6 * CD, HC), BF),
        vmem((2, 3 * RD * 8, HC), BF),
        vmem((4, 6 * 8, HC), BF),
        vmem((2, 6 * CD, HC), BF),
        vmem((2, 3 * RD * 8, HC), BF),
        vmem((4, 6 * 8, HC), BF),
        vmem((STEPS, 16, 1280), F32),
        vmem((STEPS, 12 * WD + 2 * EDGE, HC), F32),
        vmem((STEPS, 12 * WD, HC), BF),
        vmem((10 * WD + 2 * EDGE, HC), F32),
        vmem((8 * WD + 2 * EDGE, HC), F32),
        vmem((KS, 10 * WD, HC), BF),
        vmem((KS, 8 * WD, HC), BF),
        vmem((8 * WD, GATES), F32),
        vmem((5, RD * WD, HC), F32),
        vmem((8 * WD, HC), F32),
        vmem((8 * WD, HC), F32),
        vmem((6 * WD, HC), F32),
        vmem((RD * WD, HC), F32),
        vmem((6 * WD, GATES), BF),
        vmem((2 * RD * WD, GATES), BF),
        vmem((6 * WD + 2 * EDGE, TAPS * HC), F32),
        vmem((RD + 2, WD, HC), F32),
        vmem((2, 1, CD, HC), F32),
        vmem((2, RD, 8, HC), F32),
        vmem((4, 1, 8, HC), F32),
        vmem((LINES, 128), BF),
        vmem((LINES, 128), F32),
        vmem((LINES, 128), BF),
        vmem((LINES, 128), BF),
        vmem((NZ - 1, cz, 128), BF),
        vmem((ny - 1, cy, 128), BF),
        vmem((NX - 1, cx, 128), BF),
        vmem((ny * uz, 128), BF),
        vmem((NZ * uy, 128), BF),
        vmem((NZ * ux, 128), BF),
        vmem((ny - 1, uz, 128), BF),
        vmem((NZ - 1, uy, 128), BF),
        vmem((NZ - 1, ux, 128), BF),
        vmem((NX, uz, 128), BF),
        vmem((NX, uy, 128), BF),
        vmem((ny, ux, 128), BF),
        vmem((ny * uz, 128), BF),
        vmem((NZ * uy, 128), BF),
        vmem((NZ * ux, 128), BF),
        vmem((2, LINES, 128), BF),
        pltpu.SemaphoreType.DMA((8, 2)),
        pltpu.SemaphoreType.DMA((8, 2)),
        pltpu.SemaphoreType.DMA((8,)),
        pltpu.SemaphoreType.DMA((8,)),
        pltpu.SemaphoreType.DMA((5 + 2 * TAPS,)),
        pltpu.SemaphoreType.DMA((3 + 2 * PARTS,)),
        pltpu.SemaphoreType.DMA((stages(n_rows),)),
        pltpu.SemaphoreType.DMA((stages(n_rows),)),
    ]
    in_hbm = pl.BlockSpec(memory_space=pltpu.HBM)
    hidden, grad_hidden, grad_cell, total = pl.pallas_call(
        functools.partial(body, n_rows, n_cols),
        out_shape=(
            jax.ShapeDtypeStruct((RD, CD, HC), BF),
            jax.ShapeDtypeStruct((RD, CD, HC), F32),
            jax.ShapeDtypeStruct((RD, CD, HC), F32),
            jax.ShapeDtypeStruct((2, LINES, 128), BF),
        ),
        in_specs=[in_hbm] * 6,
        out_specs=(in_hbm,) * 4,
        scratch_shapes=scratch,
        compiler_params=pltpu.CompilerParams(
            collective_id=0, has_side_effects=True, vmem_limit_bytes=63 * 1024 * 1024
        ),
    )(frames, hidden_start, cell_start, kernel, gate_bias.reshape(1, GATES), cotangent)
    scale = 1.0 / math.sqrt(STEPS * n_rows * RD * n_cols * CD)
    outs = pl.pallas_call(
        functools.partial(finish, scale),
        out_shape=(
            jax.ShapeDtypeStruct((RD, CD, HC), BF),
            jax.ShapeDtypeStruct((RD, CD, HC), F32),
            jax.ShapeDtypeStruct((RD, CD, HC), F32),
            jax.ShapeDtypeStruct((KIN, GATES), F32),
            jax.ShapeDtypeStruct((1, GATES), F32),
        ),
        in_specs=[in_hbm] * 4,
        out_specs=(in_hbm,) * 5,
        scratch_shapes=[
            vmem((2, LINES, 128), BF),
            vmem((RD, CD, HC), BF),
            vmem((RD, CD, HC), F32),
            vmem((RD, CD, HC), F32),
            vmem((KIN, GATES), F32),
            vmem((1, GATES), F32),
            pltpu.SemaphoreType.DMA((PARTS + 3,)),
            pltpu.SemaphoreType.DMA((TAPS + 4,)),
        ],
        compiler_params=pltpu.CompilerParams(vmem_limit_bytes=63 * 1024 * 1024),
    )(hidden, grad_hidden, grad_cell, total)
    return outs[0], outs[1], outs[2], outs[3], outs[4].reshape(GATES)


def finish(
    scale,
    hid_in,
    gh_in,
    gc_in,
    total_in,
    hid_out,
    gh_out,
    gc_out,
    kg_out,
    bg_out,
    total,
    hid,
    gh,
    gc,
    kg,
    bg,
    in_sem,
    sem,
):
    copies = []

    def put(src, dst):
        copy = pltpu.make_async_copy(src, dst, sem.at[len(copies)])
        copy.start()
        copies.append(copy)

    fetched = []

    def fetch(src, dst):
        copy = pltpu.make_async_copy(src, dst, in_sem.at[len(fetched)])
        copy.start()
        fetched.append(copy)

    for base, lines in AREAS[::-1]:
        area = pl.ds(base, 2 * lines)
        fetch(total_in.at[:, area, :], total.at[:, area, :])
    for src, dst in ((hid_in, hid), (gh_in, gh), (gc_in, gc)):
        fetch(src, dst)

    def take(core, panel, p, row, count):
        base, lines = AREAS[p]
        return total[core, pl.ds(base + panel * lines + row, count), :].astype(F32) * scale

    for p in (2, 1, 0):
        fetched[2 - p].wait()
        for b in range(KS):
            at = (p * KS + b) * 160
            for core in range(2):
                for panel in range(2):
                    cols = pl.ds((2 * core + panel) * 128, 128)
                    kg[pl.ds(at, CI), cols] = take(
                        core, panel, 2, KS * HC + FRAME_ROWS[p][0] + b * CI, CI
                    )
                    kg[pl.ds(at + CI, HC), cols] = take(core, panel, p, b * HC, HC)
            put(kg.at[pl.ds(at, 160), :], kg_out.at[pl.ds(at, 160), :])
    for core in range(2):
        for panel in range(2):
            bg[:, pl.ds((2 * core + panel) * 128, 128)] = take(core, panel, 2, BIAS_ROW, 16)[:1, :]
    put(bg, bg_out)
    for i, (src, dst) in enumerate(((hid, hid_out), (gh, gh_out), (gc, gc_out))):
        fetched[PARTS + i].wait()
        put(src, dst)
    for copy in copies:
        copy.wait()


def stages(n_rows):
    ny = (n_rows // NX) * NYL
    one = (NZ - 1) + (ny - 1) + (NX - 1)
    two = (ny - 1) + (NZ - 1) + (NZ - 1)
    three = (NX - 1) + (NX - 1) + (ny - 1)
    return 2 * PARTS + 2 * one + 2 * two + three


def solution(mesh):
    placed = (
        P(None, "rows", "cols"),
        P("rows", "cols", None),
        P("rows", "cols", None),
        P(),
        P(),
        P(None, "rows", "cols", None),
    )
    return jax.shard_map(
        shards,
        mesh=mesh,
        in_specs=placed,
        out_specs=(
            P("rows", "cols", None),
            P("rows", "cols", None),
            P("rows", "cols", None),
            P(),
            P(),
        ),
        check_vma=False,
    )
```
